128 devices in a mesh: dp: 2 (over z_hi), space: 64 (over z_lo, x, y, core).
Axes of the slice: x: 4, y: 4, z: 4 (z_hi: 2, z_lo: 2; z = z_hi * 2 + z_lo), core: 2. Of those that a mesh axis runs over, the one named last changes fastest.
Arguments:
- inputs: float32 [2, 32, 128, 128, 128], P('dp', None, 'space'), may hold values from -6 to 6
- preact: float32 [2, 32, 128, 128, 128], P('dp', None, 'space'), may hold values from -6 to 6
- cotangent: float32 [2, 32, 128, 128, 128], P('dp', None, 'space'), may hold values from -6 to 6
- spectral_weight: float32 [32, 1024, 2048], P(None, 'space'), may hold values from -3 to 3
- skip_weight: float32 [32, 32], replicated, may hold values from -1 to 1
Outputs:
- input_grad: float32 [2, 32, 128, 128, 128], P('dp', None, 'space')
- weight_grad: float32 [32, 1024, 2048], P('dp', 'space')
- skip_grad: float32 [32, 32], replicated
The draws below stay inside these ranges and needn't reach their ends.
All inputs are finite; a program needn't handle non-finite values.
Results may differ from the reference program's by a relative error of at most 0.00016.
Values sent between devices are 32-bit elements; how exact they have to be, the bound alone decides.
No kernel may reach another device: no remote copies, remote signals or barrier semaphores. Data moves between devices by JAX's collectives and lax.ppermute only.
A program may use at most 128 MiB of HBM per device.

```python
import jax
import jax.numpy as jnp
from jax import lax

N = 128
C = 32
MX = 32
MY = 64
MZ = 16
BATCH = 2


def block_scale(stream_key, extent, cuts, low, high):
    def one(dim, parts):
        steps = jax.random.uniform(jax.random.fold_in(jax.random.fold_in(stream_key, 6), dim), (parts,), jnp.float32, low / len(cuts), high / len(cuts))
        return jnp.repeat(jnp.exp(steps), extent[dim] // parts).reshape((-1,) + (1,) * (len(extent) - dim - 1))

    loudness = one(*cuts[0])
    for cut in cuts[1:]:
        loudness = loudness * one(*cut)
    return loudness


def gaussian(key, dims, scale, reach, split=(), held_as=jnp.bfloat16):
    entries = jax.random.normal(key, dims, jnp.float32) * scale
    if len(split) > 0:
        entries = block_scale(key, dims, split, -0.22, 0.18) * entries
    return jnp.clip(entries, min=-reach, max=reach).astype(held_as)


def setup_inputs(seed: int = 0) -> dict:
    arg_keys = jax.random.split(jax.random.key(seed), 6)
    inputs = gaussian(arg_keys[0], (BATCH, C, N, N, N), 1.0, 6.0, ((0, 2), (2, 64)), jnp.float32)
    preact = gaussian(arg_keys[1], (BATCH, C, N, N, N), 1.5, 6.0, ((0, 2), (2, 64)), jnp.float32)
    cotangent = gaussian(arg_keys[2], (BATCH, C, N, N, N), 1.0, 6.0, ((0, 2), (2, 64)), jnp.float32)
    spectral_weight = gaussian(arg_keys[3], (MX, MY * MZ, 2 * C * C), 0.5, 3.0, ((1, 64),), jnp.float32)
    skip_weight = gaussian(arg_keys[4], (C, C), C ** -0.5, 1.0, (), jnp.float32)
    return {"inputs": inputs, "preact": preact, "cotangent": cotangent, "spectral_weight": spectral_weight, "skip_weight": skip_weight}


highest = lax.Precision.HIGHEST
tanh_scale = 0.7978845608028654
cubic_term = 0.044715


def gelu_slope(preact):
    bounded = jnp.tanh(tanh_scale * (preact + cubic_term * preact * preact * preact))
    return 0.5 * (1.0 + bounded) + 0.5 * preact * (1.0 - bounded * bounded) * tanh_scale * (1.0 + 3.0 * cubic_term * preact * preact)


def signed_modes(modes_count):
    positions = jnp.arange(modes_count, dtype=jnp.int32)
    return jnp.where(positions < modes_count // 2, positions, positions - modes_count)


def phases(frequency, grid_size):
    points = jnp.arange(grid_size, dtype=jnp.int32)
    product = jnp.mod(frequency[:, None] * points[None, :], grid_size)
    return (2.0 * jnp.pi / grid_size) * product.astype(jnp.float32)


def make_tables(grid_size, modes_x, modes_y, modes_z):
    angle_y = phases(signed_modes(modes_y), grid_size)
    angle_z = phases(jnp.arange(modes_z, dtype=jnp.int32), grid_size)
    angle_x = phases(signed_modes(modes_x), grid_size)
    cos_y, sin_y = jnp.cos(angle_y), jnp.sin(angle_y)
    cos_z, sin_z = jnp.cos(angle_z), jnp.sin(angle_z)
    cos_x, sin_x = jnp.cos(angle_x), jnp.sin(angle_x)
    forward_y = jnp.stack([cos_y.T, -sin_y.T], 1)
    forward_z = jnp.stack([jnp.stack([cos_z.T, -sin_z.T], 1), jnp.stack([sin_z.T, cos_z.T], 1)], 0)
    forward_x = jnp.stack([jnp.stack([cos_x.T, -sin_x.T], 1), jnp.stack([sin_x.T, cos_x.T], 1)], 0)
    inverse_x = jnp.stack([jnp.stack([cos_x, sin_x], 1), jnp.stack([-sin_x, cos_x], 1)], 0)
    inverse_z = jnp.stack([jnp.stack([cos_z, sin_z], 1), jnp.stack([-sin_z, cos_z], 1)], 0)
    inverse_y = jnp.stack([cos_y, -sin_y], 1)
    return forward_y, forward_z, forward_x, inverse_x, inverse_z, inverse_y


def transform_yz(field, forward_y, forward_z):
    halfway = jnp.einsum("bcxyz,yrj->bcxrjz", field, forward_y, precision=highest)
    mixed = jnp.einsum("bcxrjz,rzsn->sbcxnj", halfway, forward_z, precision=highest)
    return mixed.reshape(mixed.shape[:4] + (mixed.shape[4] * mixed.shape[5],))


def transform_x(stacked, forward_x, norm_scale):
    return jnp.einsum("rbcxk,rxsm->sbcmk", stacked, forward_x, precision=highest) * norm_scale


def weight_terms(spectra, input_spectra):
    real_part = jnp.einsum("bomk,bimk->mkoi", spectra[0], input_spectra[0], precision=highest)
    real_part = real_part + jnp.einsum("bomk,bimk->mkoi", spectra[1], input_spectra[1], precision=highest)
    imag_part = jnp.einsum("bomk,bimk->mkoi", spectra[1], input_spectra[0], precision=highest)
    imag_part = imag_part - jnp.einsum("bomk,bimk->mkoi", spectra[0], input_spectra[1], precision=highest)
    stacked = jnp.stack([real_part, imag_part], 2)
    return stacked.reshape(stacked.shape[0], stacked.shape[1], -1)


def mode_products(weights, spectra):
    channels = spectra.shape[2]
    pieces = weights.reshape(weights.shape[0], weights.shape[1], 2, channels, channels)
    weight_real = pieces[:, :, 0]
    weight_imag = pieces[:, :, 1]
    real_part = jnp.einsum("mkoi,bomk->bimk", weight_real, spectra[0], precision=highest)
    real_part = real_part + jnp.einsum("mkoi,bomk->bimk", weight_imag, spectra[1], precision=highest)
    imag_part = jnp.einsum("mkoi,bomk->bimk", weight_real, spectra[1], precision=highest)
    imag_part = imag_part - jnp.einsum("mkoi,bomk->bimk", weight_imag, spectra[0], precision=highest)
    return jnp.stack([real_part, imag_part], 0)


def restore_x(dual, inverse_x):
    return jnp.einsum("rbcmk,rmsx->sbcxk", dual, inverse_x, precision=highest)


def restore_yz(stacked, inverse_z, inverse_y):
    depth_modes = inverse_z.shape[1]
    shaped = stacked.reshape(stacked.shape[:4] + (depth_modes, stacked.shape[4] // depth_modes))
    planes = jnp.einsum("rbcxnj,rnsz->bcxjsz", shaped, inverse_z, precision=highest)
    return jnp.einsum("bcxjsz,jsy->bcxyz", planes, inverse_y, precision=highest)


def reference(inputs, preact, cotangent, spectral_weight, skip_weight):
    norm_scale = float(N) ** -1.5
    tables = make_tables(N, MX, MY, MZ)
    grad_pre = cotangent * gelu_slope(preact)

    def per_sample(field):
        return transform_x(transform_yz(field[None], tables[0], tables[1]), tables[2], norm_scale)[:, 0]

    spec_grad = jnp.moveaxis(lax.map(per_sample, grad_pre), 0, 1)
    spec_input = jnp.moveaxis(lax.map(per_sample, inputs), 0, 1)
    weight_grad = weight_terms(spec_grad, spec_input)
    dual = mode_products(spectral_weight, spec_grad)

    def back_sample(piece):
        return restore_yz(restore_x(piece[:, None], tables[3]), tables[4], tables[5])[0]

    spatial = lax.map(back_sample, jnp.moveaxis(dual, 1, 0))
    skip_term = jnp.einsum("oi,boxyz->bixyz", skip_weight, grad_pre, precision=highest)
    input_grad = norm_scale * spatial + skip_term
    skip_grad = norm_scale * jnp.einsum("boxyz,bixyz->oi", grad_pre, inputs, precision=highest)
    return input_grad, weight_grad, skip_grad
```

```python
import functools

import jax
import jax.numpy as jnp
import numpy as np
from jax import lax
from jax.experimental import pallas as pl
from jax.experimental.pallas import tpu as pltpu
from jax.sharding import PartitionSpec as P

N = 128
C = 32
MX = 32
MY = 64
MZ = 16
SPACE = 64
GROUPS = C // 2
JL = 16
NORM = float(N) ** (-1.5)
TANH_SCALE = 0.7978845608028654
CUBIC = 0.044715
F32 = jnp.float32
BF16 = jnp.bfloat16
VMEM = 56 * 1024 * 1024


def signed(count):
    index = np.arange(count)
    return np.where(index < count // 2, index, index - count)


def angles(frequency):
    points = np.arange(N)
    return 2.0 * np.pi / N * np.mod(frequency[:, None] * points[None, :], N)


ANGLE_X = angles(signed(MX))
ANGLE_Y = angles(signed(MY))
ANGLE_Z = angles(np.arange(MZ))


def halves(table):
    table = np.asarray(table, np.float64)
    high = table.astype(np.float32).astype(BF16)
    low = (table - high.astype(np.float64)).astype(np.float32).astype(BF16)
    return high, low


def split(value):
    high = value.astype(BF16)
    return high, (value - high.astype(F32)).astype(BF16)


def dot(left, right):
    return jnp.dot(left, right, preferred_element_type=F32)


def z_tables():
    high, low = halves(np.concatenate([np.cos(ANGLE_Z).T, -np.sin(ANGLE_Z).T], 1))
    table = np.zeros((4, 2, N, 2, 4, 2 * MZ), BF16)
    for plane in range(4):
        table[plane, 0, :, 0, plane] = high
        table[plane, 1, :, 0, plane] = high
        table[plane, 0, :, 1, plane] = low
    return table.reshape(8 * N, 256)


def y_tables():
    high, low = halves(np.concatenate([np.cos(ANGLE_Y), -np.sin(ANGLE_Y)], 0))
    return np.concatenate([high, high, low], 1)


def x_tables():
    cos_x, sin_x = np.cos(ANGLE_X), np.sin(ANGLE_X)
    table = np.zeros((2, MX, 2, N))
    table[0, :, 0], table[0, :, 1] = cos_x, sin_x
    table[1, :, 0], table[1, :, 1] = -sin_x, cos_x
    table = table.reshape(2, 2, MX // 2, 2, SPACE, 2).transpose(1, 0, 2, 5, 3, 4) * NORM
    high, low = halves(table.reshape(2 * MX, 4 * SPACE))
    return np.concatenate([high, low], 0)


def back_x_tables():
    cos_x, sin_x = np.cos(ANGLE_X), np.sin(ANGLE_X)
    table = np.zeros((2, MX, 2, N))
    table[0, :, 0], table[0, :, 1] = cos_x, sin_x
    table[1, :, 0], table[1, :, 1] = -sin_x, cos_x
    table = table.reshape(2, 2, MX // 2, 2, SPACE, 2).transpose(5, 3, 4, 1, 0, 2) * NORM
    high, low = halves(table.reshape(4 * SPACE, 2 * MX))
    return np.concatenate([high, high, low], 1)


def back_y_tables():
    high, low = halves(np.concatenate([np.cos(ANGLE_Y).T, np.sin(ANGLE_Y).T], 1))
    return np.concatenate([high, high, low], 1)


def back_z_tables():
    high, low = halves(np.concatenate([np.cos(ANGLE_Z), -np.sin(ANGLE_Z)], 0))
    table = np.zeros((3, 4, 2 * MZ, 4, N), BF16)
    for plane in range(4):
        table[0, plane, :, plane] = high
        table[1, plane, :, plane] = high
        table[2, plane, :, plane] = low
    return table.reshape(3 * 128, 4 * N)


def channel_order():
    return np.arange(C).reshape(2, 8, 2).transpose(0, 2, 1).reshape(-1)


def reorder_table():
    table = np.zeros((C, JL, JL, C), BF16)
    order = channel_order()
    for place in range(C):
        for j in range(JL):
            table[place, j, j, order[place]] = 1
    return table.reshape(C * JL, JL * C)


def spread_table():
    table = np.zeros((C, C, C), BF16)
    for o in range(C):
        table[o, o, :] = 1
    table = table.reshape(C, C * C)
    return np.concatenate([table, table], 0)


def skip_matrix(skip_weight):
    order = np.arange(C).reshape(GROUPS, 2).T.reshape(-1)
    eye = jnp.eye(8, dtype=F32)
    matrix = skip_weight.T[:, order][:, None, :, None] * eye[None, :, None, :]
    return matrix.reshape(256, 256)


def fold_table():
    table = np.zeros((2, GROUPS, 8, C), np.float32)
    for inner in range(2):
        for group in range(GROUPS):
            table[inner, group, :, 2 * group + inner] = 1
    return table.reshape(256, C)


def gelu_slope(h):
    square = h * h
    t = jnp.tanh(h * (TANH_SCALE + (TANH_SCALE * CUBIC) * square))
    inner = h * (0.5 * TANH_SCALE + (1.5 * TANH_SCALE * CUBIC) * square)
    return (0.5 + 0.5 * t) + (1.0 - t * t) * inner


def lane_swap(value, first_sign):
    lanes = lax.broadcasted_iota(jnp.int32, value.shape, value.ndim - 1)
    up = pltpu.roll(value, 128 - MZ, value.ndim - 1)
    down = pltpu.roll(value, MZ, value.ndim - 1)
    return jnp.where((lanes & MZ) == 0, first_sign * up, -first_sign * down)


YB = 16


def forward_kernel(
    pre_ref, cot_ref, inp_ref, ztab_ref, ytab_ref, skip_ref, fold_ref,
    sendg_ref, sendi_ref, term_ref, zg, zi, acc, half,
):
    step = pl.program_id(0)

    @pl.when(step == 0)
    def _():
        acc[...] = jnp.zeros_like(acc)

    skip_high, skip_low = split(skip_ref[...])
    for chunk in range(YB // 8):
        rows = slice(8 * chunk, 8 * chunk + 8)
        grad = cot_ref[0, :, :, rows, :] * gelu_slope(pre_ref[0, :, :, rows, :])
        field = inp_ref[0, :, :, rows, :]
        pieces = []
        for value, scratch in ((grad, zg), (field, zi)):
            value = value.reshape(GROUPS, 2, 2, 8, N)
            high, low = {}, {}
            for inner in range(2):
                for plane in range(2):
                    block = value[:, inner, plane].reshape(GROUPS * 8, N)
                    high[inner, plane], low[inner, plane] = split(block)
            wide = []
            for inner in range(2):
                for plane in range(2):
                    wide += [high[inner, plane], low[inner, plane]]
            out = dot(jnp.concatenate(wide, 1), ztab_ref[...])
            out = out[:, :128] + out[:, 128:]
            place = pl.multiple_of(step * YB + 8 * chunk, 8)
            scratch[:, pl.ds(place, 8), :] = out.reshape(GROUPS, 8, 128)
            pieces.append([
                jnp.concatenate([
                    jnp.concatenate([part[inner, 0], part[inner, 1]], 1) for inner in range(2)
                ], 0)
                for part in (high, low)
            ])
        (g_high, g_low), (i_high, i_low) = pieces
        term = dot(skip_high, g_high) + dot(skip_high, g_low) + dot(skip_low, g_high)
        for plane in range(2):
            term_ref[:, plane, rows, :] = term[:, 128 * plane:128 * plane + 128].reshape(C, 8, N)
        contract = (((1,), (1,)), ((), ()))
        acc[...] += (
            lax.dot_general(g_high, i_high, contract, preferred_element_type=F32)
            + lax.dot_general(g_low, i_high, contract, preferred_element_type=F32)
            + lax.dot_general(g_high, i_low, contract, preferred_element_type=F32)
        )

    @pl.when(step == pl.num_programs(0) - 1)
    def _():
        for scratch, send_ref, rows_each in ((zg, sendg_ref, 16), (zi, sendi_ref, 24)):
            for pair in range(GROUPS // 2):
                wide = jnp.concatenate([scratch[2 * pair], scratch[2 * pair + 1]], 1)
                high, low = split(wide)
                out = dot(ytab_ref[...], jnp.concatenate([high, low, high], 0))
                for member in range(2):
                    mine = out[:, 128 * member:128 * member + 128]
                    half[2 * pair + member] = mine[:MY] + lane_swap(mine[MY:], -1.0)
            for jq in range(4):
                for group_set in range(2):
                    block = half[8 * group_set:8 * group_set + 8, JL * jq:JL * jq + JL, :]
                    turned = block.reshape(128, 128).T
                    for r in range(8):
                        row = jq * rows_each + 8 * group_set + r
                        send_ref[pl.ds(row, MZ, stride=4 * rows_each), :] = turned[MZ * r:MZ * r + MZ]
        left = lax.broadcasted_iota(jnp.int32, (256, 256), 0) & 7
        right = lax.broadcasted_iota(jnp.int32, (256, 256), 1) & 7
        kept = jnp.where(left == right, acc[...], 0.0) * NORM
        fold = fold_ref[...]
        folded = jnp.dot(kept, fold, preferred_element_type=F32, precision=lax.Precision.HIGHEST)
        summed = lax.dot_general(
            fold, folded, (((0,), (0,)), ((), ())), preferred_element_type=F32,
            precision=lax.Precision.HIGHEST,
        )
        tile = jnp.concatenate([summed[8 * q:8 * q + 8, :] for q in range(4)], 1)
        for dest in range(SPACE):
            sendi_ref[24 * dest + 16:24 * dest + 24, :] = tile


def forward(preact, cotangent, inputs, skip_weight):
    field = pl.BlockSpec((1, C, 2, YB, N), lambda s: (0, 0, 0, s, 0))
    whole = lambda *shape: pl.BlockSpec(shape, lambda s: (0,) * len(shape))
    return pl.pallas_call(
        forward_kernel,
        grid=(N // YB,),
        in_specs=[field, field, field, whole(1024, 256), whole(128, 384), whole(256, 256), whole(256, C)],
        out_specs=[
            whole(SPACE * 16, 128), whole(SPACE * 24, 128),
            pl.BlockSpec((C, 2, YB, N), lambda s: (0, 0, s, 0)),
        ],
        out_shape=[
            jax.ShapeDtypeStruct((SPACE * 16, 128), F32),
            jax.ShapeDtypeStruct((SPACE * 24, 128), F32),
            jax.ShapeDtypeStruct((C, 2, N, N), F32),
        ],
        scratch_shapes=[
            pltpu.VMEM((GROUPS, N, 128), F32), pltpu.VMEM((GROUPS, N, 128), F32),
            pltpu.VMEM((256, 256), F32), pltpu.VMEM((GROUPS, MY, 128), F32),
        ],
        compiler_params=pltpu.CompilerParams(vmem_limit_bytes=VMEM),
        name="forward",
    )(preact, cotangent, inputs, z_tables(), y_tables(), skip_matrix(skip_weight), fold_table())


def transform_x(recv_ref, rows_each, xtab_ref, reorder_ref):
    blocks = []
    for q in range(4):
        column = [recv_ref[pl.ds(4 * q + r, SPACE, stride=rows_each), :] for r in range(4)]
        blocks.append(jnp.concatenate(column, 0))
    high, low = split(jnp.concatenate(blocks, 1))
    out = dot(xtab_ref[...], high)
    spectrum = out[:2 * MX] + out[2 * MX:] + dot(xtab_ref[:2 * MX], low)
    high, low = split(spectrum)
    return dot(high, reorder_ref[...]) + dot(low, reorder_ref[...])


def to_rows(spectrum, scratch):
    for j in range(JL):
        scratch[:, j, :] = spectrum[:, C * j:C * j + C]


def middle_kernel(
    dp_ref, recv_ref, w_ref, xtab_ref, reorder_ref, spread_ref, back_ref, unorder_ref,
    send_ref, mine_ref, theirs_ref, spec, dual,
):
    spectrum = transform_x(recv_ref, 16, xtab_ref, reorder_ref)
    first = dp_ref[0] == 0
    mine_ref[...] = jnp.where(first, spectrum[:MX], spectrum[MX:])
    theirs_ref[...] = jnp.where(first, spectrum[MX:], spectrum[:MX])
    to_rows(spectrum, spec)

    def one(step, _):
        m_half = step // 16
        m = step - 16 * m_half
        where = 32 * m_half + m
        both = jnp.concatenate([spec[where], spec[where + 16]], 0)
        high, low = split(both)
        wide = dot(jnp.concatenate([high, low], 1), spread_ref[...])
        real, imag = wide[:JL], wide[JL:]
        w_real = w_ref[step, :, :C * C]
        w_imag = w_ref[step, :, C * C:]
        out_real = w_real * real + w_imag * imag
        out_imag = w_real * imag - w_imag * real
        for value, place in ((out_real, where), (out_imag, where + 16)):
            total = value[:, :128]
            for tile in range(1, 8):
                total = total + value[:, 128 * tile:128 * tile + 128]
            total = total + pltpu.roll(total, 64, 1)
            total = total + pltpu.roll(total, 32, 1)
            dual[place] = total
        return 0

    lax.fori_loop(0, MX, one, 0, unroll=4)

    lanes = lax.broadcasted_iota(jnp.int32, (2 * MX, 128), 1) // C
    blocks = []
    for j4 in range(4):
        block = dual[:, 4 * j4, :]
        for k in range(1, 4):
            block = jnp.where(lanes == k, dual[:, 4 * j4 + k, :], block)
        blocks.append(block)
    high, low = split(jnp.concatenate(blocks, 1))
    ordered = dot(high, unorder_ref[...]) + dot(low, unorder_ref[...])
    high, low = split(ordered)
    out = dot(back_ref[...], jnp.concatenate([high, low, high], 0))
    for q in range(4):
        for r in range(4):
            send_ref[pl.ds(4 * q + r, SPACE, stride=16), :] = (
                out[SPACE * r:SPACE * r + SPACE, 128 * q:128 * q + 128]
            )


def in_vmem(count):
    return [pl.BlockSpec(memory_space=pltpu.VMEM) for _ in range(count)]


def middle(dp, received, weights):
    reorder = reorder_table()
    return pl.pallas_call(
        middle_kernel,
        in_specs=[pl.BlockSpec(memory_space=pltpu.SMEM)] + in_vmem(7),
        out_specs=in_vmem(3),
        out_shape=[
            jax.ShapeDtypeStruct((SPACE * 16, 128), F32),
            jax.ShapeDtypeStruct((MX, JL * C), F32),
            jax.ShapeDtypeStruct((MX, JL * C), F32),
        ],
        scratch_shapes=[pltpu.VMEM((2 * MX, JL, C), F32), pltpu.VMEM((2 * MX, JL, 128), F32)],
        compiler_params=pltpu.CompilerParams(vmem_limit_bytes=VMEM),
        name="middle",
    )(dp, received, weights, x_tables(), reorder, spread_table(), back_x_tables(), reorder.T.copy())


def inputs_kernel(dp_ref, recv_ref, theirs_ref, xtab_ref, reorder_ref, mine_ref, out_ref):
    spectrum = transform_x(recv_ref, 24, xtab_ref, reorder_ref)
    first = dp_ref[0] == 0
    mine_ref[...] = jnp.where(first, spectrum[:MX], spectrum[MX:])
    out_ref[:MX, :] = theirs_ref[...]
    out_ref[MX:2 * MX, :] = jnp.where(first, spectrum[MX:], spectrum[:MX])
    total = recv_ref[16:24, :]
    for source in range(1, SPACE):
        total = total + recv_ref[24 * source + 16:24 * source + 24, :]
    out_ref[2 * MX:, :] = jnp.concatenate([total] * 4, 1)


def inputs_spectrum(dp, received, theirs):
    return pl.pallas_call(
        inputs_kernel,
        in_specs=[pl.BlockSpec(memory_space=pltpu.SMEM)] + in_vmem(4),
        out_specs=in_vmem(2),
        out_shape=[
            jax.ShapeDtypeStruct((MX, JL * C), F32),
            jax.ShapeDtypeStruct((2 * MX + 8, JL * C), F32),
        ],
        compiler_params=pltpu.CompilerParams(vmem_limit_bytes=VMEM),
        name="inputs_spectrum",
    )(dp, received, theirs, x_tables(), reorder_table())


MB = 4


def weight_kernel(
    grad_ref, field_ref, sent_ref, got_ref, spread_ref, out_ref, skip_ref, grads, fields,
):
    step = pl.program_id(0)

    @pl.when(step == 0)
    def _():
        to_rows(grad_ref[...], grads.at[0])
        to_rows(got_ref[:MX], grads.at[1])
        for b, value in enumerate((field_ref[...], got_ref[MX:2 * MX])):
            for j in range(JL):
                piece = value[:, C * j:C * j + C]
                fields[b, :, j, :] = jnp.concatenate([piece] * 4, 1)
        total = sent_ref[2 * MX:, :128] + got_ref[2 * MX:, :128]
        for q in range(4):
            skip_ref[8 * q:8 * q + 8, :] = total[:, C * q:C * q + C]

    for local in range(MB):
        m = step * MB + local
        rows = jnp.concatenate([grads[b, m + 16 * s] for b in range(2) for s in range(2)], 0)
        high, low = split(rows)
        wide = dot(jnp.concatenate([high, low], 1), spread_ref[...])
        in_parts = [fields[b, m + 16 * s] for b in range(2) for s in range(2)]
        for tile in range(8):
            lanes = slice(128 * tile, 128 * tile + 128)
            g = [wide[JL * q:JL * q + JL, lanes] for q in range(4)]
            out_ref[local, :, 128 * tile:128 * tile + 128] = (
                g[0] * in_parts[0] + g[1] * in_parts[1] + g[2] * in_parts[2] + g[3] * in_parts[3]
            )
            out_ref[local, :, 1024 + 128 * tile:1024 + 128 * tile + 128] = (
                g[1] * in_parts[0] - g[0] * in_parts[1] + g[3] * in_parts[2] - g[2] * in_parts[3]
            )


def weight_gradient(grad_mine, field_mine, sent, got):
    whole = lambda *shape: pl.BlockSpec(shape, lambda s: (0,) * len(shape))
    return pl.pallas_call(
        weight_kernel,
        grid=(16 // MB,),
        in_specs=[whole(MX, 512), whole(MX, 512), whole(2 * MX + 8, 512), whole(2 * MX + 8, 512), whole(64, 1024)],
        out_specs=[pl.BlockSpec((MB, JL, 2048), lambda s: (s, 0, 0)), whole(C, C)],
        out_shape=[
            jax.ShapeDtypeStruct((16, JL, 2 * C * C), F32),
            jax.ShapeDtypeStruct((C, C), F32),
        ],
        scratch_shapes=[pltpu.VMEM((2, MX, JL, C), F32), pltpu.VMEM((2, MX, JL, 128), F32)],
        compiler_params=pltpu.CompilerParams(vmem_limit_bytes=VMEM),
        name="weight_gradient",
    )(grad_mine, field_mine, sent, got, spread_table())


def backward_kernel(recv_ref, term_ref, ytab_ref, ztab_ref, out_ref, half):
    step = pl.program_id(0)

    @pl.when(step == 0)
    def _():
        for jq in range(4):
            for group_set in range(2):
                rows = [
                    recv_ref[pl.ds(jq * 16 + 8 * group_set + r, MZ, stride=64), :] for r in range(8)
                ]
                turned = jnp.concatenate(rows, 0).T
                half[8 * group_set:8 * group_set + 8, JL * jq:JL * jq + JL, :] = turned.reshape(8, JL, 128)

    both = []
    for member in range(2):
        value = half[2 * step + member]
        both.append(jnp.concatenate([value, lane_swap(value, -1.0)], 0))
    high, low = split(jnp.concatenate(both, 1))
    lines = dot(ytab_ref[...], jnp.concatenate([high, low, high], 0))
    lines = jnp.concatenate([lines[:, :128], lines[:, 128:]], 0)
    high, low = split(lines)
    out = dot(jnp.concatenate([high, low, high], 1), ztab_ref[...])
    for member in range(2):
        for inner in range(2):
            for plane in range(2):
                lane = 128 * (2 * inner + plane)
                out_ref[0, 2 * member + inner, plane] = (
                    out[128 * member:128 * member + 128, lane:lane + 128]
                    + term_ref[2 * member + inner, plane]
                )


def backward(received, term):
    whole = lambda *shape: pl.BlockSpec(shape, lambda s: (0,) * len(shape))
    return pl.pallas_call(
        backward_kernel,
        grid=(GROUPS // 2,),
        in_specs=[
            whole(SPACE * 16, 128), pl.BlockSpec((4, 2, N, N), lambda s: (s, 0, 0, 0)),
            whole(128, 384), whole(384, 512),
        ],
        out_specs=pl.BlockSpec((1, 4, 2, N, N), lambda s: (0, s, 0, 0, 0)),
        out_shape=jax.ShapeDtypeStruct((1, C, 2, N, N), F32),
        scratch_shapes=[pltpu.VMEM((GROUPS, MY, 128), F32)],
        compiler_params=pltpu.CompilerParams(vmem_limit_bytes=VMEM),
        name="backward",
    )(received, term, back_y_tables(), back_z_tables())


def exchange(sent, rows):
    swapped = lax.all_to_all(sent.reshape(SPACE, rows, 128), "space", 0, 0, tiled=True)
    return swapped.reshape(SPACE * rows, 128)


def body(inputs, preact, cotangent, spectral_weight, skip_weight):
    dp = lax.axis_index("dp").astype(jnp.int32).reshape(1)
    send_grad, send_input, term = forward(preact, cotangent, inputs, skip_weight)
    got_grad = exchange(send_grad, 16)
    got_input = exchange(send_input, 24)
    send_dual, grad_mine, grad_theirs = middle(dp, got_grad, spectral_weight)
    got_dual = exchange(send_dual, 16)
    field_mine, sent = inputs_spectrum(dp, got_input, grad_theirs)
    got = lax.ppermute(sent, "dp", [(0, 1), (1, 0)])
    weight_grad, skip_grad = weight_gradient(grad_mine, field_mine, sent, got)
    input_grad = backward(got_dual, term)
    return input_grad, weight_grad, skip_grad


def solution(mesh):
    in_specs = (
        P("dp", None, "space", None, None),
        P("dp", None, "space", None, None),
        P("dp", None, "space", None, None),
        P(None, "space", None),
        P(),
    )
    out_specs = (P("dp", None, "space", None, None), P("dp", "space", None), P())
    return jax.shard_map(body, mesh=mesh, in_specs=in_specs, out_specs=out_specs, check_vma=False)
```

```python
import functools

import jax
import jax.numpy as jnp
import numpy as np
from jax import lax
from jax.experimental import pallas as pl
from jax.experimental.pallas import tpu as pltpu
from jax.sharding import PartitionSpec as P

N = 128
C = 32
MX = 32
MY = 64
MZ = 16
SPACE = 64
GROUPS = C // 2
JL = 16
NORM = float(N) ** (-1.5)
TANH_SCALE = 0.7978845608028654
CUBIC = 0.044715
F32 = jnp.float32
BF16 = jnp.bfloat16
LIMIT = 40 * 1024 * 1024


def signed(count):
    index = np.arange(count)
    return np.where(index < count // 2, index, index - count)


def angles(frequency):
    points = np.arange(N)
    return 2.0 * np.pi / N * np.mod(frequency[:, None] * points[None, :], N)


ANGLE_X = angles(signed(MX))
ANGLE_Y = angles(signed(MY))
ANGLE_Z = angles(np.arange(MZ))


def halves(table):
    table = np.asarray(table, np.float64)
    high = table.astype(np.float32).astype(BF16)
    low = (table - high.astype(np.float64)).astype(np.float32).astype(BF16)
    return high, low


def split(value):
    high = value.astype(BF16)
    return high, (value - high.astype(F32)).astype(BF16)


def dot(left, right):
    return jnp.dot(left, right, preferred_element_type=F32)


def z_tables():
    high, low = halves(np.concatenate([np.cos(ANGLE_Z).T, -np.sin(ANGLE_Z).T], 1))
    table = np.zeros((4, 2, N, 2, 4, 2 * MZ), BF16)
    for plane in range(4):
        table[plane, 0, :, 0, plane] = high
        table[plane, 1, :, 0, plane] = high
        table[plane, 0, :, 1, plane] = low
    return table.reshape(8 * N, 256)


def y_tables():
    high, low = halves(np.concatenate([np.cos(ANGLE_Y), -np.sin(ANGLE_Y)], 0))
    return np.concatenate([high, high, low], 1)


def x_tables():
    cos_x, sin_x = np.cos(ANGLE_X), np.sin(ANGLE_X)
    table = np.zeros((2, MX, 2, N))
    table[0, :, 0], table[0, :, 1] = cos_x, sin_x
    table[1, :, 0], table[1, :, 1] = -sin_x, cos_x
    table = table.reshape(2, 2, MX // 2, 2, SPACE, 2).transpose(1, 0, 2, 5, 3, 4) * NORM
    high, low = halves(table.reshape(2 * MX, 4 * SPACE))
    return np.concatenate([high, low], 0)


def back_x_tables():
    cos_x, sin_x = np.cos(ANGLE_X), np.sin(ANGLE_X)
    table = np.zeros((2, MX, 2, N))
    table[0, :, 0], table[0, :, 1] = cos_x, sin_x
    table[1, :, 0], table[1, :, 1] = -sin_x, cos_x
    table = table.reshape(2, 2, MX // 2, 2, SPACE, 2).transpose(5, 3, 4, 1, 0, 2) * NORM
    high, low = halves(table.reshape(4 * SPACE, 2 * MX))
    return np.concatenate([high, high, low], 1)


def back_y_tables():
    high, low = halves(np.concatenate([np.cos(ANGLE_Y).T, np.sin(ANGLE_Y).T], 1))
    return np.concatenate([high, high, low], 1)


def back_z_tables():
    high, low = halves(np.concatenate([np.cos(ANGLE_Z), -np.sin(ANGLE_Z)], 0))
    table = np.zeros((3, 4, 2 * MZ, 4, N), BF16)
    for plane in range(4):
        table[0, plane, :, plane] = high
        table[1, plane, :, plane] = high
        table[2, plane, :, plane] = low
    return table.reshape(3 * 128, 4 * N)


def one_hot(hits):
    return jnp.where(hits, 1.0, 0.0).astype(BF16)


def reorder_matrix():
    row = lax.broadcasted_iota(jnp.int32, (C * JL, C * JL), 0)
    column = lax.broadcasted_iota(jnp.int32, (C * JL, C * JL), 1)
    sent, j = row >> 4, row & (JL - 1)
    channel = ((sent >> 4) * 8 + (sent & 7)) * 2 + ((sent >> 3) & 1)
    return one_hot(column == j * C + channel)


def spread_matrix():
    row = lax.broadcasted_iota(jnp.int32, (2 * C, C * C), 0)
    column = lax.broadcasted_iota(jnp.int32, (2 * C, C * C), 1)
    return one_hot((row & (C - 1)) == (column >> 5))


def rows_table():
    return np.repeat(np.eye(C), 8, 0).astype(BF16)


def fold_table():
    table = np.zeros((2, GROUPS, 8, C), BF16)
    for inner in range(2):
        for group in range(GROUPS):
            table[inner, group, :, 2 * group + inner] = 1
    return table.reshape(256, C)


def gelu_slope(h):
    square = h * h
    t = jnp.tanh(h * (TANH_SCALE + (TANH_SCALE * CUBIC) * square))
    inner = h * (0.5 * TANH_SCALE + (1.5 * TANH_SCALE * CUBIC) * square)
    return (0.5 + 0.5 * t) + (1.0 - t * t) * inner


def lane_swap(value, first_sign):
    lanes = lax.broadcasted_iota(jnp.int32, value.shape, value.ndim - 1)
    up = pltpu.roll(value, 128 - MZ, value.ndim - 1)
    down = pltpu.roll(value, MZ, value.ndim - 1)
    return jnp.where((lanes & MZ) == 0, first_sign * up, -first_sign * down)


YB = 32
CHUNKS = N // YB
TILES = YB // 8


def chunk_copy(ref, buffer, sem, chunk):
    rows = pl.ds(YB * chunk, YB)
    copy = pltpu.make_async_copy(ref.at[0, :, :, rows, :], buffer.at[:, :, rows, :], sem)
    copy.start()
    return copy


def whole_copy(ref, buffer, sem):
    copy = pltpu.make_async_copy(ref, buffer, sem)
    copy.start()
    return copy


def spread_planes(value, highs, lows, tile):
    value = value.reshape(GROUPS, 2, 2, 8, N)
    for inner in range(2):
        for plane in range(2):
            high, low = split(value[:, inner, plane].reshape(GROUPS * 8, N))
            place = (tile, slice(128 * inner, 128 * inner + 128), slice(128 * plane, 128 * plane + 128))
            highs[place] = high
            lows[place] = low


def transform_z(highs, lows, ztab_ref, scratch, chunk):
    rows = []
    for tile in range(TILES * chunk, TILES * chunk + TILES):
        wide = []
        for inner in range(2):
            for plane in range(2):
                place = (tile, slice(128 * inner, 128 * inner + 128), slice(128 * plane, 128 * plane + 128))
                wide += [highs[place], lows[place]]
        rows.append(jnp.concatenate(wide, 1))
    out = dot(jnp.concatenate(rows, 0), ztab_ref[...])
    out = out[:, :128] + out[:, 128:]
    for tile in range(TILES):
        place = YB * chunk + 8 * tile
        scratch[:, place:place + 8, :] = out[128 * tile:128 * tile + 128].reshape(GROUPS, 8, 128)


def transform_y(scratch, ytab_ref, half, send_ref, offset):
    for pair in range(GROUPS // 2):
        wide = jnp.concatenate([scratch[2 * pair], scratch[2 * pair + 1]], 1)
        high, low = split(wide)
        out = dot(ytab_ref[...], jnp.concatenate([high, low, high], 0))
        for member in range(2):
            mine = out[:, 128 * member:128 * member + 128]
            half[2 * pair + member] = mine[:MY] + lane_swap(mine[MY:], -1.0)
    for jq in range(4):
        for group_set in range(2):
            block = half[8 * group_set:8 * group_set + 8, JL * jq:JL * jq + JL, :]
            turned = block.reshape(128, 128).T
            for r in range(8):
                row = offset + 8 * group_set + r
                send_ref[pl.ds(jq, MZ, stride=4), row, :] = turned[MZ * r:MZ * r + MZ]


def forward_kernel(
    pre_hbm, cot_hbm, inp_hbm, ztab_hbm, ytab_hbm, send_hbm,
    pre, cot, inp, ztab, ytab, g_high, g_low, i_high, i_low, g_lines, i_lines, half, send, sems, tab_sems, out_sems,
):
    copies = []
    for chunk in range(CHUNKS):
        copies.append([
            chunk_copy(ref, buffer, sems.at[chunk, k], chunk)
            for k, (ref, buffer) in enumerate(((inp_hbm, inp), (pre_hbm, pre), (cot_hbm, cot)))
        ])
        if chunk == 0:
            ztab_copy = whole_copy(ztab_hbm, ztab, tab_sems.at[0])
    ytab_copy = whole_copy(ytab_hbm, ytab, tab_sems.at[1])
    for chunk in range(CHUNKS):
        tiles = range(TILES * chunk, TILES * chunk + TILES)
        copies[chunk][0].wait()
        for tile in tiles:
            spread_planes(inp[:, :, 8 * tile:8 * tile + 8, :], i_high, i_low, tile)
        if chunk == 0:
            ztab_copy.wait()
        transform_z(i_high, i_low, ztab, i_lines, chunk)
        copies[chunk][1].wait()
        copies[chunk][2].wait()
        for tile in tiles:
            rows = slice(8 * tile, 8 * tile + 8)
            spread_planes(cot[:, :, rows, :] * gelu_slope(pre[:, :, rows, :]), g_high, g_low, tile)
        transform_z(g_high, g_low, ztab, g_lines, chunk)
    ytab_copy.wait()
    outs = []
    for k, lines in enumerate((g_lines, i_lines)):
        transform_y(lines, ytab, half.at[k], send, 16 * k)
        rows = pl.ds(16 * k, 16)
        outs.append(whole_copy(send.at[:, rows], send_hbm.at[:, rows], out_sems.at[k]))
    for copy in outs:
        copy.wait()


def in_vmem(count):
    return [pl.BlockSpec(memory_space=pltpu.VMEM) for _ in range(count)]


def vmem_spec():
    return pl.BlockSpec(memory_space=pltpu.VMEM)


def any_spec():
    return pl.BlockSpec(memory_space=pl.ANY)


FIELD = (C, 2, N, N)
HALF = (C // 2, 2, N, N)


PAIR = (N // 8, 256, 256)


def in_hbm(value):
    return pltpu.with_memory_space_constraint(value, pltpu.HBM)


def kept(value):
    return pltpu.with_memory_space_constraint(value, pltpu.VMEM)


def forward(preact, cotangent, inputs):
    ztab, ytab = jnp.asarray(z_tables()), jnp.asarray(y_tables())
    return pl.pallas_call(
        forward_kernel,
        in_specs=[any_spec()] * 5,
        out_specs=any_spec(),
        out_shape=pltpu.HBM((SPACE, FIRST, 128), F32),
        scratch_shapes=[pltpu.VMEM(FIELD, F32)] * 3 + [
            pltpu.VMEM(ztab.shape, BF16), pltpu.VMEM(ytab.shape, BF16),
        ] + [pltpu.VMEM(PAIR, BF16)] * 4 + [
            pltpu.VMEM((GROUPS, N, 128), F32), pltpu.VMEM((GROUPS, N, 128), F32),
            pltpu.VMEM((2, GROUPS, MY, 128), F32), pltpu.VMEM((SPACE, FIRST, 128), F32),
            pltpu.SemaphoreType.DMA((CHUNKS, 3)), pltpu.SemaphoreType.DMA((2,)), pltpu.SemaphoreType.DMA((2,)),
        ],
        compiler_params=pltpu.CompilerParams(vmem_limit_bytes=LIMIT),
        name="forward",
    )(in_hbm(preact), in_hbm(cotangent), in_hbm(inputs), in_hbm(ztab), in_hbm(ytab))


ACROSS = (((1,), (1,)), ((), ()))


def same_row():
    left = lax.broadcasted_iota(jnp.int32, (256, 256), 0) & 7
    right = lax.broadcasted_iota(jnp.int32, (256, 256), 1) & 7
    return left == right


def skip_kernel(
    pre_hbm, cot_hbm, inp_hbm, skip_ref, rows_ref, fold_ref, near, term_hbm, part_ref,
    pre, cot, inp, term, g_high, g_low, i_high, i_low, acc, sems, out_sems,
):
    copies = []
    for chunk in range(CHUNKS):
        copies.append([
            chunk_copy(ref, buffer, sems.at[chunk, k], chunk)
            for k, (ref, buffer) in enumerate(((inp_hbm, inp), (pre_hbm, pre), (cot_hbm, cot)))
        ])
    matrix = []
    for part in split(skip_ref[...]):
        wide = lax.dot_general(rows_ref[...], part, ACROSS, preferred_element_type=F32).astype(BF16)
        wide = lax.dot_general(wide, fold_ref[...], ACROSS, preferred_element_type=F32)
        matrix.append(jnp.where(same_row(), wide, 0.0).astype(BF16))
    matrix = jnp.concatenate(matrix, 0)
    outs = []
    for chunk in range(CHUNKS):
        for copy in copies[chunk]:
            copy.wait()
        for tile in range(TILES * chunk, TILES * chunk + TILES):
            rows = slice(8 * tile, 8 * tile + 8)
            spread_planes(inp[:, :, rows, :], i_high, i_low, tile)
            spread_planes(cot[:, :, rows, :] * gelu_slope(pre[:, :, rows, :]), g_high, g_low, tile)
            out = dot(matrix, g_high[tile])
            out = out[:256] + out[256:] + dot(matrix[:256], g_low[tile])
            for plane in range(2):
                value = out[:, 128 * plane:128 * plane + 128].reshape(C, 8, N)
                near[:, plane, rows, :] = value[:C // 2]
                term[:, plane, rows, :] = value[C // 2:]
            total = (
                lax.dot_general(g_high[tile], i_high[tile], ACROSS, preferred_element_type=F32)
                + lax.dot_general(g_low[tile], i_high[tile], ACROSS, preferred_element_type=F32)
                + lax.dot_general(g_high[tile], i_low[tile], ACROSS, preferred_element_type=F32)
            )
            if tile == 0:
                acc[...] = total
            else:
                acc[...] += total
        rows = pl.ds(YB * chunk, YB)
        outs.append(whole_copy(term.at[:, :, rows, :], term_hbm.at[:, :, rows, :], out_sems.at[chunk]))
    diagonal = jnp.where(same_row(), acc[...], 0.0) * NORM
    fold = fold_ref[...].astype(F32)
    folded = jnp.dot(diagonal, fold, preferred_element_type=F32, precision=lax.Precision.HIGHEST)
    summed = lax.dot_general(
        fold, folded, (((0,), (0,)), ((), ())), preferred_element_type=F32,
        precision=lax.Precision.HIGHEST,
    )
    part_ref[...] = jnp.concatenate([summed[8 * q:8 * q + 8, :] for q in range(4)], 1)
    for copy in outs:
        copy.wait()


def skip_products(preact, cotangent, inputs, skip_weight):
    return pl.pallas_call(
        skip_kernel,
        in_specs=[any_spec()] * 3 + in_vmem(3),
        out_specs=[vmem_spec(), any_spec(), vmem_spec()],
        out_shape=[pltpu.VMEM(HALF, F32), pltpu.HBM(HALF, F32), jax.ShapeDtypeStruct((8, 128), F32)],
        scratch_shapes=[pltpu.VMEM(FIELD, F32)] * 3 + [pltpu.VMEM(HALF, F32)] + [pltpu.VMEM(PAIR, BF16)] * 4 + [
            pltpu.VMEM((256, 256), F32),
            pltpu.SemaphoreType.DMA((CHUNKS, 3)), pltpu.SemaphoreType.DMA((CHUNKS,)),
        ],
        compiler_params=pltpu.CompilerParams(vmem_limit_bytes=LIMIT),
        name="skip_products",
    )(in_hbm(preact), in_hbm(cotangent), in_hbm(inputs), skip_weight, rows_table(), fold_table())


FIRST = 32
SECOND = 24


def transform_x(recv_ref, offset, xtab_ref, reorder):
    blocks = []
    for q in range(4):
        column = [recv_ref[pl.ds(offset + 4 * q + r, SPACE, stride=FIRST), :] for r in range(4)]
        blocks.append(jnp.concatenate(column, 0))
    high, low = split(jnp.concatenate(blocks, 1))
    out = dot(xtab_ref[...], high)
    spectrum = out[:2 * MX] + out[2 * MX:] + dot(xtab_ref[:2 * MX], low)
    out = dot(jnp.concatenate(split(spectrum), 0), reorder)
    return out[:2 * MX] + out[2 * MX:]


def to_rows(spectrum, scratch):
    for j in range(JL):
        scratch[:, j, :] = spectrum[:, C * j:C * j + C]


def spectrum_kernel(dp_ref, recv_ref, xtab_ref, part_ref, w_hbm, spec_ref, mine_ref, theirs_ref, w_ref, sem):
    early = whole_copy(w_hbm.at[pl.ds(0, MX // 2)], w_ref, sem.at[0])
    reorder = reorder_matrix()
    first = dp_ref[0] == 0
    for k in range(2):
        spectrum = transform_x(recv_ref, 16 * k, xtab_ref, reorder)
        if k == 0:
            spec_ref[...] = spectrum
        mine_ref[MX * k:MX * k + MX, :] = jnp.where(first, spectrum[:MX], spectrum[MX:])
        theirs_ref[MX * k:MX * k + MX, :] = jnp.where(first, spectrum[MX:], spectrum[:MX])
    early.wait()


def spectra(dp, received, part, weights):
    return pl.pallas_call(
        spectrum_kernel,
        in_specs=[pl.BlockSpec(memory_space=pltpu.SMEM)] + in_vmem(2) + [any_spec()] * 2,
        out_specs=in_vmem(4),
        out_shape=[
            jax.ShapeDtypeStruct((2 * MX, JL * C), F32),
            jax.ShapeDtypeStruct((2 * MX, JL * C), F32),
            jax.ShapeDtypeStruct((2 * MX, JL * C), F32),
            pltpu.VMEM((MX // 2, JL, 2 * C * C), F32),
        ],
        scratch_shapes=[pltpu.SemaphoreType.DMA((1,))],
        compiler_params=pltpu.CompilerParams(vmem_limit_bytes=LIMIT),
        name="spectra",
    )(dp, received, x_tables(), part, in_hbm(weights))


WB = 8


def dual_kernel(
    spec_ref, early_ref, w_hbm, dual, late_ref, spec, wide, sems,
):
    copies = []
    for block in range(MX // WB // 2):
        rows = pl.ds(WB * block, WB)
        copies.append(whole_copy(w_hbm.at[pl.ds(MX // 2 + WB * block, WB)], late_ref.at[rows], sems.at[block]))
    spread = spread_matrix()
    to_rows(spec_ref[...], spec)
    for block in range(MX // WB):
        start = 32 * (WB * block // 16) + WB * block % 16
        both = jnp.concatenate([spec[start:start + WB], spec[start + 16:start + 16 + WB]], 0)
        high, low = split(both.reshape(2 * WB * JL, C))
        wide[block % 2] = dot(jnp.concatenate([high, low], 1), spread)
        w_ref = early_ref if block < MX // WB // 2 else late_ref
        if block >= MX // WB // 2:
            copies[block - MX // WB // 2].wait()
        for local in range(WB):
            total_real, total_imag = None, None
            for tile in range(8):
                lanes = slice(128 * tile, 128 * tile + 128)
                real = wide[block % 2, JL * local:JL * local + JL, lanes]
                imag = wide[block % 2, JL * (WB + local):JL * (WB + local) + JL, lanes]
                m = (WB * block + local) % (MX // 2)
                w_real = w_ref[m, :, lanes]
                w_imag = w_ref[m, :, 1024 + 128 * tile:1024 + 128 * tile + 128]
                out_real = w_real * real + w_imag * imag
                out_imag = w_real * imag - w_imag * real
                total_real = out_real if tile == 0 else total_real + out_real
                total_imag = out_imag if tile == 0 else total_imag + out_imag
            for total, place in ((total_real, start + local), (total_imag, start + 16 + local)):
                total = total + pltpu.roll(total, 64, 1)
                dual[place] = total + pltpu.roll(total, 32, 1)


def lines_kernel(dual, part_ref, other_ref, back_ref, got_ref, send_hbm, send, sems):
    skip = part_ref[...] + other_ref[...]
    for dest in range(SPACE):
        send[dest, 16:] = skip
    rows = pl.ds(16, 8)
    copies = [whole_copy(send.at[:, rows], send_hbm.at[:, rows], sems.at[2])]
    reorder = reorder_matrix()
    lanes = lax.broadcasted_iota(jnp.int32, (2 * MX, 128), 1) // C
    blocks = []
    for j4 in range(4):
        block = dual[:, 4 * j4, :]
        for k in range(1, 4):
            block = jnp.where(lanes == k, dual[:, 4 * j4 + k, :], block)
        blocks.append(block)
    both = jnp.concatenate(split(jnp.concatenate(blocks, 1)), 0)
    ordered = lax.dot_general(both, reorder, ACROSS, preferred_element_type=F32)
    high, low = split(ordered[:2 * MX] + ordered[2 * MX:])
    out = dot(back_ref[...], jnp.concatenate([high, low, high], 0))
    for half in range(2):
        for q in (2 * half, 2 * half + 1):
            for r in range(4):
                send[:, 4 * q + r, :] = out[SPACE * r:SPACE * r + SPACE, 128 * q:128 * q + 128]
        rows = pl.ds(8 * half, 8)
        copies.append(whole_copy(send.at[:, rows], send_hbm.at[:, rows], sems.at[half]))
    for copy in copies:
        copy.wait()


def dual_rows(spectrum, early, weights):
    return pl.pallas_call(
        dual_kernel,
        in_specs=in_vmem(2) + [any_spec()],
        out_specs=vmem_spec(),
        out_shape=jax.ShapeDtypeStruct((2 * MX, JL, 128), F32),
        scratch_shapes=[
            pltpu.VMEM((MX // 2, JL, 2 * C * C), F32), pltpu.VMEM((2 * MX, JL, C), F32),
            pltpu.VMEM((2, 2 * WB * JL, C * C), F32),
            pltpu.SemaphoreType.DMA((MX // WB // 2,)),
        ],
        compiler_params=pltpu.CompilerParams(vmem_limit_bytes=LIMIT),
        name="dual_rows",
    )(spectrum, kept(early), in_hbm(weights))


def dual_lines(dual, part, other, got):
    return pl.pallas_call(
        lines_kernel,
        in_specs=in_vmem(4) + [any_spec()],
        out_specs=any_spec(),
        out_shape=pltpu.HBM((SPACE, SECOND, 128), F32),
        scratch_shapes=[pltpu.VMEM((SPACE, SECOND, 128), F32), pltpu.SemaphoreType.DMA((3,))],
        compiler_params=pltpu.CompilerParams(vmem_limit_bytes=LIMIT),
        name="dual_lines",
    )(dual, part, other, back_x_tables(), got)


MB = 4


def weight_kernel(
    mine_ref, got_ref, out_hbm, grads, fields, wide, out, sems,
):
    spread = spread_matrix()
    to_rows(mine_ref[:MX], grads.at[0])
    to_rows(got_ref[:MX], grads.at[1])
    for b, value in enumerate((mine_ref[MX:], got_ref[MX:])):
        for j in range(JL):
            piece = value[:, C * j:C * j + C]
            fields[b, :, j, :] = jnp.concatenate([piece] * 4, 1)
    copies = []
    for block in range(16 // MB):
        rows = jnp.concatenate(
            [grads[b, 16 * s + MB * block:16 * s + MB * block + MB] for b in range(2) for s in range(2)], 0
        )
        high, low = split(rows.reshape(4 * MB * JL, C))
        wide[...] = dot(jnp.concatenate([high, low], 1), spread)
        for local in range(MB):
            m = MB * block + local
            f = [fields[b, m + 16 * s] for b in range(2) for s in range(2)]
            for tile in range(8):
                lanes = slice(128 * tile, 128 * tile + 128)
                g = [wide[JL * (MB * q + local):JL * (MB * q + local) + JL, lanes] for q in range(4)]
                out[m, :, lanes] = g[0] * f[0] + g[1] * f[1] + g[2] * f[2] + g[3] * f[3]
                out[m, :, 1024 + 128 * tile:1024 + 128 * tile + 128] = (
                    g[1] * f[0] - g[0] * f[1] + g[3] * f[2] - g[2] * f[3]
                )
        rows = pl.ds(MB * block, MB)
        copy = pltpu.make_async_copy(out.at[rows], out_hbm.at[rows], sems.at[block])
        copy.start()
        copies.append(copy)
    for copy in copies:
        copy.wait()


def weight_gradient(mine, got):
    return pl.pallas_call(
        weight_kernel,
        in_specs=in_vmem(2),
        out_specs=any_spec(),
        out_shape=pltpu.HBM((16, JL, 2 * C * C), F32),
        scratch_shapes=[
            pltpu.VMEM((2, MX, JL, C), F32), pltpu.VMEM((2, MX, JL, 128), F32),
            pltpu.VMEM((4 * MB * JL, C * C), F32), pltpu.VMEM((16, JL, 2 * C * C), F32),
            pltpu.SemaphoreType.DMA((16 // MB,)),
        ],
        compiler_params=pltpu.CompilerParams(vmem_limit_bytes=LIMIT),
        name="weight_gradient",
    )(mine, got)


GB = 4


def backward_kernel(
    recv_ref, near, term_hbm, ytab_ref, ztab_hbm, out_hbm, skip_ref, term, ztab, out, half, lhs, sems, out_sems,
):
    ztab_copy = whole_copy(ztab_hbm, ztab, sems.at[0])
    term_copy = whole_copy(term_hbm, term, sems.at[1])
    for jq in range(4):
        for group_set in range(2):
            rows = [recv_ref[pl.ds(jq * SECOND + 8 * group_set + r, MZ, stride=4 * SECOND), :] for r in range(8)]
            turned = jnp.concatenate(rows, 0).T
            half[8 * group_set:8 * group_set + 8, JL * jq:JL * jq + JL, :] = turned.reshape(8, JL, 128)
    total = recv_ref[16:24, :]
    for source in range(1, SPACE):
        total = total + recv_ref[SECOND * source + 16:SECOND * source + 24, :]
    for q in range(4):
        skip_ref[8 * q:8 * q + 8, :] = total[:, C * q:C * q + C]
    outs = []
    for block in range(GROUPS // GB):
        for pair in range(GB // 2):
            both = []
            for member in range(2):
                value = half[GB * block + 2 * pair + member]
                both.append(jnp.concatenate([value, lane_swap(value, -1.0)], 0))
            high, low = split(jnp.concatenate(both, 1))
            lines = dot(ytab_ref[...], jnp.concatenate([high, low, high], 0))
            for member in range(2):
                high, low = split(lines[:, 128 * member:128 * member + 128])
                rows = slice(128 * (2 * pair + member), 128 * (2 * pair + member) + 128)
                lhs[rows, :128] = high
                lhs[rows, 128:256] = low
                lhs[rows, 256:] = high
        if block == 0:
            ztab_copy.wait()
        value = dot(lhs[...], ztab[...])
        if 2 * block == GROUPS // GB:
            term_copy.wait()
        for group in range(GB):
            for inner in range(2):
                for plane in range(2):
                    lane = 128 * (2 * inner + plane)
                    place = 2 * (GB * block + group) + inner
                    extra = near[place, plane] if place < C // 2 else term[place - C // 2, plane]
                    out[place, plane] = value[128 * group:128 * group + 128, lane:lane + 128] + extra
        rows = pl.ds(2 * GB * block, 2 * GB)
        copy = pltpu.make_async_copy(out.at[rows], out_hbm.at[0, rows], out_sems.at[block])
        copy.start()
        outs.append(copy)
    for copy in outs:
        copy.wait()


def backward(received, near, term):
    ztab = jnp.asarray(back_z_tables())
    return pl.pallas_call(
        backward_kernel,
        in_specs=in_vmem(2) + [any_spec(), vmem_spec(), any_spec()],
        out_specs=[any_spec(), vmem_spec()],
        out_shape=[pltpu.HBM((1, C, 2, N, N), F32), jax.ShapeDtypeStruct((C, C), F32)],
        scratch_shapes=[
            pltpu.VMEM(HALF, F32), pltpu.VMEM(ztab.shape, BF16), pltpu.VMEM(FIELD, F32),
            pltpu.VMEM((GROUPS, MY, 128), F32), pltpu.VMEM((GB * 128, 384), BF16),
            pltpu.SemaphoreType.DMA((2,)), pltpu.SemaphoreType.DMA((GROUPS // GB,)),
        ],
        compiler_params=pltpu.CompilerParams(vmem_limit_bytes=LIMIT),
        name="backward",
    )(received, kept(near), in_hbm(term), back_y_tables(), in_hbm(ztab))


def exchange(sent, rows):
    swapped = lax.all_to_all(sent, "space", 0, 0, tiled=True)
    return swapped.reshape(SPACE * rows, 128)


def body(inputs, preact, cotangent, spectral_weight, skip_weight):
    dp = lax.axis_index("dp").astype(jnp.int32).reshape(1)
    pair = [(0, 1), (1, 0)]
    received = exchange(forward(preact, cotangent, inputs), FIRST)
    near, term, part = skip_products(preact, cotangent, inputs, skip_weight)
    other = lax.ppermute(part, "dp", pair)
    spectrum, mine, theirs, early = spectra(dp, received, other, spectral_weight)
    got = lax.ppermute(theirs, "dp", pair)
    dual = dual_rows(spectrum, early, spectral_weight)
    got_dual = exchange(dual_lines(dual, part, other, got), SECOND)
    weight_grad = weight_gradient(mine, got)
    input_grad, skip_grad = backward(got_dual, near, term)
    return input_grad, weight_grad, skip_grad


def solution(mesh):
    in_specs = (
        P("dp", None, "space", None, None),
        P("dp", None, "space", None, None),
        P("dp", None, "space", None, None),
        P(None, "space", None),
        P(),
    )
    out_specs = (P("dp", None, "space", None, None), P("dp", "space", None), P())
    return jax.shard_map(body, mesh=mesh, in_specs=in_specs, out_specs=out_specs, check_vma=False)
```

```python
import functools

import jax
import jax.numpy as jnp
import numpy as np
from jax import lax
from jax.experimental import pallas as pl
from jax.experimental.pallas import tpu as pltpu
from jax.sharding import PartitionSpec as P

N = 128
C = 32
MX = 32
MY = 64
MZ = 16
SPACE = 64
GROUPS = C // 2
JL = 16
NORM = float(N) ** (-1.5)
TANH_SCALE = 0.7978845608028654
CUBIC = 0.044715
F32 = jnp.float32
BF16 = jnp.bfloat16
LIMIT = 40 * 1024 * 1024


def signed(count):
    index = np.arange(count)
    return np.where(index < count // 2, index, index - count)


def angles(frequency):
    points = np.arange(N)
    return 2.0 * np.pi / N * np.mod(frequency[:, None] * points[None, :], N)


ANGLE_X = angles(signed(MX))
ANGLE_Y = angles(signed(MY))
ANGLE_Z = angles(np.arange(MZ))


def halves(table):
    table = np.asarray(table, np.float64)
    high = table.astype(np.float32).astype(BF16)
    low = (table - high.astype(np.float64)).astype(np.float32).astype(BF16)
    return high, low


def split(value):
    high = value.astype(BF16)
    return high, (value - high.astype(F32)).astype(BF16)


def dot(left, right):
    return jnp.dot(left, right, preferred_element_type=F32)


def z_tables():
    high, low = halves(np.concatenate([np.cos(ANGLE_Z).T, -np.sin(ANGLE_Z).T], 1))
    table = np.zeros((4, 2, N, 2, 4, 2 * MZ), BF16)
    for plane in range(4):
        table[plane, 0, :, 0, plane] = high
        table[plane, 1, :, 0, plane] = high
        table[plane, 0, :, 1, plane] = low
    return table.reshape(8 * N, 256)


def y_tables():
    high, low = halves(np.concatenate([np.cos(ANGLE_Y), -np.sin(ANGLE_Y)], 0))
    return np.concatenate([high, high, low], 1)


def x_tables():
    cos_x, sin_x = np.cos(ANGLE_X), np.sin(ANGLE_X)
    table = np.zeros((2, MX, 2, N))
    table[0, :, 0], table[0, :, 1] = cos_x, sin_x
    table[1, :, 0], table[1, :, 1] = -sin_x, cos_x
    table = table.reshape(2, 2, MX // 2, 2, SPACE, 2).transpose(1, 0, 2, 5, 3, 4) * NORM
    high, low = halves(table.reshape(2 * MX, 4 * SPACE))
    return np.concatenate([high, low], 0)


def back_x_tables():
    cos_x, sin_x = np.cos(ANGLE_X), np.sin(ANGLE_X)
    table = np.zeros((2, MX, 2, N))
    table[0, :, 0], table[0, :, 1] = cos_x, sin_x
    table[1, :, 0], table[1, :, 1] = -sin_x, cos_x
    table = table.reshape(2, 2, MX // 2, 2, SPACE, 2).transpose(5, 3, 4, 1, 0, 2) * NORM
    high, low = halves(table.reshape(4 * SPACE, 2 * MX))
    return np.concatenate([high, high, low], 1)


def back_y_tables():
    high, low = halves(np.concatenate([np.cos(ANGLE_Y).T, np.sin(ANGLE_Y).T], 1))
    return np.concatenate([high, high, low], 1)


def back_z_tables():
    high, low = halves(np.concatenate([np.cos(ANGLE_Z), -np.sin(ANGLE_Z)], 0))
    table = np.zeros((3, 4, 2 * MZ, 4, N), BF16)
    for plane in range(4):
        table[0, plane, :, plane] = high
        table[1, plane, :, plane] = high
        table[2, plane, :, plane] = low
    return table.reshape(3 * 128, 4 * N)


def one_hot(hits):
    return jnp.where(hits, 1.0, 0.0).astype(BF16)


def reorder_matrix():
    row = lax.broadcasted_iota(jnp.int32, (C * JL, C * JL), 0)
    column = lax.broadcasted_iota(jnp.int32, (C * JL, C * JL), 1)
    sent, j = row >> 4, row & (JL - 1)
    channel = ((sent >> 4) * 8 + (sent & 7)) * 2 + ((sent >> 3) & 1)
    return one_hot(column == j * C + channel)


def spread_matrix():
    row = lax.broadcasted_iota(jnp.int32, (2 * C, C * C), 0)
    column = lax.broadcasted_iota(jnp.int32, (2 * C, C * C), 1)
    return one_hot((row & (C - 1)) == (column >> 5))


def rows_table():
    return np.repeat(np.eye(C), 8, 0).astype(BF16)


def fold_table():
    table = np.zeros((2, GROUPS, 8, C), BF16)
    for inner in range(2):
        for group in range(GROUPS):
            table[inner, group, :, 2 * group + inner] = 1
    return table.reshape(256, C)


def gelu_slope(h):
    square = h * h
    t = jnp.tanh(h * (TANH_SCALE + (TANH_SCALE * CUBIC) * square))
    inner = h * (0.5 * TANH_SCALE + (1.5 * TANH_SCALE * CUBIC) * square)
    return (0.5 + 0.5 * t) + (1.0 - t * t) * inner


def lane_swap(value, first_sign):
    lanes = lax.broadcasted_iota(jnp.int32, value.shape, value.ndim - 1)
    up = pltpu.roll(value, 128 - MZ, value.ndim - 1)
    down = pltpu.roll(value, MZ, value.ndim - 1)
    return jnp.where((lanes & MZ) == 0, first_sign * up, -first_sign * down)


YB = 32
CHUNKS = N // YB
TILES = YB // 8


def chunk_copy(ref, buffer, sem, chunk):
    rows = pl.ds(YB * chunk, YB)
    copy = pltpu.make_async_copy(ref.at[0, :, :, rows, :], buffer.at[:, :, rows, :], sem)
    copy.start()
    return copy


def whole_copy(ref, buffer, sem):
    copy = pltpu.make_async_copy(ref, buffer, sem)
    copy.start()
    return copy


def spread_lines(value, lhs, tile):
    value = value.reshape(GROUPS, 2, 2, 8, N)
    rows = slice(128 * tile, 128 * tile + 128)
    for inner in range(2):
        for plane in range(2):
            high, low = split(value[:, inner, plane].reshape(GROUPS * 8, N))
            lane = 256 * (2 * inner + plane)
            lhs[rows, lane:lane + 128] = high
            lhs[rows, lane + 128:lane + 256] = low


def transform_z(lhs, ztab_ref, scratch, chunk):
    out = dot(lhs[128 * TILES * chunk:128 * TILES * (chunk + 1), :], ztab_ref[...])
    out = out[:, :128] + out[:, 128:]
    for tile in range(TILES):
        place = YB * chunk + 8 * tile
        scratch[:, place:place + 8, :] = out[128 * tile:128 * tile + 128].reshape(GROUPS, 8, 128)


def transform_y(scratch, ytab_ref, half):
    for pair in range(GROUPS // 2):
        wide = jnp.concatenate([scratch[2 * pair], scratch[2 * pair + 1]], 1)
        high, low = split(wide)
        out = dot(ytab_ref[...], jnp.concatenate([high, low, high], 0))
        for member in range(2):
            mine = out[:, 128 * member:128 * member + 128]
            half[2 * pair + member] = mine[:MY] + lane_swap(mine[MY:], -1.0)


def lay_out(half, send_ref, offset, group_set):
    for jq in range(4):
        block = half[8 * group_set:8 * group_set + 8, JL * jq:JL * jq + JL, :]
        turned = block.reshape(128, 128).T
        for r in range(8):
            row = offset + 8 * group_set + r
            send_ref[pl.ds(jq, MZ, stride=4), row, :] = turned[MZ * r:MZ * r + MZ]


def finish(ytab, lines, half, send, send_hbm, out_sems):
    transform_y(lines, ytab, half)
    copies = []
    for group_set in range(2):
        lay_out(half, send, 0, group_set)
        rows = pl.ds(8 * group_set, 8)
        copies.append(whole_copy(send.at[:, rows], send_hbm.at[:, rows], out_sems.at[group_set]))
    return copies


def line_rows(chunk):
    return pl.ds(128 * TILES * chunk, 128 * TILES)


def gradient_kernel(
    pre_hbm, cot_hbm, ztab_hbm, ytab_hbm, send_hbm, lhs_hbm,
    pre, cot, ztab, ytab, lhs, lines, half, send, sems, tab_sems, out_sems, lhs_sems,
):
    copies = [
        [chunk_copy(ref, buffer, sems.at[chunk, k], chunk) for k, ref, buffer in ((0, pre_hbm, pre), (1, cot_hbm, cot))]
        for chunk in range(CHUNKS)
    ]
    tables = [whole_copy(ztab_hbm, ztab, tab_sems.at[0]), whole_copy(ytab_hbm, ytab, tab_sems.at[1])]
    outs = []
    for chunk in range(CHUNKS):
        for copy in copies[chunk]:
            copy.wait()
        for tile in range(TILES * chunk, TILES * chunk + TILES):
            rows = slice(8 * tile, 8 * tile + 8)
            spread_lines(cot[:, :, rows, :] * gelu_slope(pre[:, :, rows, :]), lhs, tile)
        rows = line_rows(chunk)
        outs.append(whole_copy(lhs.at[rows], lhs_hbm.at[rows], lhs_sems.at[chunk]))
    for table in tables:
        table.wait()
    for chunk in range(CHUNKS):
        transform_z(lhs, ztab, lines, chunk)
    outs += finish(ytab, lines, half, send, send_hbm, out_sems)
    for copy in outs:
        copy.wait()


def in_vmem(count):
    return [pl.BlockSpec(memory_space=pltpu.VMEM) for _ in range(count)]


def vmem_spec():
    return pl.BlockSpec(memory_space=pltpu.VMEM)


def any_spec():
    return pl.BlockSpec(memory_space=pl.ANY)


FIELD = (C, 2, N, N)


PAIR = (N // 8, 256, 256)


def in_hbm(value):
    return pltpu.with_memory_space_constraint(value, pltpu.HBM)


def kept(value):
    return pltpu.with_memory_space_constraint(value, pltpu.VMEM)


LINES = (2048, 1024)


def gradient_spectrum(preact, cotangent):
    ztab, ytab = jnp.asarray(z_tables()), jnp.asarray(y_tables())
    return pl.pallas_call(
        gradient_kernel,
        in_specs=[any_spec()] * 4,
        out_specs=[any_spec()] * 2,
        out_shape=[pltpu.HBM((SPACE, FIRST, 128), F32), pltpu.HBM(LINES, BF16)],
        scratch_shapes=[pltpu.VMEM(FIELD, F32)] * 2 + [
            pltpu.VMEM(ztab.shape, BF16), pltpu.VMEM(ytab.shape, BF16), pltpu.VMEM(LINES, BF16),
            pltpu.VMEM((GROUPS, N, 128), F32), pltpu.VMEM((GROUPS, MY, 128), F32), pltpu.VMEM((SPACE, FIRST, 128), F32),
            pltpu.SemaphoreType.DMA((CHUNKS, 2)), pltpu.SemaphoreType.DMA((2,)), pltpu.SemaphoreType.DMA((2,)),
            pltpu.SemaphoreType.DMA((CHUNKS,)),
        ],
        compiler_params=pltpu.CompilerParams(vmem_limit_bytes=LIMIT),
        name="gradient_spectrum",
    )(in_hbm(preact), in_hbm(cotangent), in_hbm(ztab), in_hbm(ytab))


ACROSS = (((1,), (1,)), ((), ()))


def same_row():
    left = lax.broadcasted_iota(jnp.int32, (256, 256), 0) & 7
    right = lax.broadcasted_iota(jnp.int32, (256, 256), 1) & 7
    return left == right


def tile_parts(lines, tile):
    rows = slice(128 * tile, 128 * tile + 128)
    return [
        jnp.concatenate([
            jnp.concatenate([
                lines[rows, 512 * inner + 256 * plane + part:512 * inner + 256 * plane + part + 128] for plane in range(2)
            ], 1) for inner in range(2)
        ], 0) for part in (0, 128)
    ]


def input_kernel(
    one_ref, lhs_hbm, inp_hbm, ztab_hbm, ytab_hbm, fold_ref, send_hbm,
    g_lines, inp, ztab, ytab, lhs, acc, lines, half, send, sems, tab_sems, out_sems,
):
    always = one_ref[0] >= 0
    copies = []
    for chunk in range(CHUNKS):
        rows = line_rows(chunk)
        copies.append([
            chunk_copy(inp_hbm, inp, sems.at[chunk, 0], chunk),
            whole_copy(lhs_hbm.at[rows], g_lines.at[rows], sems.at[chunk, 1]),
        ])
    tables = [whole_copy(ztab_hbm, ztab, tab_sems.at[0]), whole_copy(ytab_hbm, ytab, tab_sems.at[1])]
    for chunk in range(CHUNKS):
        for copy in copies[chunk]:
            copy.wait()

        @pl.when(always)
        def _():
            for tile in range(TILES * chunk, TILES * chunk + TILES):
                spread_lines(inp[:, :, 8 * tile:8 * tile + 8, :], lhs, tile)

        if chunk == 0:
            tables[0].wait()

        @pl.when(always)
        def _():
            transform_z(lhs, ztab, lines, chunk)

        @pl.when(always)
        def _():
            for tile in range(TILES * chunk, TILES * chunk + TILES):
                g_high, g_low = tile_parts(g_lines, tile)
                i_high, i_low = tile_parts(lhs, tile)
                total = (
                    lax.dot_general(g_high, i_high, ACROSS, preferred_element_type=F32)
                    + lax.dot_general(g_low, i_high, ACROSS, preferred_element_type=F32)
                    + lax.dot_general(g_high, i_low, ACROSS, preferred_element_type=F32)
                )
                if tile == 0:
                    acc[...] = total
                else:
                    acc[...] += total

    diagonal = jnp.where(same_row(), acc[...], 0.0) * NORM
    fold = fold_ref[...].astype(F32)
    folded = jnp.dot(diagonal, fold, preferred_element_type=F32, precision=lax.Precision.HIGHEST)
    summed = lax.dot_general(
        fold, folded, (((0,), (0,)), ((), ())), preferred_element_type=F32,
        precision=lax.Precision.HIGHEST,
    )
    part = jnp.concatenate([summed[8 * q:8 * q + 8, :] for q in range(4)], 1)
    for dest in range(SPACE):
        send[dest, 16:] = part
    rows = pl.ds(16, 8)
    outs = [whole_copy(send.at[:, rows], send_hbm.at[:, rows], out_sems.at[2])]
    tables[1].wait()
    outs += finish(ytab, lines, half, send, send_hbm, out_sems)
    for copy in outs:
        copy.wait()


def input_spectrum(one, lines, inputs):
    ztab, ytab = jnp.asarray(z_tables()), jnp.asarray(y_tables())
    return pl.pallas_call(
        input_kernel,
        in_specs=[pl.BlockSpec(memory_space=pltpu.SMEM)] + [any_spec()] * 4 + [vmem_spec()],
        out_specs=any_spec(),
        out_shape=pltpu.HBM((SPACE, 24, 128), F32),
        scratch_shapes=[
            pltpu.VMEM(LINES, BF16), pltpu.VMEM(FIELD, F32),
            pltpu.VMEM(ztab.shape, BF16), pltpu.VMEM(ytab.shape, BF16), pltpu.VMEM(LINES, BF16),
            pltpu.VMEM((256, 256), F32),
            pltpu.VMEM((GROUPS, N, 128), F32), pltpu.VMEM((GROUPS, MY, 128), F32), pltpu.VMEM((SPACE, 24, 128), F32),
            pltpu.SemaphoreType.DMA((CHUNKS, 2)), pltpu.SemaphoreType.DMA((2,)), pltpu.SemaphoreType.DMA((3,)),
        ],
        compiler_params=pltpu.CompilerParams(vmem_limit_bytes=LIMIT),
        name="input_spectrum",
    )(one, in_hbm(lines), in_hbm(inputs), in_hbm(ztab), in_hbm(ytab), fold_table())


def skip_kernel(lhs_hbm, after_hbm, skip_ref, rows_ref, fold_ref, term_hbm, g_lines, term, sems, out_sems):
    copies = []
    for chunk in range(CHUNKS):
        rows = line_rows(chunk)
        copies.append(whole_copy(lhs_hbm.at[rows], g_lines.at[rows], sems.at[chunk]))
    matrix = []
    for part in split(skip_ref[...]):
        wide = lax.dot_general(rows_ref[...], part, ACROSS, preferred_element_type=F32).astype(BF16)
        wide = lax.dot_general(wide, fold_ref[...], ACROSS, preferred_element_type=F32)
        matrix.append(jnp.where(same_row(), wide, 0.0).astype(BF16))
    matrix = jnp.concatenate(matrix, 0)
    outs = []
    for chunk in range(CHUNKS):
        copies[chunk].wait()
        for tile in range(TILES * chunk, TILES * chunk + TILES):
            rows = slice(8 * tile, 8 * tile + 8)
            g_high, g_low = tile_parts(g_lines, tile)
            out = dot(matrix, g_high)
            out = out[:256] + out[256:] + dot(matrix[:256], g_low)
            for plane in range(2):
                value = out[:, 128 * plane:128 * plane + 128].reshape(C, 8, N)
                term[:, plane, rows, :] = value
        rows = pl.ds(YB * chunk, YB)
        outs.append(whole_copy(term.at[:, :, rows, :], term_hbm.at[:, :, rows, :], out_sems.at[chunk]))
    for copy in outs:
        copy.wait()


def skip_term(lines, after, skip_weight):
    return pl.pallas_call(
        skip_kernel,
        in_specs=[any_spec()] * 2 + in_vmem(3),
        out_specs=any_spec(),
        out_shape=pltpu.HBM(FIELD, F32),
        scratch_shapes=[
            pltpu.VMEM(LINES, BF16), pltpu.VMEM(FIELD, F32),
            pltpu.SemaphoreType.DMA((CHUNKS,)), pltpu.SemaphoreType.DMA((CHUNKS,)),
        ],
        compiler_params=pltpu.CompilerParams(vmem_limit_bytes=LIMIT),
        name="skip_term",
    )(in_hbm(lines), after, skip_weight, rows_table(), fold_table())


FIRST = 16
SECOND = 40


def transform_x(recv_ref, rows_each, offset, xtab_ref, reorder):
    blocks = []
    for q in range(4):
        column = [recv_ref[pl.ds(offset + 4 * q + r, SPACE, stride=rows_each), :] for r in range(4)]
        blocks.append(jnp.concatenate(column, 0))
    high, low = split(jnp.concatenate(blocks, 1))
    out = dot(xtab_ref[...], high)
    spectrum = out[:2 * MX] + out[2 * MX:] + dot(xtab_ref[:2 * MX], low)
    out = dot(jnp.concatenate(split(spectrum), 0), reorder)
    return out[:2 * MX] + out[2 * MX:]


def to_rows(spectrum, scratch):
    for j in range(JL):
        scratch[:, j, :] = spectrum[:, C * j:C * j + C]


WB = 8


def middle_kernel(
    dp_ref, recv_ref, xtab_ref, back_ref, w_hbm, input_hbm, send_hbm, mine_ref, theirs_ref,
    w_ref, spec, wide, dual, send, sems, out_sems,
):
    copies = []
    for block in range(MX // WB):
        rows = pl.ds(WB * block, WB)
        copies.append(whole_copy(w_hbm.at[rows], w_ref.at[rows], sems.at[block]))
    onward = pl.ds(16, 24)
    arriving = whole_copy(input_hbm, send.at[:, onward], out_sems.at[3])
    reorder = reorder_matrix()
    spread = spread_matrix()
    first = dp_ref[0] == 0
    spectrum = transform_x(recv_ref, FIRST, 0, xtab_ref, reorder)
    mine_ref[...] = jnp.where(first, spectrum[:MX], spectrum[MX:])
    theirs_ref[...] = jnp.where(first, spectrum[MX:], spectrum[:MX])
    to_rows(spectrum, spec)

    for block in range(MX // WB):
        start = 32 * (WB * block // 16) + WB * block % 16
        both = jnp.concatenate([spec[start:start + WB], spec[start + 16:start + 16 + WB]], 0)
        high, low = split(both.reshape(2 * WB * JL, C))
        wide[block % 2] = dot(jnp.concatenate([high, low], 1), spread)
        copies[block].wait()
        for local in range(WB):
            total_real, total_imag = None, None
            for tile in range(8):
                lanes = slice(128 * tile, 128 * tile + 128)
                real = wide[block % 2, JL * local:JL * local + JL, lanes]
                imag = wide[block % 2, JL * (WB + local):JL * (WB + local) + JL, lanes]
                m = WB * block + local
                w_real = w_ref[m, :, lanes]
                w_imag = w_ref[m, :, 1024 + 128 * tile:1024 + 128 * tile + 128]
                out_real = w_real * real + w_imag * imag
                out_imag = w_real * imag - w_imag * real
                total_real = out_real if tile == 0 else total_real + out_real
                total_imag = out_imag if tile == 0 else total_imag + out_imag
            for total, place in ((total_real, start + local), (total_imag, start + 16 + local)):
                total = total + pltpu.roll(total, 64, 1)
                dual[place] = total + pltpu.roll(total, 32, 1)

    arriving.wait()
    copies = [whole_copy(send.at[:, onward], send_hbm.at[:, onward], out_sems.at[2])]
    lanes = lax.broadcasted_iota(jnp.int32, (2 * MX, 128), 1) // C
    blocks = []
    for j4 in range(4):
        block = dual[:, 4 * j4, :]
        for k in range(1, 4):
            block = jnp.where(lanes == k, dual[:, 4 * j4 + k, :], block)
        blocks.append(block)
    both = jnp.concatenate(split(jnp.concatenate(blocks, 1)), 0)
    ordered = lax.dot_general(both, reorder, ACROSS, preferred_element_type=F32)
    high, low = split(ordered[:2 * MX] + ordered[2 * MX:])
    out = dot(back_ref[...], jnp.concatenate([high, low, high], 0))
    for half in range(2):
        for q in (2 * half, 2 * half + 1):
            for r in range(4):
                send[:, 4 * q + r, :] = out[SPACE * r:SPACE * r + SPACE, 128 * q:128 * q + 128]
        rows = pl.ds(8 * half, 8)
        copies.append(whole_copy(send.at[:, rows], send_hbm.at[:, rows], sems.at[half]))
    for copy in copies:
        copy.wait()


def middle(dp, received, weights, input_rows):
    return pl.pallas_call(
        middle_kernel,
        in_specs=[pl.BlockSpec(memory_space=pltpu.SMEM)] + in_vmem(3) + [any_spec()] * 2,
        out_specs=[any_spec()] + in_vmem(2),
        out_shape=[
            pltpu.HBM((SPACE, SECOND, 128), F32),
            jax.ShapeDtypeStruct((MX, JL * C), F32),
            jax.ShapeDtypeStruct((MX, JL * C), F32),
        ],
        scratch_shapes=[
            pltpu.VMEM((MX, JL, 2 * C * C), F32), pltpu.VMEM((2 * MX, JL, C), F32),
            pltpu.VMEM((2, 2 * WB * JL, C * C), F32), pltpu.VMEM((2 * MX, JL, 128), F32),
            pltpu.VMEM((SPACE, SECOND, 128), F32),
            pltpu.SemaphoreType.DMA((MX // WB,)), pltpu.SemaphoreType.DMA((4,)),
        ],
        compiler_params=pltpu.CompilerParams(vmem_limit_bytes=LIMIT),
        name="middle",
    )(dp, received, x_tables(), back_x_tables(), in_hbm(weights), in_hbm(input_rows))


def inputs_kernel(dp_ref, recv_ref, theirs_ref, xtab_ref, after_hbm, mine_ref, out_ref):
    spectrum = transform_x(recv_ref, SECOND, 16, xtab_ref, reorder_matrix())
    first = dp_ref[0] == 0
    mine_ref[...] = jnp.where(first, spectrum[:MX], spectrum[MX:])
    out_ref[:MX, :] = theirs_ref[...]
    out_ref[MX:2 * MX, :] = jnp.where(first, spectrum[MX:], spectrum[:MX])
    total = recv_ref[32:40, :]
    for source in range(1, SPACE):
        total = total + recv_ref[SECOND * source + 32:SECOND * source + 40, :]
    out_ref[2 * MX:, :] = jnp.concatenate([total] * 4, 1)


def inputs_spectrum(dp, received, theirs, after):
    return pl.pallas_call(
        inputs_kernel,
        in_specs=[pl.BlockSpec(memory_space=pltpu.SMEM)] + in_vmem(3) + [any_spec()],
        out_specs=in_vmem(2),
        out_shape=[
            jax.ShapeDtypeStruct((MX, JL * C), F32),
            jax.ShapeDtypeStruct((2 * MX + 8, JL * C), F32),
        ],
        compiler_params=pltpu.CompilerParams(vmem_limit_bytes=LIMIT),
        name="inputs_spectrum",
    )(dp, received, theirs, x_tables(), after)


MB = 4


def weight_kernel(
    grad_ref, field_ref, sent_ref, got_ref, out_hbm, skip_ref, grads, fields, wide, out, sems,
):
    spread = spread_matrix()
    to_rows(grad_ref[...], grads.at[0])
    to_rows(got_ref[:MX], grads.at[1])
    for b, value in enumerate((field_ref[...], got_ref[MX:2 * MX])):
        for j in range(JL):
            piece = value[:, C * j:C * j + C]
            fields[b, :, j, :] = jnp.concatenate([piece] * 4, 1)
    copies = []
    for block in range(16 // MB):
        rows = jnp.concatenate(
            [grads[b, 16 * s + MB * block:16 * s + MB * block + MB] for b in range(2) for s in range(2)], 0
        )
        high, low = split(rows.reshape(4 * MB * JL, C))
        wide[...] = dot(jnp.concatenate([high, low], 1), spread)
        for local in range(MB):
            m = MB * block + local
            f = [fields[b, m + 16 * s] for b in range(2) for s in range(2)]
            for tile in range(8):
                lanes = slice(128 * tile, 128 * tile + 128)
                g = [wide[JL * (MB * q + local):JL * (MB * q + local) + JL, lanes] for q in range(4)]
                out[m, :, lanes] = g[0] * f[0] + g[1] * f[1] + g[2] * f[2] + g[3] * f[3]
                out[m, :, 1024 + 128 * tile:1024 + 128 * tile + 128] = (
                    g[1] * f[0] - g[0] * f[1] + g[3] * f[2] - g[2] * f[3]
                )
        rows = pl.ds(MB * block, MB)
        copy = pltpu.make_async_copy(out.at[rows], out_hbm.at[rows], sems.at[block])
        copy.start()
        copies.append(copy)
    total = sent_ref[2 * MX:, :128] + got_ref[2 * MX:, :128]
    for q in range(4):
        skip_ref[8 * q:8 * q + 8, :] = total[:, C * q:C * q + C]
    for copy in copies:
        copy.wait()


def weight_gradient(grad_mine, field_mine, sent, got):
    return pl.pallas_call(
        weight_kernel,
        in_specs=in_vmem(4),
        out_specs=[any_spec(), vmem_spec()],
        out_shape=[pltpu.HBM((16, JL, 2 * C * C), F32), jax.ShapeDtypeStruct((C, C), F32)],
        scratch_shapes=[
            pltpu.VMEM((2, MX, JL, C), F32), pltpu.VMEM((2, MX, JL, 128), F32),
            pltpu.VMEM((4 * MB * JL, C * C), F32), pltpu.VMEM((16, JL, 2 * C * C), F32),
            pltpu.SemaphoreType.DMA((16 // MB,)),
        ],
        compiler_params=pltpu.CompilerParams(vmem_limit_bytes=LIMIT),
        name="weight_gradient",
    )(grad_mine, field_mine, sent, got)


GB = 4


def backward_kernel(
    recv_ref, term_hbm, ytab_ref, ztab_hbm, out_hbm, term, ztab, out, half, lhs, sems, out_sems,
):
    copies = []
    for block in range(GROUPS // GB):
        rows = pl.ds(2 * GB * block, 2 * GB)
        copies.append(whole_copy(term_hbm.at[rows], term.at[rows], sems.at[block]))
        if block == 0:
            ztab_copy = whole_copy(ztab_hbm, ztab, sems.at[GROUPS // GB])
    for jq in range(4):
        for group_set in range(2):
            rows = [recv_ref[pl.ds(jq * SECOND + 8 * group_set + r, MZ, stride=4 * SECOND), :] for r in range(8)]
            turned = jnp.concatenate(rows, 0).T
            half[8 * group_set:8 * group_set + 8, JL * jq:JL * jq + JL, :] = turned.reshape(8, JL, 128)
    outs = []
    for block in range(GROUPS // GB):
        for pair in range(GB // 2):
            both = []
            for member in range(2):
                value = half[GB * block + 2 * pair + member]
                both.append(jnp.concatenate([value, lane_swap(value, -1.0)], 0))
            high, low = split(jnp.concatenate(both, 1))
            lines = dot(ytab_ref[...], jnp.concatenate([high, low, high], 0))
            for member in range(2):
                high, low = split(lines[:, 128 * member:128 * member + 128])
                rows = slice(128 * (2 * pair + member), 128 * (2 * pair + member) + 128)
                lhs[rows, :128] = high
                lhs[rows, 128:256] = low
                lhs[rows, 256:] = high
        if block == 0:
            ztab_copy.wait()
        value = dot(lhs[...], ztab[...])
        copies[block].wait()
        for group in range(GB):
            for inner in range(2):
                for plane in range(2):
                    lane = 128 * (2 * inner + plane)
                    place = 2 * (GB * block + group) + inner
                    out[place, plane] = value[128 * group:128 * group + 128, lane:lane + 128] + term[place, plane]
        rows = pl.ds(2 * GB * block, 2 * GB)
        copy = pltpu.make_async_copy(out.at[rows], out_hbm.at[0, rows], out_sems.at[block])
        copy.start()
        outs.append(copy)
    for copy in outs:
        copy.wait()


def backward(received, term):
    ztab = jnp.asarray(back_z_tables())
    return pl.pallas_call(
        backward_kernel,
        in_specs=[vmem_spec(), any_spec(), vmem_spec(), any_spec()],
        out_specs=any_spec(),
        out_shape=pltpu.HBM((1, C, 2, N, N), F32),
        scratch_shapes=[
            pltpu.VMEM(FIELD, F32), pltpu.VMEM(ztab.shape, BF16), pltpu.VMEM(FIELD, F32),
            pltpu.VMEM((GROUPS, MY, 128), F32), pltpu.VMEM((GB * 128, 384), BF16),
            pltpu.SemaphoreType.DMA((GROUPS // GB + 1,)), pltpu.SemaphoreType.DMA((GROUPS // GB,)),
        ],
        compiler_params=pltpu.CompilerParams(vmem_limit_bytes=LIMIT),
        name="backward",
    )(received, in_hbm(term), back_y_tables(), in_hbm(ztab))


def exchange(sent, rows):
    swapped = lax.all_to_all(sent, "space", 0, 0, tiled=True)
    return swapped.reshape(SPACE * rows, 128)


def body(inputs, preact, cotangent, spectral_weight, skip_weight):
    dp = lax.axis_index("dp").astype(jnp.int32).reshape(1)
    send_grad, lines = gradient_spectrum(preact, cotangent)
    got_grad = exchange(send_grad, FIRST)
    input_rows = input_spectrum(dp, lines, inputs)
    send_dual, grad_mine, grad_theirs = middle(dp, got_grad, spectral_weight, input_rows)
    got_dual = exchange(send_dual, SECOND)
    term = skip_term(lines, grad_mine, skip_weight)
    field_mine, sent = inputs_spectrum(dp, got_dual, grad_theirs, term)
    got = lax.ppermute(sent, "dp", [(0, 1), (1, 0)])
    input_grad = backward(got_dual, term)
    weight_grad, skip_grad = weight_gradient(grad_mine, field_mine, sent, got)
    return input_grad, weight_grad, skip_grad


def solution(mesh):
    in_specs = (
        P("dp", None, "space", None, None),
        P("dp", None, "space", None, None),
        P("dp", None, "space", None, None),
        P(None, "space", None),
        P(),
    )
    out_specs = (P("dp", None, "space", None, None), P("dp", "space", None), P())
    return jax.shard_map(body, mesh=mesh, in_specs=in_specs, out_specs=out_specs, check_vma=False)
```

```python
import functools

import jax
import jax.numpy as jnp
import numpy as np
from jax import lax
from jax.experimental import pallas as pl
from jax.experimental.pallas import tpu as pltpu
from jax.sharding import PartitionSpec as P

N = 128
C = 32
MX = 32
MY = 64
MZ = 16
SPACE = 64
GROUPS = C // 2
JL = 16
NORM = float(N) ** (-1.5)
TANH_SCALE = 0.7978845608028654
CUBIC = 0.044715
F32 = jnp.float32
BF16 = jnp.bfloat16
LIMIT = 40 * 1024 * 1024


def signed(count):
    index = np.arange(count)
    return np.where(index < count // 2, index, index - count)


def angles(frequency):
    points = np.arange(N)
    return 2.0 * np.pi / N * np.mod(frequency[:, None] * points[None, :], N)


ANGLE_X = angles(signed(MX))
ANGLE_Y = angles(signed(MY))
ANGLE_Z = angles(np.arange(MZ))


def halves(table):
    table = np.asarray(table, np.float64)
    high = table.astype(np.float32).astype(BF16)
    low = (table - high.astype(np.float64)).astype(np.float32).astype(BF16)
    return high, low


def split(value):
    high = value.astype(BF16)
    return high, (value - high.astype(F32)).astype(BF16)


def dot(left, right):
    return jnp.dot(left, right, preferred_element_type=F32)


def z_tables():
    high, low = halves(np.concatenate([np.cos(ANGLE_Z).T, -np.sin(ANGLE_Z).T], 1))
    table = np.zeros((4, 2, N, 2, 4, 2 * MZ), BF16)
    for plane in range(4):
        table[plane, 0, :, 0, plane] = high
        table[plane, 1, :, 0, plane] = high
        table[plane, 0, :, 1, plane] = low
    return table.reshape(8 * N, 256)


def y_tables():
    high, low = halves(np.concatenate([np.cos(ANGLE_Y), -np.sin(ANGLE_Y)], 0))
    return np.concatenate([high, high, low], 1)


def x_tables():
    cos_x, sin_x = np.cos(ANGLE_X), np.sin(ANGLE_X)
    table = np.zeros((2, MX, 2, N))
    table[0, :, 0], table[0, :, 1] = cos_x, sin_x
    table[1, :, 0], table[1, :, 1] = -sin_x, cos_x
    table = table.reshape(2, 2, MX // 2, 2, SPACE, 2).transpose(1, 0, 2, 5, 3, 4) * NORM
    high, low = halves(table.reshape(2 * MX, 4 * SPACE))
    return np.concatenate([high, low], 0)


def back_x_tables():
    cos_x, sin_x = np.cos(ANGLE_X), np.sin(ANGLE_X)
    table = np.zeros((2, MX, 2, N))
    table[0, :, 0], table[0, :, 1] = cos_x, sin_x
    table[1, :, 0], table[1, :, 1] = -sin_x, cos_x
    table = table.reshape(2, 2, MX // 2, 2, SPACE, 2).transpose(5, 3, 4, 1, 0, 2) * NORM
    high, low = halves(table.reshape(4 * SPACE, 2 * MX))
    return np.concatenate([high, high, low], 1)


def back_y_tables():
    high, low = halves(np.concatenate([np.cos(ANGLE_Y).T, np.sin(ANGLE_Y).T], 1))
    return np.concatenate([high, high, low], 1)


def back_z_tables():
    high, low = halves(np.concatenate([np.cos(ANGLE_Z), -np.sin(ANGLE_Z)], 0))
    table = np.zeros((3, 4, 2 * MZ, 4, N), BF16)
    for plane in range(4):
        table[0, plane, :, plane] = high
        table[1, plane, :, plane] = high
        table[2, plane, :, plane] = low
    return table.reshape(3 * 128, 4 * N)


def one_hot(hits):
    return jnp.where(hits, 1.0, 0.0).astype(BF16)


def reorder_matrix():
    row = lax.broadcasted_iota(jnp.int32, (C * JL, C * JL), 0)
    column = lax.broadcasted_iota(jnp.int32, (C * JL, C * JL), 1)
    sent, j = row >> 4, row & (JL - 1)
    channel = ((sent >> 4) * 8 + (sent & 7)) * 2 + ((sent >> 3) & 1)
    return one_hot(column == j * C + channel)


def spread_matrix():
    row = lax.broadcasted_iota(jnp.int32, (8 * C, C * C), 0)
    column = lax.broadcasted_iota(jnp.int32, (8 * C, C * C), 1)
    return one_hot((row & (C - 1)) == (column >> 5))


def rows_table():
    return np.repeat(np.eye(C), 8, 0).astype(BF16)


def fold_table():
    table = np.zeros((2, GROUPS, 8, C), BF16)
    for inner in range(2):
        for group in range(GROUPS):
            table[inner, group, :, 2 * group + inner] = 1
    return table.reshape(256, C)


def gelu_slope(h):
    square = h * h
    t = jnp.tanh(h * (TANH_SCALE + (TANH_SCALE * CUBIC) * square))
    inner = h * (0.5 * TANH_SCALE + (1.5 * TANH_SCALE * CUBIC) * square)
    return (0.5 + 0.5 * t) + (1.0 - t * t) * inner


def lane_swap(value, first_sign):
    lanes = lax.broadcasted_iota(jnp.int32, value.shape, value.ndim - 1)
    up = pltpu.roll(value, 128 - MZ, value.ndim - 1)
    down = pltpu.roll(value, MZ, value.ndim - 1)
    return jnp.where((lanes & MZ) == 0, first_sign * up, -first_sign * down)


YB = 32
CHUNKS = N // YB
TILES = YB // 8


def chunk_copy(ref, buffer, sem, chunk):
    rows = pl.ds(YB * chunk, YB)
    copy = pltpu.make_async_copy(ref.at[0, :, :, rows, :], buffer.at[:, :, rows, :], sem)
    copy.start()
    return copy


def whole_copy(ref, buffer, sem):
    copy = pltpu.make_async_copy(ref, buffer, sem)
    copy.start()
    return copy


def spread_lines(value, lhs, tile):
    value = value.reshape(GROUPS, 2, 2, 8, N)
    rows = slice(128 * tile, 128 * tile + 128)
    for inner in range(2):
        for plane in range(2):
            high, low = split(value[:, inner, plane].reshape(GROUPS * 8, N))
            lane = 256 * (2 * inner + plane)
            lhs[rows, lane:lane + 128] = high
            lhs[rows, lane + 128:lane + 256] = low


def transform_z(lhs, ztab_ref, scratch, chunk):
    out = dot(lhs[128 * TILES * chunk:128 * TILES * (chunk + 1), :], ztab_ref[...])
    out = out[:, :128] + out[:, 128:]
    for tile in range(TILES):
        place = YB * chunk + 8 * tile
        scratch[:, place:place + 8, :] = out[128 * tile:128 * tile + 128].reshape(GROUPS, 8, 128)


def transform_y(scratch, ytab_ref, half):
    for pair in range(GROUPS // 2):
        wide = jnp.concatenate([scratch[2 * pair], scratch[2 * pair + 1]], 1)
        high, low = split(wide)
        out = dot(ytab_ref[...], jnp.concatenate([high, low, high], 0))
        for member in range(2):
            mine = out[:, 128 * member:128 * member + 128]
            half[2 * pair + member] = mine[:MY] + lane_swap(mine[MY:], -1.0)


def blocks_of(send):
    return send.reshape(SPACE, send.shape[0] // SPACE, 128)


def lay_out(half, send_ref, group_set):
    rows_each = send_ref.shape[0] // SPACE
    for jq in range(4):
        block = half[8 * group_set:8 * group_set + 8, JL * jq:JL * jq + JL, :]
        turned = block.reshape(128, 128).T
        for r in range(8):
            row = jq * rows_each + 8 * group_set + r
            send_ref[pl.ds(row, MZ, stride=4 * rows_each), :] = turned[MZ * r:MZ * r + MZ]


def finish(ytab, lines, half, send, send_hbm, out_sems):
    transform_y(lines, ytab, half)
    copies = []
    for group_set in range(2):
        lay_out(half, send, group_set)
        rows = pl.ds(8 * group_set, 8)
        copies.append(whole_copy(blocks_of(send).at[:, rows], send_hbm.at[:, rows], out_sems.at[group_set]))
    return copies


def line_rows(chunk):
    return pl.ds(128 * TILES * chunk, 128 * TILES)


def gradient_kernel(
    pre_hbm, cot_hbm, ztab_hbm, ytab_hbm, send_hbm, lhs_hbm,
    pre, cot, ztab, ytab, lhs, lines, half, send, sems, tab_sems, out_sems, lhs_sems,
):
    copies = [
        [chunk_copy(ref, buffer, sems.at[chunk, k], chunk) for k, ref, buffer in ((0, pre_hbm, pre), (1, cot_hbm, cot))]
        for chunk in range(CHUNKS)
    ]
    tables = [whole_copy(ztab_hbm, ztab, tab_sems.at[0]), whole_copy(ytab_hbm, ytab, tab_sems.at[1])]
    outs = []
    for chunk in range(CHUNKS):
        for copy in copies[chunk]:
            copy.wait()
        for tile in range(TILES * chunk, TILES * chunk + TILES):
            rows = slice(8 * tile, 8 * tile + 8)
            spread_lines(cot[:, :, rows, :] * gelu_slope(pre[:, :, rows, :]), lhs, tile)
        rows = line_rows(chunk)
        outs.append(whole_copy(lhs.at[rows], lhs_hbm.at[rows], lhs_sems.at[chunk]))
    for table in tables:
        table.wait()
    for chunk in range(CHUNKS):
        transform_z(lhs, ztab, lines, chunk)
    outs += finish(ytab, lines, half, send, send_hbm, out_sems)
    for copy in outs:
        copy.wait()


def in_vmem(count):
    return [pl.BlockSpec(memory_space=pltpu.VMEM) for _ in range(count)]


def vmem_spec():
    return pl.BlockSpec(memory_space=pltpu.VMEM)


def any_spec():
    return pl.BlockSpec(memory_space=pl.ANY)


FIELD = (C, 2, N, N)


PAIR = (N // 8, 256, 256)


def in_hbm(value):
    return pltpu.with_memory_space_constraint(value, pltpu.HBM)


def kept(value):
    return pltpu.with_memory_space_constraint(value, pltpu.VMEM)


LINES = (2048, 1024)


def gradient_spectrum(preact, cotangent):
    ztab, ytab = jnp.asarray(z_tables()), jnp.asarray(y_tables())
    return pl.pallas_call(
        gradient_kernel,
        in_specs=[any_spec()] * 4,
        out_specs=[any_spec()] * 2,
        out_shape=[pltpu.HBM((SPACE, FIRST, 128), F32), pltpu.HBM(LINES, BF16)],
        scratch_shapes=[pltpu.VMEM(FIELD, F32)] * 2 + [
            pltpu.VMEM(ztab.shape, BF16), pltpu.VMEM(ytab.shape, BF16), pltpu.VMEM(LINES, BF16),
            pltpu.VMEM((GROUPS, N, 128), F32), pltpu.VMEM((GROUPS, MY, 128), F32), pltpu.VMEM((SPACE * FIRST, 128), F32),
            pltpu.SemaphoreType.DMA((CHUNKS, 2)), pltpu.SemaphoreType.DMA((2,)), pltpu.SemaphoreType.DMA((2,)),
            pltpu.SemaphoreType.DMA((CHUNKS,)),
        ],
        compiler_params=pltpu.CompilerParams(vmem_limit_bytes=LIMIT),
        name="gradient_spectrum",
    )(in_hbm(preact), in_hbm(cotangent), in_hbm(ztab), in_hbm(ytab))


ACROSS = (((1,), (1,)), ((), ()))


def same_row():
    left = lax.broadcasted_iota(jnp.int32, (256, 256), 0) & 7
    right = lax.broadcasted_iota(jnp.int32, (256, 256), 1) & 7
    return left == right


def tile_parts(lines, tile):
    rows = slice(128 * tile, 128 * tile + 128)
    return [
        jnp.concatenate([
            jnp.concatenate([
                lines[rows, 512 * inner + 256 * plane + part:512 * inner + 256 * plane + part + 128] for plane in range(2)
            ], 1) for inner in range(2)
        ], 0) for part in (0, 128)
    ]


def input_kernel(
    one_ref, lhs_hbm, inp_hbm, ztab_hbm, ytab_hbm, fold_ref, send_hbm,
    g_lines, inp, ztab, ytab, lhs, acc, lines, half, send, sems, tab_sems, out_sems,
):
    always = one_ref[0] >= 0
    copies = []
    for chunk in range(CHUNKS):
        rows = line_rows(chunk)
        copies.append([
            chunk_copy(inp_hbm, inp, sems.at[chunk, 0], chunk),
            whole_copy(lhs_hbm.at[rows], g_lines.at[rows], sems.at[chunk, 1]),
        ])
    tables = [whole_copy(ztab_hbm, ztab, tab_sems.at[0]), whole_copy(ytab_hbm, ytab, tab_sems.at[1])]
    for chunk in range(CHUNKS):
        for copy in copies[chunk]:
            copy.wait()

        @pl.when(always)
        def _():
            for tile in range(TILES * chunk, TILES * chunk + TILES):
                spread_lines(inp[:, :, 8 * tile:8 * tile + 8, :], lhs, tile)

        if chunk == 0:
            tables[0].wait()

        @pl.when(always)
        def _():
            transform_z(lhs, ztab, lines, chunk)

        @pl.when(always)
        def _():
            for tile in range(TILES * chunk, TILES * chunk + TILES):
                g_high, g_low = tile_parts(g_lines, tile)
                i_high, i_low = tile_parts(lhs, tile)
                total = (
                    lax.dot_general(g_high, i_high, ACROSS, preferred_element_type=F32)
                    + lax.dot_general(g_low, i_high, ACROSS, preferred_element_type=F32)
                    + lax.dot_general(g_high, i_low, ACROSS, preferred_element_type=F32)
                )
                if tile == 0:
                    acc[...] = total
                else:
                    acc[...] += total

    diagonal = jnp.where(same_row(), acc[...], 0.0) * NORM
    fold = fold_ref[...].astype(F32)
    folded = jnp.dot(diagonal, fold, preferred_element_type=F32, precision=lax.Precision.HIGHEST)
    summed = lax.dot_general(
        fold, folded, (((0,), (0,)), ((), ())), preferred_element_type=F32,
        precision=lax.Precision.HIGHEST,
    )
    part = jnp.concatenate([summed[8 * q:8 * q + 8, :] for q in range(4)], 1)
    for dest in range(SPACE):
        send[24 * dest + 16:24 * dest + 24, :] = part
    rows = pl.ds(16, 8)
    outs = [whole_copy(blocks_of(send).at[:, rows], send_hbm.at[:, rows], out_sems.at[2])]
    tables[1].wait()
    outs += finish(ytab, lines, half, send, send_hbm, out_sems)
    for copy in outs:
        copy.wait()


def input_spectrum(one, lines, inputs):
    ztab, ytab = jnp.asarray(z_tables()), jnp.asarray(y_tables())
    return pl.pallas_call(
        input_kernel,
        in_specs=[pl.BlockSpec(memory_space=pltpu.SMEM)] + [any_spec()] * 4 + [vmem_spec()],
        out_specs=any_spec(),
        out_shape=pltpu.HBM((SPACE, 24, 128), F32),
        scratch_shapes=[
            pltpu.VMEM(LINES, BF16), pltpu.VMEM(FIELD, F32),
            pltpu.VMEM(ztab.shape, BF16), pltpu.VMEM(ytab.shape, BF16), pltpu.VMEM(LINES, BF16),
            pltpu.VMEM((256, 256), F32),
            pltpu.VMEM((GROUPS, N, 128), F32), pltpu.VMEM((GROUPS, MY, 128), F32), pltpu.VMEM((SPACE * 24, 128), F32),
            pltpu.SemaphoreType.DMA((CHUNKS, 2)), pltpu.SemaphoreType.DMA((2,)), pltpu.SemaphoreType.DMA((3,)),
        ],
        compiler_params=pltpu.CompilerParams(vmem_limit_bytes=LIMIT),
        name="input_spectrum",
    )(one, in_hbm(lines), in_hbm(inputs), in_hbm(ztab), in_hbm(ytab), fold_table())


def skip_kernel(lhs_hbm, after_hbm, skip_ref, rows_ref, fold_ref, term_hbm, g_lines, term, sems, out_sems):
    copies = []
    for chunk in range(CHUNKS):
        rows = line_rows(chunk)
        copies.append(whole_copy(lhs_hbm.at[rows], g_lines.at[rows], sems.at[chunk]))
    matrix = []
    for part in split(skip_ref[...]):
        wide = lax.dot_general(rows_ref[...], part, ACROSS, preferred_element_type=F32).astype(BF16)
        wide = lax.dot_general(wide, fold_ref[...], ACROSS, preferred_element_type=F32)
        matrix.append(jnp.where(same_row(), wide, 0.0).astype(BF16))
    matrix = jnp.concatenate(matrix, 0)
    outs = []
    for chunk in range(CHUNKS):
        copies[chunk].wait()
        for tile in range(TILES * chunk, TILES * chunk + TILES):
            rows = slice(8 * tile, 8 * tile + 8)
            g_high, g_low = tile_parts(g_lines, tile)
            out = dot(matrix, g_high)
            out = out[:256] + out[256:] + dot(matrix[:256], g_low)
            for plane in range(2):
                value = out[:, 128 * plane:128 * plane + 128].reshape(C, 8, N)
                term[:, plane, rows, :] = value
        rows = pl.ds(YB * chunk, YB)
        outs.append(whole_copy(term.at[:, :, rows, :], term_hbm.at[:, :, rows, :], out_sems.at[chunk]))
    for copy in outs:
        copy.wait()


def skip_term(lines, after, skip_weight):
    return pl.pallas_call(
        skip_kernel,
        in_specs=[any_spec()] * 2 + in_vmem(3),
        out_specs=any_spec(),
        out_shape=pltpu.HBM(FIELD, F32),
        scratch_shapes=[
            pltpu.VMEM(LINES, BF16), pltpu.VMEM(FIELD, F32),
            pltpu.SemaphoreType.DMA((CHUNKS,)), pltpu.SemaphoreType.DMA((CHUNKS,)),
        ],
        compiler_params=pltpu.CompilerParams(vmem_limit_bytes=LIMIT),
        name="skip_term",
    )(in_hbm(lines), after, skip_weight, rows_table(), fold_table())


FIRST = 16
SECOND = 40


def transform_x(recv_ref, rows_each, offset, xtab_ref, reorder):
    blocks = []
    for q in range(4):
        column = [recv_ref[pl.ds(offset + 4 * q + r, SPACE, stride=rows_each), :] for r in range(4)]
        blocks.append(jnp.concatenate(column, 0))
    high, low = split(jnp.concatenate(blocks, 1))
    out = dot(xtab_ref[...], high)
    spectrum = out[:2 * MX] + out[2 * MX:] + dot(xtab_ref[:2 * MX], low)
    out = dot(jnp.concatenate(split(spectrum), 0), reorder)
    return out[:2 * MX] + out[2 * MX:]


def to_rows(spectrum, scratch):
    count = spectrum.shape[0]
    lanes = lax.broadcasted_iota(jnp.int32, (count, 128), 1) >> 5
    for j in range(JL):
        block = spectrum[:, 128 * (j // 4):128 * (j // 4) + 128]
        scratch[pl.ds(j, count, stride=JL), :] = jnp.where(lanes == j % 4, block, 0.0)


WB = 8


def middle_kernel(
    dp_ref, recv_ref, xtab_ref, back_ref, w_hbm, input_hbm, send_hbm, mine_ref, theirs_ref,
    w_ref, spec, wide, dual, send, sems, out_sems,
):
    copies = []
    for block in range(MX // WB):
        rows = pl.ds(WB * block, WB)
        copies.append(whole_copy(w_hbm.at[rows], w_ref.at[rows], sems.at[block]))
    onward = pl.ds(16, 24)
    arriving = whole_copy(input_hbm, blocks_of(send).at[:, onward], out_sems.at[3])
    reorder = reorder_matrix()
    spread = spread_matrix()
    first = dp_ref[0] == 0
    spectrum = transform_x(recv_ref, FIRST, 0, xtab_ref, reorder)
    mine_ref[...] = jnp.where(first, spectrum[:MX], spectrum[MX:])
    theirs_ref[...] = jnp.where(first, spectrum[MX:], spectrum[:MX])
    to_rows(spectrum, spec)

    for block in range(MX // WB):
        start = 32 * (WB * block // 16) + WB * block % 16
        both = jnp.concatenate([spec[JL * k:JL * (k + WB), :] for k in (start, start + 16)], 0)
        high, low = split(both)
        wide[block % 2] = dot(jnp.concatenate([high, low], 1), spread)
        copies[block].wait()
        for local in range(WB):
            total_real, total_imag = None, None
            for tile in range(8):
                lanes = slice(128 * tile, 128 * tile + 128)
                real = wide[block % 2, JL * local:JL * local + JL, lanes]
                imag = wide[block % 2, JL * (WB + local):JL * (WB + local) + JL, lanes]
                m = WB * block + local
                w_real = w_ref[m, :, lanes]
                w_imag = w_ref[m, :, 1024 + 128 * tile:1024 + 128 * tile + 128]
                out_real = w_real * real + w_imag * imag
                out_imag = w_real * imag - w_imag * real
                total_real = out_real if tile == 0 else total_real + out_real
                total_imag = out_imag if tile == 0 else total_imag + out_imag
            for total, place in ((total_real, start + local), (total_imag, start + 16 + local)):
                total = total + pltpu.roll(total, 64, 1)
                dual[JL * place:JL * place + JL, :] = total + pltpu.roll(total, 32, 1)

    arriving.wait()
    copies = [whole_copy(blocks_of(send).at[:, onward], send_hbm.at[:, onward], out_sems.at[2])]
    lanes = lax.broadcasted_iota(jnp.int32, (2 * MX, 128), 1) // C
    blocks = []
    for j4 in range(4):
        block = dual[pl.ds(4 * j4, 2 * MX, stride=JL), :]
        for k in range(1, 4):
            block = jnp.where(lanes == k, dual[pl.ds(4 * j4 + k, 2 * MX, stride=JL), :], block)
        blocks.append(block)
    both = jnp.concatenate(split(jnp.concatenate(blocks, 1)), 0)
    ordered = lax.dot_general(both, reorder, ACROSS, preferred_element_type=F32)
    high, low = split(ordered[:2 * MX] + ordered[2 * MX:])
    out = dot(back_ref[...], jnp.concatenate([high, low, high], 0))
    for half in range(2):
        for q in (2 * half, 2 * half + 1):
            for r in range(4):
                send[pl.ds(4 * q + r, SPACE, stride=SECOND), :] = out[SPACE * r:SPACE * r + SPACE, 128 * q:128 * q + 128]
        rows = pl.ds(8 * half, 8)
        copies.append(whole_copy(blocks_of(send).at[:, rows], send_hbm.at[:, rows], sems.at[half]))
    for copy in copies:
        copy.wait()


def middle(dp, received, weights, input_rows):
    return pl.pallas_call(
        middle_kernel,
        in_specs=[pl.BlockSpec(memory_space=pltpu.SMEM)] + in_vmem(3) + [any_spec()] * 2,
        out_specs=[any_spec()] + in_vmem(2),
        out_shape=[
            pltpu.HBM((SPACE, SECOND, 128), F32),
            jax.ShapeDtypeStruct((MX, JL * C), F32),
            jax.ShapeDtypeStruct((MX, JL * C), F32),
        ],
        scratch_shapes=[
            pltpu.VMEM((MX, JL, 2 * C * C), F32), pltpu.VMEM((2 * MX * JL, 128), F32),
            pltpu.VMEM((2, 2 * WB * JL, C * C), F32), pltpu.VMEM((2 * MX * JL, 128), F32),
            pltpu.VMEM((SPACE * SECOND, 128), F32),
            pltpu.SemaphoreType.DMA((MX // WB,)), pltpu.SemaphoreType.DMA((4,)),
        ],
        compiler_params=pltpu.CompilerParams(vmem_limit_bytes=LIMIT),
        name="middle",
    )(dp, received, x_tables(), back_x_tables(), in_hbm(weights), in_hbm(input_rows))


def inputs_kernel(dp_ref, recv_ref, theirs_ref, xtab_ref, after_hbm, mine_ref, out_ref):
    spectrum = transform_x(recv_ref, SECOND, 16, xtab_ref, reorder_matrix())
    first = dp_ref[0] == 0
    mine_ref[...] = jnp.where(first, spectrum[:MX], spectrum[MX:])
    out_ref[:MX, :] = theirs_ref[...]
    out_ref[MX:2 * MX, :] = jnp.where(first, spectrum[MX:], spectrum[:MX])
    total = recv_ref[32:40, :]
    for source in range(1, SPACE):
        total = total + recv_ref[SECOND * source + 32:SECOND * source + 40, :]
    out_ref[2 * MX:, :] = jnp.concatenate([total] * 4, 1)


def inputs_spectrum(dp, received, theirs, after):
    return pl.pallas_call(
        inputs_kernel,
        in_specs=[pl.BlockSpec(memory_space=pltpu.SMEM)] + in_vmem(3) + [any_spec()],
        out_specs=in_vmem(2),
        out_shape=[
            jax.ShapeDtypeStruct((MX, JL * C), F32),
            jax.ShapeDtypeStruct((2 * MX + 8, JL * C), F32),
        ],
        compiler_params=pltpu.CompilerParams(vmem_limit_bytes=LIMIT),
        name="inputs_spectrum",
    )(dp, received, theirs, x_tables(), in_hbm(after))


MB = 4


def weight_kernel(
    grad_ref, field_ref, sent_ref, got_ref, out_hbm, skip_ref, grads, fields, wide, out, sems,
):
    spread = spread_matrix()
    to_rows(grad_ref[...], grads.at[0])
    to_rows(got_ref[:MX], grads.at[1])
    for b, value in enumerate((field_ref[...], got_ref[MX:2 * MX])):
        for j in range(JL):
            piece = value[:, C * j:C * j + C]
            fields[b, pl.ds(j, MX, stride=JL), :] = jnp.concatenate([piece] * 4, 1)
    copies = []
    for block in range(16 // MB):
        rows = jnp.concatenate(
            [grads[b, JL * k:JL * (k + MB), :] for b in range(2) for k in (MB * block, 16 + MB * block)], 0
        )
        high, low = split(rows)
        wide[...] = dot(jnp.concatenate([high, low], 1), spread)
        for local in range(MB):
            m = MB * block + local
            f = [fields[b, JL * k:JL * k + JL, :] for b in range(2) for k in (m, m + 16)]
            for tile in range(8):
                lanes = slice(128 * tile, 128 * tile + 128)
                g = [wide[JL * (MB * q + local):JL * (MB * q + local) + JL, lanes] for q in range(4)]
                out[m, :, lanes] = g[0] * f[0] + g[1] * f[1] + g[2] * f[2] + g[3] * f[3]
                out[m, :, 1024 + 128 * tile:1024 + 128 * tile + 128] = (
                    g[1] * f[0] - g[0] * f[1] + g[3] * f[2] - g[2] * f[3]
                )
        rows = pl.ds(MB * block, MB)
        copy = pltpu.make_async_copy(out.at[rows], out_hbm.at[rows], sems.at[block])
        copy.start()
        copies.append(copy)
    total = sent_ref[2 * MX:, :128] + got_ref[2 * MX:, :128]
    for q in range(4):
        skip_ref[8 * q:8 * q + 8, :] = total[:, C * q:C * q + C]
    for copy in copies:
        copy.wait()


def weight_gradient(grad_mine, field_mine, sent, got):
    return pl.pallas_call(
        weight_kernel,
        in_specs=in_vmem(4),
        out_specs=[any_spec(), vmem_spec()],
        out_shape=[pltpu.HBM((16, JL, 2 * C * C), F32), jax.ShapeDtypeStruct((C, C), F32)],
        scratch_shapes=[
            pltpu.VMEM((2, MX * JL, 128), F32), pltpu.VMEM((2, MX * JL, 128), F32),
            pltpu.VMEM((4 * MB * JL, C * C), F32), pltpu.VMEM((16, JL, 2 * C * C), F32),
            pltpu.SemaphoreType.DMA((16 // MB,)),
        ],
        compiler_params=pltpu.CompilerParams(vmem_limit_bytes=LIMIT),
        name="weight_gradient",
    )(grad_mine, field_mine, sent, got)


GB = 4


def backward_kernel(
    recv_ref, term_hbm, ytab_ref, ztab_hbm, out_hbm, term, ztab, out, half, lhs, sems, out_sems,
):
    copies = []
    for block in range(GROUPS // GB):
        rows = pl.ds(2 * GB * block, 2 * GB)
        copies.append(whole_copy(term_hbm.at[rows], term.at[rows], sems.at[block]))
        if block == 0:
            ztab_copy = whole_copy(ztab_hbm, ztab, sems.at[GROUPS // GB])
    for jq in range(4):
        for group_set in range(2):
            rows = [recv_ref[pl.ds(jq * SECOND + 8 * group_set + r, MZ, stride=4 * SECOND), :] for r in range(8)]
            turned = jnp.concatenate(rows, 0).T
            half[8 * group_set:8 * group_set + 8, JL * jq:JL * jq + JL, :] = turned.reshape(8, JL, 128)
    outs = []
    for block in range(GROUPS // GB):
        for pair in range(GB // 2):
            both = []
            for member in range(2):
                value = half[GB * block + 2 * pair + member]
                both.append(jnp.concatenate([value, lane_swap(value, -1.0)], 0))
            high, low = split(jnp.concatenate(both, 1))
            lines = dot(ytab_ref[...], jnp.concatenate([high, low, high], 0))
            for member in range(2):
                high, low = split(lines[:, 128 * member:128 * member + 128])
                rows = slice(128 * (2 * pair + member), 128 * (2 * pair + member) + 128)
                lhs[rows, :128] = high
                lhs[rows, 128:256] = low
                lhs[rows, 256:] = high
        if block == 0:
            ztab_copy.wait()
        value = dot(lhs[...], ztab[...])
        copies[block].wait()
        for group in range(GB):
            for inner in range(2):
                for plane in range(2):
                    lane = 128 * (2 * inner + plane)
                    place = 2 * (GB * block + group) + inner
                    out[place, plane] = value[128 * group:128 * group + 128, lane:lane + 128] + term[place, plane]
        rows = pl.ds(2 * GB * block, 2 * GB)
        copy = pltpu.make_async_copy(out.at[rows], out_hbm.at[0, rows], out_sems.at[block])
        copy.start()
        outs.append(copy)
    for copy in outs:
        copy.wait()


def backward(received, term):
    ztab = jnp.asarray(back_z_tables())
    return pl.pallas_call(
        backward_kernel,
        in_specs=[vmem_spec(), any_spec(), vmem_spec(), any_spec()],
        out_specs=any_spec(),
        out_shape=pltpu.HBM((1, C, 2, N, N), F32),
        scratch_shapes=[
            pltpu.VMEM(FIELD, F32), pltpu.VMEM(ztab.shape, BF16), pltpu.VMEM(FIELD, F32),
            pltpu.VMEM((GROUPS, MY, 128), F32), pltpu.VMEM((GB * 128, 384), BF16),
            pltpu.SemaphoreType.DMA((GROUPS // GB + 1,)), pltpu.SemaphoreType.DMA((GROUPS // GB,)),
        ],
        compiler_params=pltpu.CompilerParams(vmem_limit_bytes=LIMIT),
        name="backward",
    )(received, in_hbm(term), back_y_tables(), in_hbm(ztab))


def exchange(sent, rows):
    swapped = lax.all_to_all(sent, "space", 0, 0, tiled=True)
    return swapped.reshape(SPACE * rows, 128)


def body(inputs, preact, cotangent, spectral_weight, skip_weight):
    dp = lax.axis_index("dp").astype(jnp.int32).reshape(1)
    send_grad, lines = gradient_spectrum(preact, cotangent)
    got_grad = exchange(send_grad, FIRST)
    input_rows = input_spectrum(dp, lines, inputs)
    send_dual, grad_mine, grad_theirs = middle(dp, got_grad, spectral_weight, input_rows)
    got_dual = exchange(send_dual, SECOND)
    term = skip_term(lines, grad_mine, skip_weight)
    field_mine, sent = inputs_spectrum(dp, got_dual, grad_theirs, term)
    got = lax.ppermute(sent, "dp", [(0, 1), (1, 0)])
    input_grad = backward(got_dual, term)
    weight_grad, skip_grad = weight_gradient(grad_mine, field_mine, sent, got)
    return input_grad, weight_grad, skip_grad


def solution(mesh):
    in_specs = (
        P("dp", None, "space", None, None),
        P("dp", None, "space", None, None),
        P("dp", None, "space", None, None),
        P(None, "space", None),
        P(),
    )
    out_specs = (P("dp", None, "space", None, None), P("dp", "space", None), P())
    return jax.shard_map(body, mesh=mesh, in_specs=in_specs, out_specs=out_specs, check_vma=False)
```

```python
import functools

import jax
import jax.numpy as jnp
import numpy as np
from jax import lax
from jax.experimental import pallas as pl
from jax.experimental.pallas import tpu as pltpu
from jax.sharding import PartitionSpec as P

N = 128
C = 32
MX = 32
MY = 64
MZ = 16
SPACE = 64
GROUPS = C // 2
JL = 16
NORM = float(N) ** (-1.5)
TANH_SCALE = 0.7978845608028654
CUBIC = 0.044715
F32 = jnp.float32
BF16 = jnp.bfloat16
LIMIT = 40 * 1024 * 1024


def signed(count):
    index = np.arange(count)
    return np.where(index < count // 2, index, index - count)


def angles(frequency):
    points = np.arange(N)
    return 2.0 * np.pi / N * np.mod(frequency[:, None] * points[None, :], N)


ANGLE_X = angles(signed(MX))
ANGLE_Y = angles(signed(MY))
ANGLE_Z = angles(np.arange(MZ))


def halves(table):
    table = np.asarray(table, np.float64)
    high = table.astype(np.float32).astype(BF16)
    low = (table - high.astype(np.float64)).astype(np.float32).astype(BF16)
    return high, low


def split(value):
    high = value.astype(BF16)
    return high, (value - high.astype(F32)).astype(BF16)


def dot(left, right):
    return jnp.dot(left, right, preferred_element_type=F32)


def z_tables():
    high, low = halves(np.concatenate([np.cos(ANGLE_Z).T, -np.sin(ANGLE_Z).T], 1))
    table = np.zeros((4, 2, N, 2, 4, 2 * MZ), BF16)
    for plane in range(4):
        table[plane, 0, :, 0, plane] = high
        table[plane, 1, :, 0, plane] = high
        table[plane, 0, :, 1, plane] = low
    return table.reshape(8 * N, 256)


def y_tables():
    high, low = halves(np.concatenate([np.cos(ANGLE_Y), -np.sin(ANGLE_Y)], 0))
    return np.concatenate([high, high, low], 1)


def x_tables():
    cos_x, sin_x = np.cos(ANGLE_X), np.sin(ANGLE_X)
    table = np.zeros((2, MX, 2, N))
    table[0, :, 0], table[0, :, 1] = cos_x, sin_x
    table[1, :, 0], table[1, :, 1] = -sin_x, cos_x
    table = table.reshape(2, 2, MX // 2, 2, SPACE, 2).transpose(1, 0, 2, 5, 3, 4) * NORM
    high, low = halves(table.reshape(2 * MX, 4 * SPACE))
    return np.concatenate([high, low], 0)


def back_x_tables():
    cos_x, sin_x = np.cos(ANGLE_X), np.sin(ANGLE_X)
    table = np.zeros((2, MX, 2, N))
    table[0, :, 0], table[0, :, 1] = cos_x, sin_x
    table[1, :, 0], table[1, :, 1] = -sin_x, cos_x
    table = table.reshape(2, 2, MX // 2, 2, SPACE, 2).transpose(5, 3, 4, 1, 0, 2) * NORM
    high, low = halves(table.reshape(4 * SPACE, 2 * MX))
    return np.concatenate([high, high, low], 1)


def back_y_tables():
    high, low = halves(np.concatenate([np.cos(ANGLE_Y).T, np.sin(ANGLE_Y).T], 1))
    return np.concatenate([high, high, low], 1)


def back_z_tables():
    high, low = halves(np.concatenate([np.cos(ANGLE_Z), -np.sin(ANGLE_Z)], 0))
    table = np.zeros((3, 4, 2 * MZ, 4, N), BF16)
    for plane in range(4):
        table[0, plane, :, plane] = high
        table[1, plane, :, plane] = high
        table[2, plane, :, plane] = low
    return table.reshape(3 * 128, 4 * N)


def one_hot(hits):
    return jnp.where(hits, 1.0, 0.0).astype(BF16)


def reorder_matrix():
    row = lax.broadcasted_iota(jnp.int32, (C * JL, C * JL), 0)
    column = lax.broadcasted_iota(jnp.int32, (C * JL, C * JL), 1)
    sent, j = row >> 4, row & (JL - 1)
    channel = ((sent >> 4) * 8 + (sent & 7)) * 2 + ((sent >> 3) & 1)
    return one_hot(column == j * C + channel)


def spread_matrix():
    row = lax.broadcasted_iota(jnp.int32, (8 * C, C * C), 0)
    column = lax.broadcasted_iota(jnp.int32, (8 * C, C * C), 1)
    return one_hot((row & (C - 1)) == (column >> 5))


def rows_table():
    return np.repeat(np.eye(C), 8, 0).astype(BF16)


def fold_table():
    table = np.zeros((2, GROUPS, 8, C), BF16)
    for inner in range(2):
        for group in range(GROUPS):
            table[inner, group, :, 2 * group + inner] = 1
    return table.reshape(256, C)


def gelu_slope(h):
    square = h * h
    t = jnp.tanh(h * (TANH_SCALE + (TANH_SCALE * CUBIC) * square))
    inner = h * (0.5 * TANH_SCALE + (1.5 * TANH_SCALE * CUBIC) * square)
    return (0.5 + 0.5 * t) + (1.0 - t * t) * inner


def lane_swap(value, first_sign):
    lanes = lax.broadcasted_iota(jnp.int32, value.shape, value.ndim - 1)
    up = pltpu.roll(value, 128 - MZ, value.ndim - 1)
    down = pltpu.roll(value, MZ, value.ndim - 1)
    return jnp.where((lanes & MZ) == 0, first_sign * up, -first_sign * down)


YB = 32
CHUNKS = N // YB
TILES = YB // 8


def chunk_copy(ref, buffer, sem, chunk):
    rows = pl.ds(YB * chunk, YB)
    copy = pltpu.make_async_copy(ref.at[0, :, :, rows, :], buffer.at[:, :, rows, :], sem)
    copy.start()
    return copy


def whole_copy(ref, buffer, sem):
    copy = pltpu.make_async_copy(ref, buffer, sem)
    copy.start()
    return copy


def spread_lines(value, lhs, tile):
    value = value.reshape(GROUPS, 2, 2, 8, N)
    rows = slice(128 * tile, 128 * tile + 128)
    for inner in range(2):
        for plane in range(2):
            high, low = split(value[:, inner, plane].reshape(GROUPS * 8, N))
            lane = 256 * (2 * inner + plane)
            lhs[rows, lane:lane + 128] = high
            lhs[rows, lane + 128:lane + 256] = low


def transform_z(lhs, ztab_ref, scratch, chunk):
    out = dot(lhs[128 * TILES * chunk:128 * TILES * (chunk + 1), :], ztab_ref[...])
    out = out[:, :128] + out[:, 128:]
    for tile in range(TILES):
        place = YB * chunk + 8 * tile
        scratch[:, place:place + 8, :] = out[128 * tile:128 * tile + 128].reshape(GROUPS, 8, 128)


def transform_y(scratch, ytab_ref, half, group_set):
    for pair in range(4 * group_set, 4 * group_set + 4):
        wide = jnp.concatenate([scratch[2 * pair], scratch[2 * pair + 1]], 1)
        high, low = split(wide)
        out = dot(ytab_ref[...], jnp.concatenate([high, low, high], 0))
        for member in range(2):
            mine = out[:, 128 * member:128 * member + 128]
            half[2 * pair + member] = mine[:MY] + lane_swap(mine[MY:], -1.0)


def blocks_of(send):
    return send.reshape(SPACE, send.shape[0] // SPACE, 128)


def lay_out(half, send_ref, group_set):
    rows_each = send_ref.shape[0] // SPACE
    for jq in range(4):
        block = half[8 * group_set:8 * group_set + 8, JL * jq:JL * jq + JL, :]
        turned = block.reshape(128, 128).T
        for r in range(8):
            row = jq * rows_each + 8 * group_set + r
            send_ref[pl.ds(row, MZ, stride=4 * rows_each), :] = turned[MZ * r:MZ * r + MZ]


def finish(ytab, lines, half, send, send_hbm, out_sems):
    copies = []
    transform_y(lines, ytab, half, 0)
    transform_y(lines, ytab, half, 1)
    for group_set in range(2):
        lay_out(half, send, group_set)
        rows = pl.ds(8 * group_set, 8)
        copies.append(whole_copy(blocks_of(send).at[:, rows], send_hbm.at[:, rows], out_sems.at[group_set]))
    return copies


def line_rows(chunk):
    return pl.ds(128 * TILES * chunk, 128 * TILES)


def gradient_kernel(
    pre_hbm, cot_hbm, ztab_hbm, ytab_hbm, send_hbm, lhs_hbm,
    pre, cot, ztab, ytab, lhs, lines, half, send, sems, tab_sems, out_sems, lhs_sems,
):
    copies = [
        [chunk_copy(ref, buffer, sems.at[chunk, k], chunk) for k, ref, buffer in ((0, pre_hbm, pre), (1, cot_hbm, cot))]
        for chunk in range(CHUNKS)
    ]
    tables = [whole_copy(ztab_hbm, ztab, tab_sems.at[0]), whole_copy(ytab_hbm, ytab, tab_sems.at[1])]
    outs = []
    for chunk in range(CHUNKS):
        for copy in copies[chunk]:
            copy.wait()
        for tile in range(TILES * chunk, TILES * chunk + TILES):
            rows = slice(8 * tile, 8 * tile + 8)
            spread_lines(cot[:, :, rows, :] * gelu_slope(pre[:, :, rows, :]), lhs, tile)
    for chunk in range(CHUNKS):
        rows = line_rows(chunk)
        outs.append(whole_copy(lhs.at[rows], lhs_hbm.at[rows], lhs_sems.at[chunk]))
    for table in tables:
        table.wait()
    for chunk in range(CHUNKS):
        transform_z(lhs, ztab, lines, chunk)
    outs += finish(ytab, lines, half, send, send_hbm, out_sems)
    for copy in outs:
        copy.wait()


def in_vmem(count):
    return [pl.BlockSpec(memory_space=pltpu.VMEM) for _ in range(count)]


def vmem_spec():
    return pl.BlockSpec(memory_space=pltpu.VMEM)


def any_spec():
    return pl.BlockSpec(memory_space=pl.ANY)


FIELD = (C, 2, N, N)


PAIR = (N // 8, 256, 256)


def in_hbm(value):
    return pltpu.with_memory_space_constraint(value, pltpu.HBM)


def kept(value):
    return pltpu.with_memory_space_constraint(value, pltpu.VMEM)


LINES = (2048, 1024)


def gradient_spectrum(preact, cotangent):
    ztab, ytab = jnp.asarray(z_tables()), jnp.asarray(y_tables())
    return pl.pallas_call(
        gradient_kernel,
        in_specs=[any_spec()] * 4,
        out_specs=[any_spec()] * 2,
        out_shape=[pltpu.HBM((SPACE, FIRST, 128), F32), pltpu.HBM(LINES, BF16)],
        scratch_shapes=[pltpu.VMEM(FIELD, F32)] * 2 + [
            pltpu.VMEM(ztab.shape, BF16), pltpu.VMEM(ytab.shape, BF16), pltpu.VMEM(LINES, BF16),
            pltpu.VMEM((GROUPS, N, 128), F32), pltpu.VMEM((GROUPS, MY, 128), F32), pltpu.VMEM((SPACE * FIRST, 128), F32),
            pltpu.SemaphoreType.DMA((CHUNKS, 2)), pltpu.SemaphoreType.DMA((2,)), pltpu.SemaphoreType.DMA((2,)),
            pltpu.SemaphoreType.DMA((CHUNKS,)),
        ],
        compiler_params=pltpu.CompilerParams(vmem_limit_bytes=LIMIT),
        name="gradient_spectrum",
    )(in_hbm(preact), in_hbm(cotangent), in_hbm(ztab), in_hbm(ytab))


ACROSS = (((1,), (1,)), ((), ()))


def same_row():
    left = lax.broadcasted_iota(jnp.int32, (256, 256), 0) & 7
    right = lax.broadcasted_iota(jnp.int32, (256, 256), 1) & 7
    return left == right


def tile_parts(lines, tile):
    rows = slice(128 * tile, 128 * tile + 128)
    return [
        jnp.concatenate([
            jnp.concatenate([
                lines[rows, 512 * inner + 256 * plane + part:512 * inner + 256 * plane + part + 128] for plane in range(2)
            ], 1) for inner in range(2)
        ], 0) for part in (0, 128)
    ]


def input_kernel(
    one_ref, lhs_hbm, inp_hbm, ztab_hbm, ytab_hbm, w_hbm, fold_ref, send_hbm, w_ref,
    g_lines, inp, ztab, ytab, lhs, acc, lines, half, send, sems, tab_sems, out_sems,
):
    always = one_ref[0] >= 0
    copies = []
    for chunk in range(CHUNKS):
        rows = line_rows(chunk)
        copies.append([
            chunk_copy(inp_hbm, inp, sems.at[chunk, 0], chunk),
            whole_copy(lhs_hbm.at[rows], g_lines.at[rows], sems.at[chunk, 1]),
        ])
    tables = [whole_copy(ztab_hbm, ztab, tab_sems.at[0]), whole_copy(ytab_hbm, ytab, tab_sems.at[1])]
    ahead = whole_copy(w_hbm.at[pl.ds(0, WB)], w_ref, tab_sems.at[2])
    for chunk in range(CHUNKS):
        for copy in copies[chunk]:
            copy.wait()

        @pl.when(always)
        def _():
            for tile in range(TILES * chunk, TILES * chunk + TILES):
                spread_lines(inp[:, :, 8 * tile:8 * tile + 8, :], lhs, tile)

        if chunk == 0:
            tables[0].wait()

        @pl.when(always)
        def _():
            transform_z(lhs, ztab, lines, chunk)

        @pl.when(always)
        def _():
            for tile in range(TILES * chunk, TILES * chunk + TILES):
                g_high, g_low = tile_parts(g_lines, tile)
                i_high, i_low = tile_parts(lhs, tile)
                total = (
                    lax.dot_general(g_high, i_high, ACROSS, preferred_element_type=F32)
                    + lax.dot_general(g_low, i_high, ACROSS, preferred_element_type=F32)
                    + lax.dot_general(g_high, i_low, ACROSS, preferred_element_type=F32)
                )
                if tile == 0:
                    acc[...] = total
                else:
                    acc[...] += total

    diagonal = jnp.where(same_row(), acc[...], 0.0) * NORM
    fold = fold_ref[...].astype(F32)
    folded = jnp.dot(diagonal, fold, preferred_element_type=F32, precision=lax.Precision.HIGHEST)
    summed = lax.dot_general(
        fold, folded, (((0,), (0,)), ((), ())), preferred_element_type=F32,
        precision=lax.Precision.HIGHEST,
    )
    part = jnp.concatenate([summed[8 * q:8 * q + 8, :] for q in range(4)], 1)
    for dest in range(SPACE):
        send[24 * dest + 16:24 * dest + 24, :] = part
    rows = pl.ds(16, 8)
    outs = [whole_copy(blocks_of(send).at[:, rows], send_hbm.at[:, rows], out_sems.at[2])]
    tables[1].wait()
    outs += finish(ytab, lines, half, send, send_hbm, out_sems)
    ahead.wait()
    for copy in outs:
        copy.wait()


def input_spectrum(one, lines, inputs, weights):
    ztab, ytab = jnp.asarray(z_tables()), jnp.asarray(y_tables())
    return pl.pallas_call(
        input_kernel,
        in_specs=[pl.BlockSpec(memory_space=pltpu.SMEM)] + [any_spec()] * 5 + [vmem_spec()],
        out_specs=[any_spec(), vmem_spec()],
        out_shape=[pltpu.HBM((SPACE, 24, 128), F32), pltpu.VMEM((WB, JL, 2 * C * C), F32)],
        scratch_shapes=[
            pltpu.VMEM(LINES, BF16), pltpu.VMEM(FIELD, F32),
            pltpu.VMEM(ztab.shape, BF16), pltpu.VMEM(ytab.shape, BF16), pltpu.VMEM(LINES, BF16),
            pltpu.VMEM((256, 256), F32),
            pltpu.VMEM((GROUPS, N, 128), F32), pltpu.VMEM((GROUPS, MY, 128), F32), pltpu.VMEM((SPACE * 24, 128), F32),
            pltpu.SemaphoreType.DMA((CHUNKS, 2)), pltpu.SemaphoreType.DMA((3,)), pltpu.SemaphoreType.DMA((3,)),
        ],
        compiler_params=pltpu.CompilerParams(vmem_limit_bytes=LIMIT),
        name="input_spectrum",
    )(one, in_hbm(lines), in_hbm(inputs), in_hbm(ztab), in_hbm(ytab), in_hbm(weights), fold_table())


def skip_kernel(lhs_hbm, after_hbm, skip_ref, rows_ref, fold_ref, term_hbm, g_lines, term, sems, out_sems):
    copies = []
    for chunk in range(CHUNKS):
        rows = line_rows(chunk)
        copies.append(whole_copy(lhs_hbm.at[rows], g_lines.at[rows], sems.at[chunk]))
    matrix = []
    for part in split(skip_ref[...]):
        wide = lax.dot_general(rows_ref[...], part, ACROSS, preferred_element_type=F32).astype(BF16)
        wide = lax.dot_general(wide, fold_ref[...], ACROSS, preferred_element_type=F32)
        matrix.append(jnp.where(same_row(), wide, 0.0).astype(BF16))
    matrix = jnp.concatenate(matrix, 0)
    outs = []
    for chunk in range(CHUNKS):
        copies[chunk].wait()
        for tile in range(TILES * chunk, TILES * chunk + TILES):
            rows = slice(8 * tile, 8 * tile + 8)
            g_high, g_low = tile_parts(g_lines, tile)
            out = dot(matrix, g_high)
            out = out[:256] + out[256:] + dot(matrix[:256], g_low)
            for plane in range(2):
                value = out[:, 128 * plane:128 * plane + 128].reshape(C, 8, N)
                term[:, plane, rows, :] = value
        rows = pl.ds(YB * chunk, YB)
        outs.append(whole_copy(term.at[:, :, rows, :], term_hbm.at[:, :, rows, :], out_sems.at[chunk]))
    for copy in outs:
        copy.wait()


def skip_term(lines, after, skip_weight):
    return pl.pallas_call(
        skip_kernel,
        in_specs=[any_spec()] * 2 + in_vmem(3),
        out_specs=any_spec(),
        out_shape=pltpu.HBM(FIELD, F32),
        scratch_shapes=[
            pltpu.VMEM(LINES, BF16), pltpu.VMEM(FIELD, F32),
            pltpu.SemaphoreType.DMA((CHUNKS,)), pltpu.SemaphoreType.DMA((CHUNKS,)),
        ],
        compiler_params=pltpu.CompilerParams(vmem_limit_bytes=LIMIT),
        name="skip_term",
    )(in_hbm(lines), after, skip_weight, rows_table(), fold_table())


FIRST = 16
SECOND = 40


def transform_x(recv_ref, rows_each, offset, xtab_ref, reorder):
    blocks = []
    for q in range(4):
        column = [recv_ref[pl.ds(offset + 4 * q + r, SPACE, stride=rows_each), :] for r in range(4)]
        blocks.append(jnp.concatenate(column, 0))
    high, low = split(jnp.concatenate(blocks, 1))
    out = dot(xtab_ref[...], high)
    spectrum = out[:2 * MX] + out[2 * MX:] + dot(xtab_ref[:2 * MX], low)
    out = dot(jnp.concatenate(split(spectrum), 0), reorder)
    return out[:2 * MX] + out[2 * MX:]


def to_rows(spectrum, scratch):
    count = spectrum.shape[0]
    lanes = lax.broadcasted_iota(jnp.int32, (count, 128), 1) >> 5
    for j in range(JL):
        block = spectrum[:, 128 * (j // 4):128 * (j // 4) + 128]
        scratch[pl.ds(j, count, stride=JL), :] = jnp.where(lanes == j % 4, block, 0.0)


WB = 8


def middle_kernel(
    dp_ref, recv_ref, xtab_ref, back_ref, early_ref, w_hbm, input_hbm, send_hbm, mine_ref, theirs_ref,
    w_ref, spec, wide, dual, send, sems, out_sems,
):
    copies = [None]
    for block in range(1, MX // WB):
        rows = pl.ds(WB * block, WB)
        copies.append(whole_copy(w_hbm.at[rows], w_ref.at[rows], sems.at[block]))
    onward = pl.ds(16, 24)
    arriving = whole_copy(input_hbm, blocks_of(send).at[:, onward], out_sems.at[3])
    reorder = reorder_matrix()
    spread = spread_matrix()
    first = dp_ref[0] == 0
    spectrum = transform_x(recv_ref, FIRST, 0, xtab_ref, reorder)
    mine_ref[...] = jnp.where(first, spectrum[:MX], spectrum[MX:])
    theirs_ref[...] = jnp.where(first, spectrum[MX:], spectrum[:MX])
    to_rows(spectrum, spec)

    for block in range(MX // WB):
        start = 32 * (WB * block // 16) + WB * block % 16
        both = jnp.concatenate([spec[JL * k:JL * (k + WB), :] for k in (start, start + 16)], 0)
        high, low = split(both)
        wide[block % 2] = dot(jnp.concatenate([high, low], 1), spread)
        if block > 0:
            copies[block].wait()
        for local in range(WB):
            total_real, total_imag = None, None
            for tile in range(8):
                lanes = slice(128 * tile, 128 * tile + 128)
                real = wide[block % 2, JL * local:JL * local + JL, lanes]
                imag = wide[block % 2, JL * (WB + local):JL * (WB + local) + JL, lanes]
                m = WB * block + local
                w_real = early_ref[m, :, lanes] if block == 0 else w_ref[m, :, lanes]
                far = slice(1024 + 128 * tile, 1024 + 128 * tile + 128)
                w_imag = early_ref[m, :, far] if block == 0 else w_ref[m, :, far]
                out_real = w_real * real + w_imag * imag
                out_imag = w_real * imag - w_imag * real
                total_real = out_real if tile == 0 else total_real + out_real
                total_imag = out_imag if tile == 0 else total_imag + out_imag
            for total, place in ((total_real, start + local), (total_imag, start + 16 + local)):
                total = total + pltpu.roll(total, 64, 1)
                dual[JL * place:JL * place + JL, :] = total + pltpu.roll(total, 32, 1)

    arriving.wait()
    copies = [whole_copy(blocks_of(send).at[:, onward], send_hbm.at[:, onward], out_sems.at[2])]
    lanes = lax.broadcasted_iota(jnp.int32, (2 * MX, 128), 1) // C
    blocks = []
    for j4 in range(4):
        block = dual[pl.ds(4 * j4, 2 * MX, stride=JL), :]
        for k in range(1, 4):
            block = jnp.where(lanes == k, dual[pl.ds(4 * j4 + k, 2 * MX, stride=JL), :], block)
        blocks.append(block)
    both = jnp.concatenate(split(jnp.concatenate(blocks, 1)), 0)
    ordered = lax.dot_general(both, reorder, ACROSS, preferred_element_type=F32)
    high, low = split(ordered[:2 * MX] + ordered[2 * MX:])
    wide_lines = jnp.concatenate([high, low, high], 0)
    for half in range(2):
        out = dot(back_ref[...], wide_lines[:, 256 * half:256 * half + 256])
        for k in range(2):
            for r in range(4):
                send[pl.ds(4 * (2 * half + k) + r, SPACE, stride=SECOND), :] = (
                    out[SPACE * r:SPACE * r + SPACE, 128 * k:128 * k + 128]
                )
        rows = pl.ds(8 * half, 8)
        copies.append(whole_copy(blocks_of(send).at[:, rows], send_hbm.at[:, rows], out_sems.at[half]))
    for copy in copies:
        copy.wait()


def middle(dp, received, early, weights, input_rows):
    return pl.pallas_call(
        middle_kernel,
        in_specs=[pl.BlockSpec(memory_space=pltpu.SMEM)] + in_vmem(4) + [any_spec()] * 2,
        out_specs=[any_spec()] + in_vmem(2),
        out_shape=[
            pltpu.HBM((SPACE, SECOND, 128), F32),
            jax.ShapeDtypeStruct((MX, JL * C), F32),
            jax.ShapeDtypeStruct((MX, JL * C), F32),
        ],
        scratch_shapes=[
            pltpu.VMEM((MX, JL, 2 * C * C), F32), pltpu.VMEM((2 * MX * JL, 128), F32),
            pltpu.VMEM((2, 2 * WB * JL, C * C), F32), pltpu.VMEM((2 * MX * JL, 128), F32),
            pltpu.VMEM((SPACE * SECOND, 128), F32),
            pltpu.SemaphoreType.DMA((MX // WB,)), pltpu.SemaphoreType.DMA((4,)),
        ],
        compiler_params=pltpu.CompilerParams(vmem_limit_bytes=LIMIT),
        name="middle",
    )(dp, received, x_tables(), back_x_tables(), kept(early), in_hbm(weights), in_hbm(input_rows))


def inputs_kernel(dp_ref, recv_ref, theirs_ref, xtab_ref, after_hbm, mine_ref, out_ref):
    spectrum = transform_x(recv_ref, SECOND, 16, xtab_ref, reorder_matrix())
    first = dp_ref[0] == 0
    mine_ref[...] = jnp.where(first, spectrum[:MX], spectrum[MX:])
    out_ref[:MX, :] = theirs_ref[...]
    out_ref[MX:2 * MX, :] = jnp.where(first, spectrum[MX:], spectrum[:MX])
    total = recv_ref[32:40, :]
    for source in range(1, SPACE):
        total = total + recv_ref[SECOND * source + 32:SECOND * source + 40, :]
    out_ref[2 * MX:, :] = jnp.concatenate([total] * 4, 1)


def inputs_spectrum(dp, received, theirs, after):
    return pl.pallas_call(
        inputs_kernel,
        in_specs=[pl.BlockSpec(memory_space=pltpu.SMEM)] + in_vmem(3) + [any_spec()],
        out_specs=in_vmem(2),
        out_shape=[
            jax.ShapeDtypeStruct((MX, JL * C), F32),
            jax.ShapeDtypeStruct((2 * MX + 8, JL * C), F32),
        ],
        compiler_params=pltpu.CompilerParams(vmem_limit_bytes=LIMIT),
        name="inputs_spectrum",
    )(dp, received, theirs, x_tables(), in_hbm(after))


MB = 4


def weight_kernel(
    grad_ref, field_ref, sent_ref, got_ref, out_hbm, skip_ref, grads, fields, wide, out, sems,
):
    spread = spread_matrix()
    to_rows(grad_ref[...], grads.at[0])
    to_rows(got_ref[:MX], grads.at[1])
    for b, value in enumerate((field_ref[...], got_ref[MX:2 * MX])):
        for j in range(JL):
            piece = value[:, C * j:C * j + C]
            fields[b, pl.ds(j, MX, stride=JL), :] = jnp.concatenate([piece] * 4, 1)
    copies = []
    for block in range(16 // MB):
        rows = jnp.concatenate(
            [grads[b, JL * k:JL * (k + MB), :] for b in range(2) for k in (MB * block, 16 + MB * block)], 0
        )
        high, low = split(rows)
        wide[...] = dot(jnp.concatenate([high, low], 1), spread)
        for local in range(MB):
            m = MB * block + local
            f = [fields[b, JL * k:JL * k + JL, :] for b in range(2) for k in (m, m + 16)]
            for tile in range(8):
                lanes = slice(128 * tile, 128 * tile + 128)
                g = [wide[JL * (MB * q + local):JL * (MB * q + local) + JL, lanes] for q in range(4)]
                out[m, :, lanes] = g[0] * f[0] + g[1] * f[1] + g[2] * f[2] + g[3] * f[3]
                out[m, :, 1024 + 128 * tile:1024 + 128 * tile + 128] = (
                    g[1] * f[0] - g[0] * f[1] + g[3] * f[2] - g[2] * f[3]
                )
        rows = pl.ds(MB * block, MB)
        copy = pltpu.make_async_copy(out.at[rows], out_hbm.at[rows], sems.at[block])
        copy.start()
        copies.append(copy)
    total = sent_ref[2 * MX:, :128] + got_ref[2 * MX:, :128]
    for q in range(4):
        skip_ref[8 * q:8 * q + 8, :] = total[:, C * q:C * q + C]
    for copy in copies:
        copy.wait()


def weight_gradient(grad_mine, field_mine, sent, got):
    return pl.pallas_call(
        weight_kernel,
        in_specs=in_vmem(4),
        out_specs=[any_spec(), vmem_spec()],
        out_shape=[pltpu.HBM((16, JL, 2 * C * C), F32), jax.ShapeDtypeStruct((C, C), F32)],
        scratch_shapes=[
            pltpu.VMEM((2, MX * JL, 128), F32), pltpu.VMEM((2, MX * JL, 128), F32),
            pltpu.VMEM((4 * MB * JL, C * C), F32), pltpu.VMEM((16, JL, 2 * C * C), F32),
            pltpu.SemaphoreType.DMA((16 // MB,)),
        ],
        compiler_params=pltpu.CompilerParams(vmem_limit_bytes=LIMIT),
        name="weight_gradient",
    )(grad_mine, field_mine, sent, got)


GB = 4


def backward_kernel(
    recv_ref, term_hbm, ytab_ref, ztab_hbm, out_hbm, term, ztab, out, half, lhs, sems, out_sems,
):
    copies = []
    for block in range(GROUPS // GB):
        rows = pl.ds(2 * GB * block, 2 * GB)
        copies.append(whole_copy(term_hbm.at[rows], term.at[rows], sems.at[block]))
        if block == 0:
            ztab_copy = whole_copy(ztab_hbm, ztab, sems.at[GROUPS // GB])
    for jq in range(4):
        for group_set in range(2):
            rows = [recv_ref[pl.ds(jq * SECOND + 8 * group_set + r, MZ, stride=4 * SECOND), :] for r in range(8)]
            turned = jnp.concatenate(rows, 0).T
            half[8 * group_set:8 * group_set + 8, JL * jq:JL * jq + JL, :] = turned.reshape(8, JL, 128)
    outs = []
    for block in range(GROUPS // GB):
        for pair in range(GB // 2):
            both = []
            for member in range(2):
                value = half[GB * block + 2 * pair + member]
                both.append(jnp.concatenate([value, lane_swap(value, -1.0)], 0))
            high, low = split(jnp.concatenate(both, 1))
            lines = dot(ytab_ref[...], jnp.concatenate([high, low, high], 0))
            for member in range(2):
                high, low = split(lines[:, 128 * member:128 * member + 128])
                rows = slice(128 * (2 * pair + member), 128 * (2 * pair + member) + 128)
                lhs[rows, :128] = high
                lhs[rows, 128:256] = low
                lhs[rows, 256:] = high
        if block == 0:
            ztab_copy.wait()
        copies[block].wait()
        value = jnp.concatenate([dot(lhs[256 * k:256 * k + 256, :], ztab[...]) for k in range(GB // 2)], 0)
        for group in range(GB):
            for inner in range(2):
                for plane in range(2):
                    lane = 128 * (2 * inner + plane)
                    place = 2 * (GB * block + group) + inner
                    out[place, plane] = value[128 * group:128 * group + 128, lane:lane + 128] + term[place, plane]
        rows = pl.ds(2 * GB * block, 2 * GB)
        copy = pltpu.make_async_copy(out.at[rows], out_hbm.at[0, rows], out_sems.at[block])
        copy.start()
        outs.append(copy)
    for copy in outs:
        copy.wait()


def backward(received, term):
    ztab = jnp.asarray(back_z_tables())
    return pl.pallas_call(
        backward_kernel,
        in_specs=[vmem_spec(), any_spec(), vmem_spec(), any_spec()],
        out_specs=any_spec(),
        out_shape=pltpu.HBM((1, C, 2, N, N), F32),
        scratch_shapes=[
            pltpu.VMEM(FIELD, F32), pltpu.VMEM(ztab.shape, BF16), pltpu.VMEM(FIELD, F32),
            pltpu.VMEM((GROUPS, MY, 128), F32), pltpu.VMEM((GB * 128, 384), BF16),
            pltpu.SemaphoreType.DMA((GROUPS // GB + 1,)), pltpu.SemaphoreType.DMA((GROUPS // GB,)),
        ],
        compiler_params=pltpu.CompilerParams(vmem_limit_bytes=LIMIT),
        name="backward",
    )(received, in_hbm(term), back_y_tables(), in_hbm(ztab))


def exchange(sent, rows):
    swapped = lax.all_to_all(sent, "space", 0, 0, tiled=True)
    return swapped.reshape(SPACE * rows, 128)


def body(inputs, preact, cotangent, spectral_weight, skip_weight):
    dp = lax.axis_index("dp").astype(jnp.int32).reshape(1)
    send_grad, lines = gradient_spectrum(preact, cotangent)
    got_grad = exchange(send_grad, FIRST)
    input_rows, early = input_spectrum(dp, lines, inputs, spectral_weight)
    send_dual, grad_mine, grad_theirs = middle(dp, got_grad, early, spectral_weight, input_rows)
    got_dual = exchange(send_dual, SECOND)
    term = skip_term(lines, grad_mine, skip_weight)
    field_mine, sent = inputs_spectrum(dp, got_dual, grad_theirs, term)
    got = lax.ppermute(sent, "dp", [(0, 1), (1, 0)])
    input_grad = backward(got_dual, term)
    weight_grad, skip_grad = weight_gradient(grad_mine, field_mine, sent, got)
    return input_grad, weight_grad, skip_grad


def solution(mesh):
    in_specs = (
        P("dp", None, "space", None, None),
        P("dp", None, "space", None, None),
        P("dp", None, "space", None, None),
        P(None, "space", None),
        P(),
    )
    out_specs = (P("dp", None, "space", None, None), P("dp", "space", None), P())
    return jax.shard_map(body, mesh=mesh, in_specs=in_specs, out_specs=out_specs, check_vma=False)
```

```python
import functools

import jax
import jax.numpy as jnp
import numpy as np
from jax import lax
from jax.experimental import pallas as pl
from jax.experimental.pallas import tpu as pltpu
from jax.sharding import PartitionSpec as P

N = 128
C = 32
MX = 32
MY = 64
MZ = 16
SPACE = 64
GROUPS = C // 2
JL = 16
NORM = float(N) ** (-1.5)
TANH_SCALE = 0.7978845608028654
CUBIC = 0.044715
F32 = jnp.float32
BF16 = jnp.bfloat16
LIMIT = 40 * 1024 * 1024


def signed(count):
    index = np.arange(count)
    return np.where(index < count // 2, index, index - count)


def angles(frequency):
    points = np.arange(N)
    return 2.0 * np.pi / N * np.mod(frequency[:, None] * points[None, :], N)


ANGLE_X = angles(signed(MX))
ANGLE_Y = angles(signed(MY))
ANGLE_Z = angles(np.arange(MZ))


def halves(table):
    table = np.asarray(table, np.float64)
    high = table.astype(np.float32).astype(BF16)
    low = (table - high.astype(np.float64)).astype(np.float32).astype(BF16)
    return high, low


def split(value):
    high = value.astype(BF16)
    return high, (value - high.astype(F32)).astype(BF16)


def dot(left, right):
    return jnp.dot(left, right, preferred_element_type=F32)


def z_tables():
    high, low = halves(np.concatenate([np.cos(ANGLE_Z).T, -np.sin(ANGLE_Z).T], 1))
    table = np.zeros((4, 2, N, 2, 4, 2 * MZ), BF16)
    for plane in range(4):
        table[plane, 0, :, 0, plane] = high
        table[plane, 1, :, 0, plane] = high
        table[plane, 0, :, 1, plane] = low
    return table.reshape(8 * N, 256)


def y_tables():
    high, low = halves(np.concatenate([np.cos(ANGLE_Y), -np.sin(ANGLE_Y)], 0))
    return np.concatenate([high, high, low], 1)


def x_tables():
    cos_x, sin_x = np.cos(ANGLE_X), np.sin(ANGLE_X)
    table = np.zeros((2, MX, 2, N))
    table[0, :, 0], table[0, :, 1] = cos_x, sin_x
    table[1, :, 0], table[1, :, 1] = -sin_x, cos_x
    table = table.reshape(2, 2, MX // 2, 2, SPACE, 2).transpose(1, 0, 2, 5, 3, 4) * NORM
    high, low = halves(table.reshape(2 * MX, 4 * SPACE))
    return np.concatenate([high, low], 0)


def back_x_tables():
    cos_x, sin_x = np.cos(ANGLE_X), np.sin(ANGLE_X)
    table = np.zeros((2, MX, 2, N))
    table[0, :, 0], table[0, :, 1] = cos_x, sin_x
    table[1, :, 0], table[1, :, 1] = -sin_x, cos_x
    table = table.reshape(2, 2, MX // 2, 2, SPACE, 2).transpose(5, 3, 4, 1, 0, 2) * NORM
    high, low = halves(table.reshape(4 * SPACE, 2 * MX))
    return np.concatenate([high, high, low], 1)


def back_y_tables():
    high, low = halves(np.concatenate([np.cos(ANGLE_Y).T, np.sin(ANGLE_Y).T], 1))
    return np.concatenate([high, high, low], 1)


def back_z_tables():
    high, low = halves(np.concatenate([np.cos(ANGLE_Z), -np.sin(ANGLE_Z)], 0))
    table = np.zeros((3, 4, 2 * MZ, 4, N), BF16)
    for plane in range(4):
        table[0, plane, :, plane] = high
        table[1, plane, :, plane] = high
        table[2, plane, :, plane] = low
    return table.reshape(3 * 128, 4 * N)


def one_hot(hits):
    return jnp.where(hits, 1.0, 0.0).astype(BF16)


def reorder_matrix():
    row = lax.broadcasted_iota(jnp.int32, (C * JL, C * JL), 0)
    column = lax.broadcasted_iota(jnp.int32, (C * JL, C * JL), 1)
    sent, j = row >> 4, row & (JL - 1)
    channel = ((sent >> 4) * 8 + (sent & 7)) * 2 + ((sent >> 3) & 1)
    return one_hot(column == j * C + channel)


def spread_matrix():
    row = lax.broadcasted_iota(jnp.int32, (8 * C, C * C), 0)
    column = lax.broadcasted_iota(jnp.int32, (8 * C, C * C), 1)
    return one_hot((row & (C - 1)) == (column >> 5))


def rows_table():
    return np.repeat(np.eye(C), 8, 0).astype(BF16)


def fold_table():
    table = np.zeros((2, GROUPS, 8, C), BF16)
    for inner in range(2):
        for group in range(GROUPS):
            table[inner, group, :, 2 * group + inner] = 1
    return table.reshape(256, C)


def gelu_slope(h):
    square = h * h
    t = jnp.tanh(h * (TANH_SCALE + (TANH_SCALE * CUBIC) * square))
    inner = h * (0.5 * TANH_SCALE + (1.5 * TANH_SCALE * CUBIC) * square)
    return (0.5 + 0.5 * t) + (1.0 - t * t) * inner


def lane_swap(value, first_sign):
    lanes = lax.broadcasted_iota(jnp.int32, value.shape, value.ndim - 1)
    up = pltpu.roll(value, 128 - MZ, value.ndim - 1)
    down = pltpu.roll(value, MZ, value.ndim - 1)
    return jnp.where((lanes & MZ) == 0, first_sign * up, -first_sign * down)


YB = 32
CHUNKS = N // YB
TILES = YB // 8


def chunk_copy(ref, buffer, sem, chunk):
    rows = pl.ds(YB * chunk, YB)
    copy = pltpu.make_async_copy(ref.at[0, :, :, rows, :], buffer.at[:, :, rows, :], sem)
    copy.start()
    return copy


def whole_copy(ref, buffer, sem):
    copy = pltpu.make_async_copy(ref, buffer, sem)
    copy.start()
    return copy


def spread_lines(value, lhs, tile):
    value = value.reshape(GROUPS, 2, 2, 8, N)
    rows = slice(128 * tile, 128 * tile + 128)
    for inner in range(2):
        for plane in range(2):
            high, low = split(value[:, inner, plane].reshape(GROUPS * 8, N))
            lane = 256 * (2 * inner + plane)
            lhs[rows, lane:lane + 128] = high
            lhs[rows, lane + 128:lane + 256] = low


def transform_z(lhs, ztab_ref, scratch, chunk):
    out = dot(lhs[128 * TILES * chunk:128 * TILES * (chunk + 1), :], ztab_ref[...])
    out = out[:, :128] + out[:, 128:]
    for tile in range(TILES):
        place = YB * chunk + 8 * tile
        scratch[:, place:place + 8, :] = out[128 * tile:128 * tile + 128].reshape(GROUPS, 8, 128)


def transform_y(scratch, ytab_ref, half, group_set):
    for pair in range(4 * group_set, 4 * group_set + 4):
        wide = jnp.concatenate([scratch[2 * pair], scratch[2 * pair + 1]], 1)
        high, low = split(wide)
        out = dot(ytab_ref[...], jnp.concatenate([high, low, high], 0))
        for member in range(2):
            mine = out[:, 128 * member:128 * member + 128]
            half[2 * pair + member] = mine[:MY] + lane_swap(mine[MY:], -1.0)


def blocks_of(send):
    return send.reshape(SPACE, send.shape[0] // SPACE, 128)


def lay_out(half, send_ref, group_set):
    rows_each = send_ref.shape[0] // SPACE
    for jq in range(4):
        block = half[8 * group_set:8 * group_set + 8, JL * jq:JL * jq + JL, :]
        turned = block.reshape(128, 128).T
        for r in range(8):
            row = jq * rows_each + 8 * group_set + r
            send_ref[pl.ds(row, MZ, stride=4 * rows_each), :] = turned[MZ * r:MZ * r + MZ]


def finish(ytab, lines, half, send, send_hbm, out_sems):
    copies = []
    transform_y(lines, ytab, half, 0)
    transform_y(lines, ytab, half, 1)
    for group_set in range(2):
        lay_out(half, send, group_set)
        rows = pl.ds(8 * group_set, 8)
        copies.append(whole_copy(blocks_of(send).at[:, rows], send_hbm.at[:, rows], out_sems.at[group_set]))
    return copies


def line_rows(chunk):
    return pl.ds(128 * TILES * chunk, 128 * TILES)


def gradient_kernel(
    pre_hbm, cot_hbm, ztab_hbm, ytab_hbm, send_hbm, lhs_hbm,
    pre, cot, ztab, ytab, lhs, lines, half, send, sems, tab_sems, out_sems, lhs_sems,
):
    copies = [
        [chunk_copy(ref, buffer, sems.at[chunk, k], chunk) for k, ref, buffer in ((0, pre_hbm, pre), (1, cot_hbm, cot))]
        for chunk in range(CHUNKS)
    ]
    tables = [whole_copy(ztab_hbm, ztab, tab_sems.at[0]), whole_copy(ytab_hbm, ytab, tab_sems.at[1])]
    outs = []
    for chunk in range(CHUNKS):
        for copy in copies[chunk]:
            copy.wait()
        for tile in range(TILES * chunk, TILES * chunk + TILES):
            rows = slice(8 * tile, 8 * tile + 8)
            spread_lines(cot[:, :, rows, :] * gelu_slope(pre[:, :, rows, :]), lhs, tile)
    for chunk in range(CHUNKS):
        rows = line_rows(chunk)
        outs.append(whole_copy(lhs.at[rows], lhs_hbm.at[rows], lhs_sems.at[chunk]))
    for table in tables:
        table.wait()
    for chunk in range(CHUNKS):
        transform_z(lhs, ztab, lines, chunk)
    outs += finish(ytab, lines, half, send, send_hbm, out_sems)
    for copy in outs:
        copy.wait()


def in_vmem(count):
    return [pl.BlockSpec(memory_space=pltpu.VMEM) for _ in range(count)]


def vmem_spec():
    return pl.BlockSpec(memory_space=pltpu.VMEM)


def any_spec():
    return pl.BlockSpec(memory_space=pl.ANY)


FIELD = (C, 2, N, N)


PAIR = (N // 8, 256, 256)


def in_hbm(value):
    return pltpu.with_memory_space_constraint(value, pltpu.HBM)


def kept(value):
    return pltpu.with_memory_space_constraint(value, pltpu.VMEM)


LINES = (2048, 1024)


def gradient_spectrum(preact, cotangent):
    ztab, ytab = jnp.asarray(z_tables()), jnp.asarray(y_tables())
    return pl.pallas_call(
        gradient_kernel,
        in_specs=[any_spec()] * 4,
        out_specs=[any_spec()] * 2,
        out_shape=[pltpu.HBM((SPACE, FIRST, 128), F32), pltpu.HBM(LINES, BF16)],
        scratch_shapes=[pltpu.VMEM(FIELD, F32)] * 2 + [
            pltpu.VMEM(ztab.shape, BF16), pltpu.VMEM(ytab.shape, BF16), pltpu.VMEM(LINES, BF16),
            pltpu.VMEM((GROUPS, N, 128), F32), pltpu.VMEM((GROUPS, MY, 128), F32), pltpu.VMEM((SPACE * FIRST, 128), F32),
            pltpu.SemaphoreType.DMA((CHUNKS, 2)), pltpu.SemaphoreType.DMA((2,)), pltpu.SemaphoreType.DMA((2,)),
            pltpu.SemaphoreType.DMA((CHUNKS,)),
        ],
        compiler_params=pltpu.CompilerParams(vmem_limit_bytes=LIMIT),
        name="gradient_spectrum",
    )(in_hbm(preact), in_hbm(cotangent), in_hbm(ztab), in_hbm(ytab))


ACROSS = (((1,), (1,)), ((), ()))


def same_row():
    left = lax.broadcasted_iota(jnp.int32, (256, 256), 0) & 7
    right = lax.broadcasted_iota(jnp.int32, (256, 256), 1) & 7
    return left == right


def tile_parts(lines, tile):
    rows = slice(128 * tile, 128 * tile + 128)
    return [
        jnp.concatenate([
            jnp.concatenate([
                lines[rows, 512 * inner + 256 * plane + part:512 * inner + 256 * plane + part + 128] for plane in range(2)
            ], 1) for inner in range(2)
        ], 0) for part in (0, 128)
    ]


def input_kernel(
    one_ref, lhs_hbm, inp_hbm, ztab_hbm, ytab_hbm, w_hbm, fold_ref, send_hbm, w_ref,
    g_lines, inp, ztab, ytab, lhs, acc, lines, half, send, sems, tab_sems, out_sems,
):
    always = one_ref[0] >= 0
    copies = []
    for chunk in range(CHUNKS):
        rows = line_rows(chunk)
        copies.append([
            chunk_copy(inp_hbm, inp, sems.at[chunk, 0], chunk),
            whole_copy(lhs_hbm.at[rows], g_lines.at[rows], sems.at[chunk, 1]),
        ])
    tables = [whole_copy(ztab_hbm, ztab, tab_sems.at[0]), whole_copy(ytab_hbm, ytab, tab_sems.at[1])]
    ahead = whole_copy(w_hbm.at[pl.ds(0, EARLY * WB)], w_ref, tab_sems.at[2])
    for chunk in range(CHUNKS):
        for copy in copies[chunk]:
            copy.wait()

        @pl.when(always)
        def _():
            for tile in range(TILES * chunk, TILES * chunk + TILES):
                spread_lines(inp[:, :, 8 * tile:8 * tile + 8, :], lhs, tile)

        if chunk == 0:
            tables[0].wait()

        @pl.when(always)
        def _():
            transform_z(lhs, ztab, lines, chunk)

        @pl.when(always)
        def _():
            for tile in range(TILES * chunk, TILES * chunk + TILES):
                g_high, g_low = tile_parts(g_lines, tile)
                i_high, i_low = tile_parts(lhs, tile)
                total = (
                    lax.dot_general(g_high, i_high, ACROSS, preferred_element_type=F32)
                    + lax.dot_general(g_low, i_high, ACROSS, preferred_element_type=F32)
                    + lax.dot_general(g_high, i_low, ACROSS, preferred_element_type=F32)
                )
                if tile == 0:
                    acc[...] = total
                else:
                    acc[...] += total

    diagonal = jnp.where(same_row(), acc[...], 0.0) * NORM
    fold = fold_ref[...].astype(F32)
    folded = jnp.dot(diagonal, fold, preferred_element_type=F32, precision=lax.Precision.HIGHEST)
    summed = lax.dot_general(
        fold, folded, (((0,), (0,)), ((), ())), preferred_element_type=F32,
        precision=lax.Precision.HIGHEST,
    )
    part = jnp.concatenate([summed[8 * q:8 * q + 8, :] for q in range(4)], 1)
    for dest in range(SPACE):
        send[24 * dest + 16:24 * dest + 24, :] = part
    rows = pl.ds(16, 8)
    outs = [whole_copy(blocks_of(send).at[:, rows], send_hbm.at[:, rows], out_sems.at[2])]
    tables[1].wait()
    outs += finish(ytab, lines, half, send, send_hbm, out_sems)
    ahead.wait()
    for copy in outs:
        copy.wait()


def input_spectrum(one, lines, inputs, weights):
    ztab, ytab = jnp.asarray(z_tables()), jnp.asarray(y_tables())
    return pl.pallas_call(
        input_kernel,
        in_specs=[pl.BlockSpec(memory_space=pltpu.SMEM)] + [any_spec()] * 5 + [vmem_spec()],
        out_specs=[any_spec(), vmem_spec()],
        out_shape=[pltpu.HBM((SPACE, 24, 128), F32), pltpu.VMEM((EARLY * WB, JL, 2 * C * C), F32)],
        scratch_shapes=[
            pltpu.VMEM(LINES, BF16), pltpu.VMEM(FIELD, F32),
            pltpu.VMEM(ztab.shape, BF16), pltpu.VMEM(ytab.shape, BF16), pltpu.VMEM(LINES, BF16),
            pltpu.VMEM((256, 256), F32),
            pltpu.VMEM((GROUPS, N, 128), F32), pltpu.VMEM((GROUPS, MY, 128), F32), pltpu.VMEM((SPACE * 24, 128), F32),
            pltpu.SemaphoreType.DMA((CHUNKS, 2)), pltpu.SemaphoreType.DMA((3,)), pltpu.SemaphoreType.DMA((3,)),
        ],
        compiler_params=pltpu.CompilerParams(vmem_limit_bytes=LIMIT),
        name="input_spectrum",
    )(one, in_hbm(lines), in_hbm(inputs), in_hbm(ztab), in_hbm(ytab), in_hbm(weights), fold_table())


def skip_kernel(lhs_hbm, after_hbm, skip_ref, rows_ref, fold_ref, term_hbm, g_lines, term, sems, out_sems):
    copies = []
    for chunk in range(CHUNKS):
        rows = line_rows(chunk)
        copies.append(whole_copy(lhs_hbm.at[rows], g_lines.at[rows], sems.at[chunk]))
    matrix = []
    for part in split(skip_ref[...]):
        wide = lax.dot_general(rows_ref[...], part, ACROSS, preferred_element_type=F32).astype(BF16)
        wide = lax.dot_general(wide, fold_ref[...], ACROSS, preferred_element_type=F32)
        matrix.append(jnp.where(same_row(), wide, 0.0).astype(BF16))
    matrix = jnp.concatenate(matrix, 0)
    outs = []
    for chunk in range(CHUNKS):
        copies[chunk].wait()
        for tile in range(TILES * chunk, TILES * chunk + TILES):
            rows = slice(8 * tile, 8 * tile + 8)
            g_high, g_low = tile_parts(g_lines, tile)
            out = dot(matrix, g_high)
            out = out[:256] + out[256:] + dot(matrix[:256], g_low)
            for plane in range(2):
                value = out[:, 128 * plane:128 * plane + 128].reshape(C, 8, N)
                term[:, plane, rows, :] = value
        rows = pl.ds(YB * chunk, YB)
        outs.append(whole_copy(term.at[:, :, rows, :], term_hbm.at[:, :, rows, :], out_sems.at[chunk]))
    for copy in outs:
        copy.wait()


def skip_term(lines, after, skip_weight):
    return pl.pallas_call(
        skip_kernel,
        in_specs=[any_spec()] * 2 + in_vmem(3),
        out_specs=any_spec(),
        out_shape=pltpu.HBM(FIELD, F32),
        scratch_shapes=[
            pltpu.VMEM(LINES, BF16), pltpu.VMEM(FIELD, F32),
            pltpu.SemaphoreType.DMA((CHUNKS,)), pltpu.SemaphoreType.DMA((CHUNKS,)),
        ],
        compiler_params=pltpu.CompilerParams(vmem_limit_bytes=LIMIT),
        name="skip_term",
    )(in_hbm(lines), after, skip_weight, rows_table(), fold_table())


FIRST = 16
SECOND = 40


def transform_x(recv_ref, rows_each, offset, xtab_ref, reorder):
    blocks = []
    for q in range(4):
        column = [recv_ref[pl.ds(offset + 4 * q + r, SPACE, stride=rows_each), :] for r in range(4)]
        blocks.append(jnp.concatenate(column, 0))
    high, low = split(jnp.concatenate(blocks, 1))
    out = dot(xtab_ref[...], high)
    spectrum = out[:2 * MX] + out[2 * MX:] + dot(xtab_ref[:2 * MX], low)
    out = dot(jnp.concatenate(split(spectrum), 0), reorder)
    return out[:2 * MX] + out[2 * MX:]


def to_rows(spectrum, scratch):
    count = spectrum.shape[0]
    lanes = lax.broadcasted_iota(jnp.int32, (count, 128), 1) >> 5
    for j in range(JL):
        block = spectrum[:, 128 * (j // 4):128 * (j // 4) + 128]
        scratch[pl.ds(j, count, stride=JL), :] = jnp.where(lanes == j % 4, block, 0.0)


WB = 8
EARLY = 2


def middle_kernel(
    dp_ref, recv_ref, xtab_ref, back_ref, early_ref, w_hbm, input_hbm, send_hbm, mine_ref, theirs_ref,
    w_ref, spec, wide, dual, send, sems, out_sems,
):
    copies = [None] * EARLY
    for block in range(EARLY, MX // WB):
        rows = pl.ds(WB * block, WB)
        copies.append(whole_copy(w_hbm.at[rows], w_ref.at[rows], sems.at[block]))
    onward = pl.ds(16, 24)
    arriving = whole_copy(input_hbm, blocks_of(send).at[:, onward], out_sems.at[3])
    reorder = reorder_matrix()
    spread = spread_matrix()
    first = dp_ref[0] == 0
    spectrum = transform_x(recv_ref, FIRST, 0, xtab_ref, reorder)
    mine_ref[...] = jnp.where(first, spectrum[:MX], spectrum[MX:])
    theirs_ref[...] = jnp.where(first, spectrum[MX:], spectrum[:MX])
    to_rows(spectrum, spec)

    for block in range(MX // WB):
        start = 32 * (WB * block // 16) + WB * block % 16
        both = jnp.concatenate([spec[JL * k:JL * (k + WB), :] for k in (start, start + 16)], 0)
        high, low = split(both)
        wide[block % 2] = dot(jnp.concatenate([high, low], 1), spread)
        if block >= EARLY:
            copies[block].wait()
        for local in range(WB):
            total_real, total_imag = None, None
            for tile in range(8):
                lanes = slice(128 * tile, 128 * tile + 128)
                real = wide[block % 2, JL * local:JL * local + JL, lanes]
                imag = wide[block % 2, JL * (WB + local):JL * (WB + local) + JL, lanes]
                m = WB * block + local
                w_real = early_ref[m, :, lanes] if block < EARLY else w_ref[m, :, lanes]
                far = slice(1024 + 128 * tile, 1024 + 128 * tile + 128)
                w_imag = early_ref[m, :, far] if block < EARLY else w_ref[m, :, far]
                out_real = w_real * real + w_imag * imag
                out_imag = w_real * imag - w_imag * real
                total_real = out_real if tile == 0 else total_real + out_real
                total_imag = out_imag if tile == 0 else total_imag + out_imag
            for total, place in ((total_real, start + local), (total_imag, start + 16 + local)):
                total = total + pltpu.roll(total, 64, 1)
                dual[JL * place:JL * place + JL, :] = total + pltpu.roll(total, 32, 1)

    arriving.wait()
    copies = [whole_copy(blocks_of(send).at[:, onward], send_hbm.at[:, onward], out_sems.at[2])]
    lanes = lax.broadcasted_iota(jnp.int32, (2 * MX, 128), 1) // C
    blocks = []
    for j4 in range(4):
        block = dual[pl.ds(4 * j4, 2 * MX, stride=JL), :]
        for k in range(1, 4):
            block = jnp.where(lanes == k, dual[pl.ds(4 * j4 + k, 2 * MX, stride=JL), :], block)
        blocks.append(block)
    both = jnp.concatenate(split(jnp.concatenate(blocks, 1)), 0)
    ordered = lax.dot_general(both, reorder, ACROSS, preferred_element_type=F32)
    high, low = split(ordered[:2 * MX] + ordered[2 * MX:])
    wide_lines = jnp.concatenate([high, low, high], 0)
    for half in range(2):
        out = dot(back_ref[...], wide_lines[:, 256 * half:256 * half + 256])
        for k in range(2):
            for r in range(4):
                send[pl.ds(4 * (2 * half + k) + r, SPACE, stride=SECOND), :] = (
                    out[SPACE * r:SPACE * r + SPACE, 128 * k:128 * k + 128]
                )
        rows = pl.ds(8 * half, 8)
        copies.append(whole_copy(blocks_of(send).at[:, rows], send_hbm.at[:, rows], out_sems.at[half]))
    for copy in copies:
        copy.wait()


def middle(dp, received, early, weights, input_rows):
    return pl.pallas_call(
        middle_kernel,
        in_specs=[pl.BlockSpec(memory_space=pltpu.SMEM)] + in_vmem(4) + [any_spec()] * 2,
        out_specs=[any_spec()] + in_vmem(2),
        out_shape=[
            pltpu.HBM((SPACE, SECOND, 128), F32),
            jax.ShapeDtypeStruct((MX, JL * C), F32),
            jax.ShapeDtypeStruct((MX, JL * C), F32),
        ],
        scratch_shapes=[
            pltpu.VMEM((MX, JL, 2 * C * C), F32), pltpu.VMEM((2 * MX * JL, 128), F32),
            pltpu.VMEM((2, 2 * WB * JL, C * C), F32), pltpu.VMEM((2 * MX * JL, 128), F32),
            pltpu.VMEM((SPACE * SECOND, 128), F32),
            pltpu.SemaphoreType.DMA((MX // WB,)), pltpu.SemaphoreType.DMA((4,)),
        ],
        compiler_params=pltpu.CompilerParams(vmem_limit_bytes=LIMIT),
        name="middle",
    )(dp, received, x_tables(), back_x_tables(), kept(early), in_hbm(weights), in_hbm(input_rows))


def inputs_kernel(dp_ref, recv_ref, theirs_ref, xtab_ref, after_hbm, mine_ref, out_ref):
    spectrum = transform_x(recv_ref, SECOND, 16, xtab_ref, reorder_matrix())
    first = dp_ref[0] == 0
    mine_ref[...] = jnp.where(first, spectrum[:MX], spectrum[MX:])
    out_ref[:MX, :] = theirs_ref[...]
    out_ref[MX:2 * MX, :] = jnp.where(first, spectrum[MX:], spectrum[:MX])
    total = recv_ref[32:40, :]
    for source in range(1, SPACE):
        total = total + recv_ref[SECOND * source + 32:SECOND * source + 40, :]
    out_ref[2 * MX:, :] = jnp.concatenate([total] * 4, 1)


def inputs_spectrum(dp, received, theirs, after):
    return pl.pallas_call(
        inputs_kernel,
        in_specs=[pl.BlockSpec(memory_space=pltpu.SMEM)] + in_vmem(3) + [any_spec()],
        out_specs=in_vmem(2),
        out_shape=[
            jax.ShapeDtypeStruct((MX, JL * C), F32),
            jax.ShapeDtypeStruct((2 * MX + 8, JL * C), F32),
        ],
        compiler_params=pltpu.CompilerParams(vmem_limit_bytes=LIMIT),
        name="inputs_spectrum",
    )(dp, received, theirs, x_tables(), in_hbm(after))


MB = 4


def weight_kernel(
    grad_ref, field_ref, sent_ref, got_ref, out_hbm, skip_ref, grads, fields, wide, out, sems,
):
    spread = spread_matrix()
    to_rows(grad_ref[...], grads.at[0])
    to_rows(got_ref[:MX], grads.at[1])
    for b, value in enumerate((field_ref[...], got_ref[MX:2 * MX])):
        for j in range(JL):
            piece = value[:, C * j:C * j + C]
            fields[b, pl.ds(j, MX, stride=JL), :] = jnp.concatenate([piece] * 4, 1)
    copies = []
    for block in range(16 // MB):
        rows = jnp.concatenate(
            [grads[b, JL * k:JL * (k + MB), :] for b in range(2) for k in (MB * block, 16 + MB * block)], 0
        )
        high, low = split(rows)
        wide[...] = dot(jnp.concatenate([high, low], 1), spread)
        for local in range(MB):
            m = MB * block + local
            f = [fields[b, JL * k:JL * k + JL, :] for b in range(2) for k in (m, m + 16)]
            for tile in range(8):
                lanes = slice(128 * tile, 128 * tile + 128)
                g = [wide[JL * (MB * q + local):JL * (MB * q + local) + JL, lanes] for q in range(4)]
                out[m, :, lanes] = g[0] * f[0] + g[1] * f[1] + g[2] * f[2] + g[3] * f[3]
                out[m, :, 1024 + 128 * tile:1024 + 128 * tile + 128] = (
                    g[1] * f[0] - g[0] * f[1] + g[3] * f[2] - g[2] * f[3]
                )
        rows = pl.ds(MB * block, MB)
        copy = pltpu.make_async_copy(out.at[rows], out_hbm.at[rows], sems.at[block])
        copy.start()
        copies.append(copy)
    total = sent_ref[2 * MX:, :128] + got_ref[2 * MX:, :128]
    for q in range(4):
        skip_ref[8 * q:8 * q + 8, :] = total[:, C * q:C * q + C]
    for copy in copies:
        copy.wait()


def weight_gradient(grad_mine, field_mine, sent, got):
    return pl.pallas_call(
        weight_kernel,
        in_specs=in_vmem(4),
        out_specs=[any_spec(), vmem_spec()],
        out_shape=[pltpu.HBM((16, JL, 2 * C * C), F32), jax.ShapeDtypeStruct((C, C), F32)],
        scratch_shapes=[
            pltpu.VMEM((2, MX * JL, 128), F32), pltpu.VMEM((2, MX * JL, 128), F32),
            pltpu.VMEM((4 * MB * JL, C * C), F32), pltpu.VMEM((16, JL, 2 * C * C), F32),
            pltpu.SemaphoreType.DMA((16 // MB,)),
        ],
        compiler_params=pltpu.CompilerParams(vmem_limit_bytes=LIMIT),
        name="weight_gradient",
    )(grad_mine, field_mine, sent, got)


GB = 4


def backward_kernel(
    recv_ref, term_hbm, ytab_ref, ztab_hbm, out_hbm, term, ztab, out, half, lhs, sems, out_sems,
):
    copies = []
    for block in range(GROUPS // GB):
        rows = pl.ds(2 * GB * block, 2 * GB)
        copies.append(whole_copy(term_hbm.at[rows], term.at[rows], sems.at[block]))
        if block == 0:
            ztab_copy = whole_copy(ztab_hbm, ztab, sems.at[GROUPS // GB])
    for jq in range(4):
        for group_set in range(2):
            rows = [recv_ref[pl.ds(jq * SECOND + 8 * group_set + r, MZ, stride=4 * SECOND), :] for r in range(8)]
            turned = jnp.concatenate(rows, 0).T
            half[8 * group_set:8 * group_set + 8, JL * jq:JL * jq + JL, :] = turned.reshape(8, JL, 128)
    outs = []
    for block in range(GROUPS // GB):
        for pair in range(GB // 2):
            both = []
            for member in range(2):
                value = half[GB * block + 2 * pair + member]
                both.append(jnp.concatenate([value, lane_swap(value, -1.0)], 0))
            high, low = split(jnp.concatenate(both, 1))
            lines = dot(ytab_ref[...], jnp.concatenate([high, low, high], 0))
            for member in range(2):
                high, low = split(lines[:, 128 * member:128 * member + 128])
                rows = slice(128 * (2 * pair + member), 128 * (2 * pair + member) + 128)
                lhs[rows, :128] = high
                lhs[rows, 128:256] = low
                lhs[rows, 256:] = high
        if block == 0:
            ztab_copy.wait()
        copies[block].wait()
        value = jnp.concatenate([dot(lhs[256 * k:256 * k + 256, :], ztab[...]) for k in range(GB // 2)], 0)
        for group in range(GB):
            for inner in range(2):
                for plane in range(2):
                    lane = 128 * (2 * inner + plane)
                    place = 2 * (GB * block + group) + inner
                    out[place, plane] = value[128 * group:128 * group + 128, lane:lane + 128] + term[place, plane]
        rows = pl.ds(2 * GB * block, 2 * GB)
        copy = pltpu.make_async_copy(out.at[rows], out_hbm.at[0, rows], out_sems.at[block])
        copy.start()
        outs.append(copy)
    for copy in outs:
        copy.wait()


def backward(received, term):
    ztab = jnp.asarray(back_z_tables())
    return pl.pallas_call(
        backward_kernel,
        in_specs=[vmem_spec(), any_spec(), vmem_spec(), any_spec()],
        out_specs=any_spec(),
        out_shape=pltpu.HBM((1, C, 2, N, N), F32),
        scratch_shapes=[
            pltpu.VMEM(FIELD, F32), pltpu.VMEM(ztab.shape, BF16), pltpu.VMEM(FIELD, F32),
            pltpu.VMEM((GROUPS, MY, 128), F32), pltpu.VMEM((GB * 128, 384), BF16),
            pltpu.SemaphoreType.DMA((GROUPS // GB + 1,)), pltpu.SemaphoreType.DMA((GROUPS // GB,)),
        ],
        compiler_params=pltpu.CompilerParams(vmem_limit_bytes=LIMIT),
        name="backward",
    )(received, in_hbm(term), back_y_tables(), in_hbm(ztab))


def exchange(sent, rows):
    swapped = lax.all_to_all(sent, "space", 0, 0, tiled=True)
    return swapped.reshape(SPACE * rows, 128)


def body(inputs, preact, cotangent, spectral_weight, skip_weight):
    dp = lax.axis_index("dp").astype(jnp.int32).reshape(1)
    send_grad, lines = gradient_spectrum(preact, cotangent)
    got_grad = exchange(send_grad, FIRST)
    input_rows, early = input_spectrum(dp, lines, inputs, spectral_weight)
    send_dual, grad_mine, grad_theirs = middle(dp, got_grad, early, spectral_weight, input_rows)
    got_dual = exchange(send_dual, SECOND)
    term = skip_term(lines, grad_mine, skip_weight)
    field_mine, sent = inputs_spectrum(dp, got_dual, grad_theirs, term)
    got = lax.ppermute(sent, "dp", [(0, 1), (1, 0)])
    input_grad = backward(got_dual, term)
    weight_grad, skip_grad = weight_gradient(grad_mine, field_mine, sent, got)
    return input_grad, weight_grad, skip_grad


def solution(mesh):
    in_specs = (
        P("dp", None, "space", None, None),
        P("dp", None, "space", None, None),
        P("dp", None, "space", None, None),
        P(None, "space", None),
        P(),
    )
    out_specs = (P("dp", None, "space", None, None), P("dp", "space", None), P())
    return jax.shard_map(body, mesh=mesh, in_specs=in_specs, out_specs=out_specs, check_vma=False)
```

```python
import functools

import jax
import jax.numpy as jnp
import numpy as np
from jax import lax
from jax.experimental import pallas as pl
from jax.experimental.pallas import tpu as pltpu
from jax.sharding import PartitionSpec as P

N = 128
C = 32
MX = 32
MY = 64
MZ = 16
SPACE = 64
GROUPS = C // 2
JL = 16
NORM = float(N) ** (-1.5)
TANH_SCALE = 0.7978845608028654
CUBIC = 0.044715
F32 = jnp.float32
BF16 = jnp.bfloat16
LIMIT = 40 * 1024 * 1024


def signed(count):
    index = np.arange(count)
    return np.where(index < count // 2, index, index - count)


def angles(frequency):
    points = np.arange(N)
    return 2.0 * np.pi / N * np.mod(frequency[:, None] * points[None, :], N)


ANGLE_X = angles(signed(MX))
ANGLE_Y = angles(signed(MY))
ANGLE_Z = angles(np.arange(MZ))


def halves(table):
    table = np.asarray(table, np.float64)
    high = table.astype(np.float32).astype(BF16)
    low = (table - high.astype(np.float64)).astype(np.float32).astype(BF16)
    return high, low


def split(value):
    high = value.astype(BF16)
    return high, (value - high.astype(F32)).astype(BF16)


def dot(left, right):
    return jnp.dot(left, right, preferred_element_type=F32)


def z_tables():
    high, low = halves(np.concatenate([np.cos(ANGLE_Z).T, -np.sin(ANGLE_Z).T], 1))
    table = np.zeros((4, 2, N, 2, 4, 2 * MZ), BF16)
    for plane in range(4):
        table[plane, 0, :, 0, plane] = high
        table[plane, 1, :, 0, plane] = high
        table[plane, 0, :, 1, plane] = low
    return table.reshape(8 * N, 256)


def y_tables():
    high, low = halves(np.concatenate([np.cos(ANGLE_Y), -np.sin(ANGLE_Y)], 0))
    return np.concatenate([high, high, low], 1)


def x_tables():
    cos_x, sin_x = np.cos(ANGLE_X), np.sin(ANGLE_X)
    table = np.zeros((2, MX, 2, N))
    table[0, :, 0], table[0, :, 1] = cos_x, sin_x
    table[1, :, 0], table[1, :, 1] = -sin_x, cos_x
    table = table.reshape(2, 2, MX // 2, 2, SPACE, 2).transpose(1, 0, 2, 5, 3, 4) * NORM
    high, low = halves(table.reshape(2 * MX, 4 * SPACE))
    return np.concatenate([high, low], 0)


def back_x_tables():
    cos_x, sin_x = np.cos(ANGLE_X), np.sin(ANGLE_X)
    table = np.zeros((2, MX, 2, N))
    table[0, :, 0], table[0, :, 1] = cos_x, sin_x
    table[1, :, 0], table[1, :, 1] = -sin_x, cos_x
    table = table.reshape(2, 2, MX // 2, 2, SPACE, 2).transpose(5, 3, 4, 1, 0, 2) * NORM
    high, low = halves(table.reshape(4 * SPACE, 2 * MX))
    return np.concatenate([high, high, low], 1)


def back_y_tables():
    high, low = halves(np.concatenate([np.cos(ANGLE_Y).T, np.sin(ANGLE_Y).T], 1))
    return np.concatenate([high, high, low], 1)


def back_z_tables():
    high, low = halves(np.concatenate([np.cos(ANGLE_Z), -np.sin(ANGLE_Z)], 0))
    table = np.zeros((3, 4, 2 * MZ, 4, N), BF16)
    for plane in range(4):
        table[0, plane, :, plane] = high
        table[1, plane, :, plane] = high
        table[2, plane, :, plane] = low
    return table.reshape(3 * 128, 4 * N)


def one_hot(hits):
    return jnp.where(hits, 1.0, 0.0).astype(BF16)


def reorder_matrix():
    row = lax.broadcasted_iota(jnp.int32, (C * JL, C * JL), 0)
    column = lax.broadcasted_iota(jnp.int32, (C * JL, C * JL), 1)
    sent, j = row >> 4, row & (JL - 1)
    channel = ((sent >> 4) * 8 + (sent & 7)) * 2 + ((sent >> 3) & 1)
    return one_hot(column == j * C + channel)


def spread_matrix():
    row = lax.broadcasted_iota(jnp.int32, (8 * C, C * C), 0)
    column = lax.broadcasted_iota(jnp.int32, (8 * C, C * C), 1)
    return one_hot((row & (C - 1)) == (column >> 5))


def rows_table():
    return np.repeat(np.eye(C), 8, 0).astype(BF16)


def fold_table():
    table = np.zeros((2, GROUPS, 8, C), BF16)
    for inner in range(2):
        for group in range(GROUPS):
            table[inner, group, :, 2 * group + inner] = 1
    return table.reshape(256, C)


def gelu_slope(h):
    square = h * h
    t = jnp.tanh(h * (TANH_SCALE + (TANH_SCALE * CUBIC) * square))
    inner = h * (0.5 * TANH_SCALE + (1.5 * TANH_SCALE * CUBIC) * square)
    return (0.5 + 0.5 * t) + (1.0 - t * t) * inner


def lane_swap(value, first_sign):
    lanes = lax.broadcasted_iota(jnp.int32, value.shape, value.ndim - 1)
    up = pltpu.roll(value, 128 - MZ, value.ndim - 1)
    down = pltpu.roll(value, MZ, value.ndim - 1)
    return jnp.where((lanes & MZ) == 0, first_sign * up, -first_sign * down)


YB = 32
CHUNKS = N // YB
TILES = YB // 8


def chunk_copy(ref, buffer, sem, chunk, size=YB):
    rows = pl.ds(size * chunk, size)
    copy = pltpu.make_async_copy(ref.at[0, :, :, rows, :], buffer.at[:, :, rows, :], sem)
    copy.start()
    return copy


def whole_copy(ref, buffer, sem):
    copy = pltpu.make_async_copy(ref, buffer, sem)
    copy.start()
    return copy


def spread_lines(value, lhs, tile):
    value = value.reshape(GROUPS, 2, 2, 8, N)
    rows = slice(128 * tile, 128 * tile + 128)
    for inner in range(2):
        for plane in range(2):
            high, low = split(value[:, inner, plane].reshape(GROUPS * 8, N))
            lane = 256 * (2 * inner + plane)
            lhs[rows, lane:lane + 128] = high
            lhs[rows, lane + 128:lane + 256] = low


def transform_z(lhs, ztab_ref, scratch, chunk):
    out = dot(lhs[128 * TILES * chunk:128 * TILES * (chunk + 1), :], ztab_ref[...])
    out = out[:, :128] + out[:, 128:]
    for tile in range(TILES):
        place = YB * chunk + 8 * tile
        scratch[:, place:place + 8, :] = out[128 * tile:128 * tile + 128].reshape(GROUPS, 8, 128)


def transform_y(scratch, ytab_ref, half, group_set):
    for pair in range(4 * group_set, 4 * group_set + 4):
        wide = jnp.concatenate([scratch[2 * pair], scratch[2 * pair + 1]], 1)
        high, low = split(wide)
        out = dot(ytab_ref[...], jnp.concatenate([high, low, high], 0))
        for member in range(2):
            mine = out[:, 128 * member:128 * member + 128]
            half[2 * pair + member] = mine[:MY] + lane_swap(mine[MY:], -1.0)


def blocks_of(send):
    return send.reshape(SPACE, send.shape[0] // SPACE, 128)


def lay_out(half, send_ref, group_set):
    rows_each = send_ref.shape[0] // SPACE
    for jq in range(4):
        block = half[8 * group_set:8 * group_set + 8, JL * jq:JL * jq + JL, :]
        turned = block.reshape(128, 128).T
        for r in range(8):
            row = jq * rows_each + 8 * group_set + r
            send_ref[pl.ds(row, MZ, stride=4 * rows_each), :] = turned[MZ * r:MZ * r + MZ]


def finish(ytab, lines, half, send, send_hbm, out_sems):
    copies = []
    transform_y(lines, ytab, half, 0)
    transform_y(lines, ytab, half, 1)
    for group_set in range(2):
        lay_out(half, send, group_set)
        rows = pl.ds(8 * group_set, 8)
        copies.append(whole_copy(blocks_of(send).at[:, rows], send_hbm.at[:, rows], out_sems.at[group_set]))
    return copies


def line_rows(chunk):
    return pl.ds(128 * TILES * chunk, 128 * TILES)


def gradient_kernel(
    pre_hbm, cot_hbm, ztab_hbm, ytab_hbm, send_hbm, lhs_hbm,
    pre, cot, ztab, ytab, lhs, lines, half, send, sems, tab_sems, out_sems, lhs_sems,
):
    copies = [
        [chunk_copy(ref, buffer, sems.at[chunk, k], chunk, 16) for k, ref, buffer in ((0, pre_hbm, pre), (1, cot_hbm, cot))]
        for chunk in range(N // 16)
    ]
    tables = [whole_copy(ztab_hbm, ztab, tab_sems.at[0]), whole_copy(ytab_hbm, ytab, tab_sems.at[1])]
    outs = []
    for chunk in range(N // 16):
        for copy in copies[chunk]:
            copy.wait()
        for tile in (2 * chunk, 2 * chunk + 1):
            rows = slice(8 * tile, 8 * tile + 8)
            spread_lines(cot[:, :, rows, :] * gelu_slope(pre[:, :, rows, :]), lhs, tile)
    for chunk in range(CHUNKS):
        rows = line_rows(chunk)
        outs.append(whole_copy(lhs.at[rows], lhs_hbm.at[rows], lhs_sems.at[chunk]))
    for table in tables:
        table.wait()
    for chunk in range(CHUNKS):
        transform_z(lhs, ztab, lines, chunk)
    outs += finish(ytab, lines, half, send, send_hbm, out_sems)
    for copy in outs:
        copy.wait()


def in_vmem(count):
    return [pl.BlockSpec(memory_space=pltpu.VMEM) for _ in range(count)]


def vmem_spec():
    return pl.BlockSpec(memory_space=pltpu.VMEM)


def any_spec():
    return pl.BlockSpec(memory_space=pl.ANY)


FIELD = (C, 2, N, N)


PAIR = (N // 8, 256, 256)


def in_hbm(value):
    return pltpu.with_memory_space_constraint(value, pltpu.HBM)


def kept(value):
    return pltpu.with_memory_space_constraint(value, pltpu.VMEM)


LINES = (2048, 1024)


def gradient_spectrum(preact, cotangent):
    ztab, ytab = jnp.asarray(z_tables()), jnp.asarray(y_tables())
    return pl.pallas_call(
        gradient_kernel,
        in_specs=[any_spec()] * 4,
        out_specs=[any_spec()] * 2,
        out_shape=[pltpu.HBM((SPACE, FIRST, 128), F32), pltpu.HBM(LINES, BF16)],
        scratch_shapes=[pltpu.VMEM(FIELD, F32)] * 2 + [
            pltpu.VMEM(ztab.shape, BF16), pltpu.VMEM(ytab.shape, BF16), pltpu.VMEM(LINES, BF16),
            pltpu.VMEM((GROUPS, N, 128), F32), pltpu.VMEM((GROUPS, MY, 128), F32), pltpu.VMEM((SPACE * FIRST, 128), F32),
            pltpu.SemaphoreType.DMA((N // 16, 2)), pltpu.SemaphoreType.DMA((2,)), pltpu.SemaphoreType.DMA((2,)),
            pltpu.SemaphoreType.DMA((CHUNKS,)),
        ],
        compiler_params=pltpu.CompilerParams(vmem_limit_bytes=LIMIT),
        name="gradient_spectrum",
    )(in_hbm(preact), in_hbm(cotangent), in_hbm(ztab), in_hbm(ytab))


ACROSS = (((1,), (1,)), ((), ()))


def same_row():
    left = lax.broadcasted_iota(jnp.int32, (256, 256), 0) & 7
    right = lax.broadcasted_iota(jnp.int32, (256, 256), 1) & 7
    return left == right


def tile_parts(lines, tile):
    rows = slice(128 * tile, 128 * tile + 128)
    return [
        jnp.concatenate([
            jnp.concatenate([
                lines[rows, 512 * inner + 256 * plane + part:512 * inner + 256 * plane + part + 128] for plane in range(2)
            ], 1) for inner in range(2)
        ], 0) for part in (0, 128)
    ]


def input_kernel(
    one_ref, lhs_hbm, inp_hbm, ztab_hbm, ytab_hbm, w_hbm, fold_ref, send_hbm, w_ref,
    g_lines, inp, ztab, ytab, lhs, acc, lines, half, send, sems, tab_sems, out_sems,
):
    always = one_ref[0] >= 0
    copies = []
    for chunk in range(CHUNKS):
        rows = line_rows(chunk)
        copies.append([
            chunk_copy(inp_hbm, inp, sems.at[chunk, 0], chunk),
            whole_copy(lhs_hbm.at[rows], g_lines.at[rows], sems.at[chunk, 1]),
        ])
    tables = [whole_copy(ztab_hbm, ztab, tab_sems.at[0]), whole_copy(ytab_hbm, ytab, tab_sems.at[1])]
    ahead = whole_copy(w_hbm.at[pl.ds(0, EARLY * WB)], w_ref, tab_sems.at[2])
    for chunk in range(CHUNKS):
        for copy in copies[chunk]:
            copy.wait()

        @pl.when(always)
        def _():
            for tile in range(TILES * chunk, TILES * chunk + TILES):
                spread_lines(inp[:, :, 8 * tile:8 * tile + 8, :], lhs, tile)

        if chunk == 0:
            tables[0].wait()

        @pl.when(always)
        def _():
            transform_z(lhs, ztab, lines, chunk)

        @pl.when(always)
        def _():
            for tile in range(TILES * chunk, TILES * chunk + TILES):
                g_high, g_low = tile_parts(g_lines, tile)
                i_high, i_low = tile_parts(lhs, tile)
                total = (
                    lax.dot_general(g_high, i_high, ACROSS, preferred_element_type=F32)
                    + lax.dot_general(g_low, i_high, ACROSS, preferred_element_type=F32)
                    + lax.dot_general(g_high, i_low, ACROSS, preferred_element_type=F32)
                )
                if tile == 0:
                    acc[...] = total
                else:
                    acc[...] += total

    diagonal = jnp.where(same_row(), acc[...], 0.0) * NORM
    fold = fold_ref[...].astype(F32)
    folded = jnp.dot(diagonal, fold, preferred_element_type=F32, precision=lax.Precision.HIGHEST)
    summed = lax.dot_general(
        fold, folded, (((0,), (0,)), ((), ())), preferred_element_type=F32,
        precision=lax.Precision.HIGHEST,
    )
    part = jnp.concatenate([summed[8 * q:8 * q + 8, :] for q in range(4)], 1)
    for dest in range(SPACE):
        send[24 * dest + 16:24 * dest + 24, :] = part
    rows = pl.ds(16, 8)
    outs = [whole_copy(blocks_of(send).at[:, rows], send_hbm.at[:, rows], out_sems.at[2])]
    tables[1].wait()
    outs += finish(ytab, lines, half, send, send_hbm, out_sems)
    ahead.wait()
    for copy in outs:
        copy.wait()


def input_spectrum(one, lines, inputs, weights):
    ztab, ytab = jnp.asarray(z_tables()), jnp.asarray(y_tables())
    return pl.pallas_call(
        input_kernel,
        in_specs=[pl.BlockSpec(memory_space=pltpu.SMEM)] + [any_spec()] * 5 + [vmem_spec()],
        out_specs=[any_spec(), vmem_spec()],
        out_shape=[pltpu.HBM((SPACE, 24, 128), F32), pltpu.VMEM((EARLY * WB, JL, 2 * C * C), F32)],
        scratch_shapes=[
            pltpu.VMEM(LINES, BF16), pltpu.VMEM(FIELD, F32),
            pltpu.VMEM(ztab.shape, BF16), pltpu.VMEM(ytab.shape, BF16), pltpu.VMEM(LINES, BF16),
            pltpu.VMEM((256, 256), F32),
            pltpu.VMEM((GROUPS, N, 128), F32), pltpu.VMEM((GROUPS, MY, 128), F32), pltpu.VMEM((SPACE * 24, 128), F32),
            pltpu.SemaphoreType.DMA((CHUNKS, 2)), pltpu.SemaphoreType.DMA((3,)), pltpu.SemaphoreType.DMA((3,)),
        ],
        compiler_params=pltpu.CompilerParams(vmem_limit_bytes=LIMIT),
        name="input_spectrum",
    )(one, in_hbm(lines), in_hbm(inputs), in_hbm(ztab), in_hbm(ytab), in_hbm(weights), fold_table())


def skip_kernel(lhs_hbm, after_hbm, skip_ref, rows_ref, fold_ref, term_hbm, g_lines, term, sems, out_sems):
    copies = []
    for chunk in range(CHUNKS):
        rows = line_rows(chunk)
        copies.append(whole_copy(lhs_hbm.at[rows], g_lines.at[rows], sems.at[chunk]))
    matrix = []
    for part in split(skip_ref[...]):
        wide = lax.dot_general(rows_ref[...], part, ACROSS, preferred_element_type=F32).astype(BF16)
        wide = lax.dot_general(wide, fold_ref[...], ACROSS, preferred_element_type=F32)
        matrix.append(jnp.where(same_row(), wide, 0.0).astype(BF16))
    matrix = jnp.concatenate(matrix, 0)
    outs = []
    for chunk in range(CHUNKS):
        copies[chunk].wait()
        for tile in range(TILES * chunk, TILES * chunk + TILES):
            rows = slice(8 * tile, 8 * tile + 8)
            g_high, g_low = tile_parts(g_lines, tile)
            out = dot(matrix, g_high)
            out = out[:256] + out[256:] + dot(matrix[:256], g_low)
            for plane in range(2):
                value = out[:, 128 * plane:128 * plane + 128].reshape(C, 8, N)
                term[:, plane, rows, :] = value
        rows = pl.ds(YB * chunk, YB)
        outs.append(whole_copy(term.at[:, :, rows, :], term_hbm.at[:, :, rows, :], out_sems.at[chunk]))
    for copy in outs:
        copy.wait()


def skip_term(lines, after, skip_weight):
    return pl.pallas_call(
        skip_kernel,
        in_specs=[any_spec()] * 2 + in_vmem(3),
        out_specs=any_spec(),
        out_shape=pltpu.HBM(FIELD, F32),
        scratch_shapes=[
            pltpu.VMEM(LINES, BF16), pltpu.VMEM(FIELD, F32),
            pltpu.SemaphoreType.DMA((CHUNKS,)), pltpu.SemaphoreType.DMA((CHUNKS,)),
        ],
        compiler_params=pltpu.CompilerParams(vmem_limit_bytes=LIMIT),
        name="skip_term",
    )(in_hbm(lines), after, skip_weight, rows_table(), fold_table())


FIRST = 16
SECOND = 40


def transform_x(recv_ref, rows_each, offset, xtab_ref, reorder):
    blocks = []
    for q in range(4):
        column = [recv_ref[pl.ds(offset + 4 * q + r, SPACE, stride=rows_each), :] for r in range(4)]
        blocks.append(jnp.concatenate(column, 0))
    high, low = split(jnp.concatenate(blocks, 1))
    out = dot(xtab_ref[...], high)
    spectrum = out[:2 * MX] + out[2 * MX:] + dot(xtab_ref[:2 * MX], low)
    out = dot(jnp.concatenate(split(spectrum), 0), reorder)
    return out[:2 * MX] + out[2 * MX:]


def to_rows(spectrum, scratch):
    count = spectrum.shape[0]
    lanes = lax.broadcasted_iota(jnp.int32, (count, 128), 1) >> 5
    for j in range(JL):
        block = spectrum[:, 128 * (j // 4):128 * (j // 4) + 128]
        scratch[pl.ds(j, count, stride=JL), :] = jnp.where(lanes == j % 4, block, 0.0)


WB = 8
EARLY = 2


def middle_kernel(
    dp_ref, recv_ref, xtab_ref, back_ref, early_ref, w_hbm, input_hbm, send_hbm, mine_ref, theirs_ref,
    w_ref, spec, wide, dual, send, sems, out_sems,
):
    copies = [None] * EARLY
    for block in range(EARLY, MX // WB):
        rows = pl.ds(WB * block, WB)
        copies.append(whole_copy(w_hbm.at[rows], w_ref.at[rows], sems.at[block]))
    onward = pl.ds(16, 24)
    arriving = whole_copy(input_hbm, blocks_of(send).at[:, onward], out_sems.at[3])
    reorder = reorder_matrix()
    spread = spread_matrix()
    first = dp_ref[0] == 0
    spectrum = transform_x(recv_ref, FIRST, 0, xtab_ref, reorder)
    mine_ref[...] = jnp.where(first, spectrum[:MX], spectrum[MX:])
    theirs_ref[...] = jnp.where(first, spectrum[MX:], spectrum[:MX])
    to_rows(spectrum, spec)

    for block in range(MX // WB):
        start = 32 * (WB * block // 16) + WB * block % 16
        both = jnp.concatenate([spec[JL * k:JL * (k + WB), :] for k in (start, start + 16)], 0)
        high, low = split(both)
        wide[block % 2] = dot(jnp.concatenate([high, low], 1), spread)
        if block >= EARLY:
            copies[block].wait()
        for local in range(WB):
            total_real, total_imag = None, None
            for tile in range(8):
                lanes = slice(128 * tile, 128 * tile + 128)
                real = wide[block % 2, JL * local:JL * local + JL, lanes]
                imag = wide[block % 2, JL * (WB + local):JL * (WB + local) + JL, lanes]
                m = WB * block + local
                w_real = early_ref[m, :, lanes] if block < EARLY else w_ref[m, :, lanes]
                far = slice(1024 + 128 * tile, 1024 + 128 * tile + 128)
                w_imag = early_ref[m, :, far] if block < EARLY else w_ref[m, :, far]
                out_real = w_real * real + w_imag * imag
                out_imag = w_real * imag - w_imag * real
                total_real = out_real if tile == 0 else total_real + out_real
                total_imag = out_imag if tile == 0 else total_imag + out_imag
            for total, place in ((total_real, start + local), (total_imag, start + 16 + local)):
                total = total + pltpu.roll(total, 64, 1)
                dual[JL * place:JL * place + JL, :] = total + pltpu.roll(total, 32, 1)

    arriving.wait()
    copies = [whole_copy(blocks_of(send).at[:, onward], send_hbm.at[:, onward], out_sems.at[2])]
    lanes = lax.broadcasted_iota(jnp.int32, (2 * MX, 128), 1) // C
    blocks = []
    for j4 in range(4):
        block = dual[pl.ds(4 * j4, 2 * MX, stride=JL), :]
        for k in range(1, 4):
            block = jnp.where(lanes == k, dual[pl.ds(4 * j4 + k, 2 * MX, stride=JL), :], block)
        blocks.append(block)
    both = jnp.concatenate(split(jnp.concatenate(blocks, 1)), 0)
    ordered = lax.dot_general(both, reorder, ACROSS, preferred_element_type=F32)
    high, low = split(ordered[:2 * MX] + ordered[2 * MX:])
    wide_lines = jnp.concatenate([high, low, high], 0)
    for half in range(2):
        out = dot(back_ref[...], wide_lines[:, 256 * half:256 * half + 256])
        for k in range(2):
            for r in range(4):
                send[pl.ds(4 * (2 * half + k) + r, SPACE, stride=SECOND), :] = (
                    out[SPACE * r:SPACE * r + SPACE, 128 * k:128 * k + 128]
                )
        rows = pl.ds(8 * half, 8)
        copies.append(whole_copy(blocks_of(send).at[:, rows], send_hbm.at[:, rows], out_sems.at[half]))
    for copy in copies:
        copy.wait()


def middle(dp, received, early, weights, input_rows):
    return pl.pallas_call(
        middle_kernel,
        in_specs=[pl.BlockSpec(memory_space=pltpu.SMEM)] + in_vmem(4) + [any_spec()] * 2,
        out_specs=[any_spec()] + in_vmem(2),
        out_shape=[
            pltpu.HBM((SPACE, SECOND, 128), F32),
            jax.ShapeDtypeStruct((MX, JL * C), F32),
            jax.ShapeDtypeStruct((MX, JL * C), F32),
        ],
        scratch_shapes=[
            pltpu.VMEM((MX, JL, 2 * C * C), F32), pltpu.VMEM((2 * MX * JL, 128), F32),
            pltpu.VMEM((2, 2 * WB * JL, C * C), F32), pltpu.VMEM((2 * MX * JL, 128), F32),
            pltpu.VMEM((SPACE * SECOND, 128), F32),
            pltpu.SemaphoreType.DMA((MX // WB,)), pltpu.SemaphoreType.DMA((4,)),
        ],
        compiler_params=pltpu.CompilerParams(vmem_limit_bytes=LIMIT),
        name="middle",
    )(dp, received, x_tables(), back_x_tables(), kept(early), in_hbm(weights), in_hbm(input_rows))


def inputs_kernel(dp_ref, recv_ref, theirs_ref, xtab_ref, after_hbm, mine_ref, out_ref):
    spectrum = transform_x(recv_ref, SECOND, 16, xtab_ref, reorder_matrix())
    first = dp_ref[0] == 0
    mine_ref[...] = jnp.where(first, spectrum[:MX], spectrum[MX:])
    out_ref[:MX, :] = theirs_ref[...]
    out_ref[MX:2 * MX, :] = jnp.where(first, spectrum[MX:], spectrum[:MX])
    total = recv_ref[32:40, :]
    for source in range(1, SPACE):
        total = total + recv_ref[SECOND * source + 32:SECOND * source + 40, :]
    out_ref[2 * MX:, :] = jnp.concatenate([total] * 4, 1)


def inputs_spectrum(dp, received, theirs, after):
    return pl.pallas_call(
        inputs_kernel,
        in_specs=[pl.BlockSpec(memory_space=pltpu.SMEM)] + in_vmem(3) + [any_spec()],
        out_specs=in_vmem(2),
        out_shape=[
            jax.ShapeDtypeStruct((MX, JL * C), F32),
            jax.ShapeDtypeStruct((2 * MX + 8, JL * C), F32),
        ],
        compiler_params=pltpu.CompilerParams(vmem_limit_bytes=LIMIT),
        name="inputs_spectrum",
    )(dp, received, theirs, x_tables(), in_hbm(after))


MB = 2


def weight_kernel(
    grad_ref, field_ref, sent_ref, got_ref, out_hbm, skip_ref, grads, fields, wide, out, sems,
):
    spread = spread_matrix()
    to_rows(grad_ref[...], grads.at[0])
    to_rows(got_ref[:MX], grads.at[1])
    for b, value in enumerate((field_ref[...], got_ref[MX:2 * MX])):
        for j in range(JL):
            piece = value[:, C * j:C * j + C]
            fields[b, pl.ds(j, MX, stride=JL), :] = jnp.concatenate([piece] * 4, 1)
    copies = []
    for block in range(16 // MB):
        rows = jnp.concatenate(
            [grads[b, JL * k:JL * (k + MB), :] for b in range(2) for k in (MB * block, 16 + MB * block)], 0
        )
        high, low = split(rows)
        wide[...] = dot(jnp.concatenate([high, low], 1), spread)
        for local in range(MB):
            m = MB * block + local
            f = [fields[b, JL * k:JL * k + JL, :] for b in range(2) for k in (m, m + 16)]
            for tile in range(8):
                lanes = slice(128 * tile, 128 * tile + 128)
                g = [wide[JL * (MB * q + local):JL * (MB * q + local) + JL, lanes] for q in range(4)]
                out[m, :, lanes] = g[0] * f[0] + g[1] * f[1] + g[2] * f[2] + g[3] * f[3]
                out[m, :, 1024 + 128 * tile:1024 + 128 * tile + 128] = (
                    g[1] * f[0] - g[0] * f[1] + g[3] * f[2] - g[2] * f[3]
                )
        rows = pl.ds(MB * block, MB)
        copy = pltpu.make_async_copy(out.at[rows], out_hbm.at[rows], sems.at[block])
        copy.start()
        copies.append(copy)
    total = sent_ref[2 * MX:, :128] + got_ref[2 * MX:, :128]
    for q in range(4):
        skip_ref[8 * q:8 * q + 8, :] = total[:, C * q:C * q + C]
    for copy in copies:
        copy.wait()


def weight_gradient(grad_mine, field_mine, sent, got):
    return pl.pallas_call(
        weight_kernel,
        in_specs=in_vmem(4),
        out_specs=[any_spec(), vmem_spec()],
        out_shape=[pltpu.HBM((16, JL, 2 * C * C), F32), jax.ShapeDtypeStruct((C, C), F32)],
        scratch_shapes=[
            pltpu.VMEM((2, MX * JL, 128), F32), pltpu.VMEM((2, MX * JL, 128), F32),
            pltpu.VMEM((4 * MB * JL, C * C), F32), pltpu.VMEM((16, JL, 2 * C * C), F32),
            pltpu.SemaphoreType.DMA((16 // MB,)),
        ],
        compiler_params=pltpu.CompilerParams(vmem_limit_bytes=LIMIT),
        name="weight_gradient",
    )(grad_mine, field_mine, sent, got)


GB = 4


def backward_kernel(
    recv_ref, term_hbm, ytab_ref, ztab_hbm, out_hbm, term, ztab, out, half, lhs, sems, out_sems,
):
    copies = []
    for block in range(GROUPS // GB):
        rows = pl.ds(2 * GB * block, 2 * GB)
        copies.append(whole_copy(term_hbm.at[rows], term.at[rows], sems.at[block]))
        if block == 0:
            ztab_copy = whole_copy(ztab_hbm, ztab, sems.at[GROUPS // GB])
    for jq in range(4):
        for group_set in range(2):
            rows = [recv_ref[pl.ds(jq * SECOND + 8 * group_set + r, MZ, stride=4 * SECOND), :] for r in range(8)]
            turned = jnp.concatenate(rows, 0).T
            half[8 * group_set:8 * group_set + 8, JL * jq:JL * jq + JL, :] = turned.reshape(8, JL, 128)
    outs = []
    for block in range(GROUPS // GB):
        for pair in range(GB // 2):
            both = []
            for member in range(2):
                value = half[GB * block + 2 * pair + member]
                both.append(jnp.concatenate([value, lane_swap(value, -1.0)], 0))
            high, low = split(jnp.concatenate(both, 1))
            lines = dot(ytab_ref[...], jnp.concatenate([high, low, high], 0))
            for member in range(2):
                high, low = split(lines[:, 128 * member:128 * member + 128])
                rows = slice(128 * (2 * pair + member), 128 * (2 * pair + member) + 128)
                lhs[rows, :128] = high
                lhs[rows, 128:256] = low
                lhs[rows, 256:] = high
        if block == 0:
            ztab_copy.wait()
        copies[block].wait()
        value = jnp.concatenate([dot(lhs[256 * k:256 * k + 256, :], ztab[...]) for k in range(GB // 2)], 0)
        for group in range(GB):
            for inner in range(2):
                for plane in range(2):
                    lane = 128 * (2 * inner + plane)
                    place = 2 * (GB * block + group) + inner
                    out[place, plane] = value[128 * group:128 * group + 128, lane:lane + 128] + term[place, plane]
        rows = pl.ds(2 * GB * block, 2 * GB)
        copy = pltpu.make_async_copy(out.at[rows], out_hbm.at[0, rows], out_sems.at[block])
        copy.start()
        outs.append(copy)
    for copy in outs:
        copy.wait()


def backward(received, term):
    ztab = jnp.asarray(back_z_tables())
    return pl.pallas_call(
        backward_kernel,
        in_specs=[vmem_spec(), any_spec(), vmem_spec(), any_spec()],
        out_specs=any_spec(),
        out_shape=pltpu.HBM((1, C, 2, N, N), F32),
        scratch_shapes=[
            pltpu.VMEM(FIELD, F32), pltpu.VMEM(ztab.shape, BF16), pltpu.VMEM(FIELD, F32),
            pltpu.VMEM((GROUPS, MY, 128), F32), pltpu.VMEM((GB * 128, 384), BF16),
            pltpu.SemaphoreType.DMA((GROUPS // GB + 1,)), pltpu.SemaphoreType.DMA((GROUPS // GB,)),
        ],
        compiler_params=pltpu.CompilerParams(vmem_limit_bytes=LIMIT),
        name="backward",
    )(received, in_hbm(term), back_y_tables(), in_hbm(ztab))


def exchange(sent, rows):
    swapped = lax.all_to_all(sent, "space", 0, 0, tiled=True)
    return swapped.reshape(SPACE * rows, 128)


def body(inputs, preact, cotangent, spectral_weight, skip_weight):
    dp = lax.axis_index("dp").astype(jnp.int32).reshape(1)
    send_grad, lines = gradient_spectrum(preact, cotangent)
    got_grad = exchange(send_grad, FIRST)
    input_rows, early = input_spectrum(dp, lines, inputs, spectral_weight)
    send_dual, grad_mine, grad_theirs = middle(dp, got_grad, early, spectral_weight, input_rows)
    got_dual = exchange(send_dual, SECOND)
    term = skip_term(lines, grad_mine, skip_weight)
    field_mine, sent = inputs_spectrum(dp, got_dual, grad_theirs, term)
    got = lax.ppermute(sent, "dp", [(0, 1), (1, 0)])
    input_grad = backward(got_dual, term)
    weight_grad, skip_grad = weight_gradient(grad_mine, field_mine, sent, got)
    return input_grad, weight_grad, skip_grad


def solution(mesh):
    in_specs = (
        P("dp", None, "space", None, None),
        P("dp", None, "space", None, None),
        P("dp", None, "space", None, None),
        P(None, "space", None),
        P(),
    )
    out_specs = (P("dp", None, "space", None, None), P("dp", "space", None), P())
    return jax.shard_map(body, mesh=mesh, in_specs=in_specs, out_specs=out_specs, check_vma=False)
```
